128 devices in a mesh: dp: 32 (over z, x, y_hi), heads: 4 (over y_lo, core).
Axes of the slice: x: 4, y: 4 (y_hi: 2, y_lo: 2; y = y_hi * 2 + y_lo), z: 4, core: 2. Of those that a mesh axis runs over, the one named last changes fastest.
Arguments:
- byte_states: bfloat16 [16384, 1280], P('dp'), may hold values from -6 to 6
- patch_states: bfloat16 [4096, 4096], P('dp'), may hold values from -6 to 6
- patch_lengths: int32 [32, 128], P('dp'), may hold values from 1 to 16, 512 in all within a row
- cotangent: bfloat16 [16384, 1280], P('dp'), may hold values from -6 to 6
- attention_gain: float32 [1280], replicated, may hold values from 0.5 to 2
- feedforward_gain: float32 [1280], replicated, may hold values from 0.5 to 1.5
- query_weight: bfloat16 [1280, 1024], P(None, 'heads'), may hold values from -0.15625 to 0.15625
- key_weight: bfloat16 [4096, 1024], P(None, 'heads'), may hold values from -0.09375 to 0.09375
- value_weight: bfloat16 [4096, 1024], P(None, 'heads'), may hold values from -0.09375 to 0.09375
- output_weight: bfloat16 [1024, 1280], P('heads'), may hold values from -0.1875 to 0.1875
- gate_weight: bfloat16 [1280, 3584], P(None, 'heads'), may hold values from -0.15625 to 0.15625
- up_weight: bfloat16 [1280, 3584], P(None, 'heads'), may hold values from -0.15625 to 0.15625
- down_weight: bfloat16 [3584, 1280], P('heads'), may hold values from -0.09375 to 0.09375
- adam_first: float32 [4, 6193152], P('heads', 'dp'), may hold values from -0.6 to 0.6
- adam_second: float32 [4, 6193152], P('heads', 'dp'), may hold values from 0.001 to 0.1
Outputs:
- input_grad: bfloat16 [16384, 1280], P(('dp', 'heads'))
- patch_grad: bfloat16 [4096, 4096], P(('dp', 'heads'))
- new_first: float32 [4, 6193152], P('heads', 'dp')
- new_second: float32 [4, 6193152], P('heads', 'dp')
- adam_step: float32 [4, 6193152], P('heads', 'dp')
The draws below stay inside these ranges and needn't reach their ends.
Inputs may be any that keep to these rules, and one draw needn't show every extreme that they name: `patch_lengths`: row s holds the lengths in bytes of the 128 patches of sequence s in order; each row sums to 512.
All inputs are finite; a program needn't handle non-finite values.
Results may differ from the reference program's by a relative error of at most 0.039.
Values may be sent and summed in bfloat16 or wider, within the bound.
A program may use at most 128 MiB of HBM per device.

```python
import math
import jax
import jax.numpy as jnp
import numpy as np
from jax import lax

D = 1280
DG = 4096
HEADS = 8
HEAD = 128
FF = 3584
BYTES = 512
MOST = 16
PATCHES = 128
GROUPS = 4
SEQS = 32
TOKENS = 16384
NPATCH = 4096
PER = 6193152
N_DP = 32


def shard_levels(key, dims, split, low, largest):
    loudness = 1.0
    for axis_at, blocks in split:
        steps = jax.random.uniform(jax.random.fold_in(jax.random.fold_in(key, 6), axis_at), (blocks,), jnp.float32, low / len(split), largest / len(split))
        loudness = loudness * jnp.repeat(jnp.exp(steps), dims[axis_at] // blocks).reshape((-1,) + (1,) * (len(dims) - 1 - axis_at))
    return loudness


def length_profile(count, total, limit, lean):
    weights = [(1 << 20) // math.isqrt(standing ** lean) + 1 for standing in range(2, count + 1)]
    rest, holding = total - limit - (count - 1), [1] * (count - 1)
    while rest > 0:
        free = [i for i in range(count - 1) if holding[i] < limit]
        whole, remaining = sum([weights[i] for i in free]), rest
        for i in free:
            addition = min(limit - holding[i], max(1, remaining * weights[i] // whole), rest)
            holding[i] = holding[i] + addition
            rest = rest - addition
    return np.array([limit] + holding)


def ragged(stream_key, amount, total, most, skew):
    if amount == 2:
        one = jax.random.randint(stream_key, (), max(1, total - most), min(most, total - 1) + 1)
        return jnp.stack([one, total - one])
    sizes = jnp.asarray(length_profile(amount, total, most, skew), jnp.int32)
    pairs = (amount - 1) // 2
    source_of, taker = sizes[1:1 + 2 * pairs:2], sizes[2:2 + 2 * pairs:2]
    room = jnp.minimum(source_of - 1, most - taker)
    moved = jax.random.randint(jax.random.fold_in(stream_key, 1), (pairs,), 0, 1 << 20) % (room + 1)
    sizes = sizes.at[1:1 + 2 * pairs:2].set(source_of - moved).at[2:2 + 2 * pairs:2].set(taker + moved)
    return sizes[jax.random.permutation(jax.random.fold_in(stream_key, 2), amount)]


def scatter_about(stream_key, dims, spread, bound, cuts=(), held_as=jnp.bfloat16):
    gain = shard_levels(stream_key, dims, cuts, -0.22, 0.18) if cuts else 1.0
    values = jax.random.normal(stream_key, dims, jnp.float32) * spread * gain
    return jnp.minimum(jnp.maximum(values, -bound), bound).astype(held_as)


def setup_inputs(seed: int = 0) -> dict:
    seeds = jax.random.split(jax.random.key(seed), 16)
    byte_states = scatter_about(seeds[0], (TOKENS, D), 1.0, 6.0, ((0, 32),))
    patch_states = scatter_about(seeds[1], (NPATCH, DG), 1.0, 6.0, ((0, 32),))
    patch_lengths = jax.vmap(lambda own: ragged(own, PATCHES, BYTES, MOST, 2))(jax.random.split(seeds[2], SEQS)).reshape((SEQS, PATCHES)).astype(jnp.int32)
    cotangent = scatter_about(seeds[3], (TOKENS, D), 1.0, 6.0, ((0, 32),))
    attention_gain = jnp.clip(jnp.exp(jax.random.uniform(seeds[4], (D,), jnp.float32, math.log(0.5), math.log(2.0))), 0.5, 2.0)
    feedforward_gain = jnp.clip(1.0 + 0.1 * jax.random.normal(seeds[5], (D,), jnp.float32), 0.5, 1.5)
    query_weight = scatter_about(seeds[6], (D, HEADS * HEAD), D ** -0.5, 0.15625, ((1, 4),))
    key_weight = scatter_about(seeds[7], (DG, HEADS * HEAD), DG ** -0.5, 0.09375, ((1, 4),))
    value_weight = scatter_about(seeds[8], (DG, HEADS * HEAD), DG ** -0.5, 0.09375, ((1, 4),))
    output_weight = scatter_about(seeds[9], (HEADS * HEAD, D), (HEADS * HEAD) ** -0.5, 0.1875, ((0, 4),))
    gate_weight = scatter_about(seeds[10], (D, FF), D ** -0.5, 0.15625, ((1, 4),))
    up_weight = scatter_about(seeds[11], (D, FF), D ** -0.5, 0.15625, ((1, 4),))
    down_weight = scatter_about(seeds[12], (FF, D), FF ** -0.5, 0.09375, ((0, 4),))
    adam_first = scatter_about(seeds[13], (GROUPS, PER), 0.1, 0.6, ((0, 4), (1, 32)), jnp.float32)
    adam_second = jnp.clip(jnp.exp(math.log(0.1) - 4.6051702 * jax.random.uniform(seeds[14], (GROUPS, PER), jnp.float32) ** shard_levels(seeds[14], (GROUPS, PER), ((0, 4), (1, 32)), -0.2, 0.2)), 0.001, 0.1)
    return {"byte_states": byte_states, "patch_states": patch_states, "patch_lengths": patch_lengths, "cotangent": cotangent, "attention_gain": attention_gain, "feedforward_gain": feedforward_gain, "query_weight": query_weight, "key_weight": key_weight, "value_weight": value_weight, "output_weight": output_weight, "gate_weight": gate_weight, "up_weight": up_weight, "down_weight": down_weight, "adam_first": adam_first, "adam_second": adam_second}


norm_epsilon = 1e-05
adam_epsilon = 1e-08
beta_first = 0.9
beta_second = 0.95
score_scale = 0.125
bias_first = 1.0 - 0.9 ** 20
bias_second = 1.0 - 0.95 ** 20

def norm_forward(inputs, gain_vec):
    inverse = lax.rsqrt(lax.optimization_barrier(jnp.mean(inputs * inputs, axis=-1, keepdims=True)) + norm_epsilon)
    return inputs * inverse * gain_vec

def norm_backward(inputs, gain_vec, grad_vec):
    inverse = lax.rsqrt(lax.optimization_barrier(jnp.mean(inputs * inputs, axis=-1, keepdims=True)) + norm_epsilon)
    scaled = grad_vec * gain_vec
    inner = lax.optimization_barrier(jnp.mean(scaled * inputs, axis=-1, keepdims=True))
    return inverse * scaled - inputs * (inverse * inverse * inverse) * inner

def rounded(values_in):
    return lax.optimization_barrier(values_in.astype(jnp.bfloat16)).astype(jnp.float32)

def group_total(group_terms):
    running_sum = jnp.zeros(group_terms[0].shape, jnp.float32)
    for group_term in group_terms:
        running_sum = running_sum + rounded(group_term)
    return running_sum

def matmul_plain(left, right):
    return jnp.dot(left, right, preferred_element_type=jnp.float32)

def reference(byte_states, patch_states, patch_lengths, cotangent, attention_gain, feedforward_gain, query_weight, key_weight, value_weight, output_weight, gate_weight, up_weight, down_weight, adam_first, adam_second):
    head_cols = HEADS * HEAD // GROUPS
    unit_cols = FF // GROUPS
    byte_float = byte_states.astype(jnp.float32)
    normed_bytes = norm_forward(byte_float, attention_gain).astype(jnp.bfloat16)
    query_full = matmul_plain(normed_bytes, query_weight).reshape(TOKENS, HEADS, HEAD)
    key_full = matmul_plain(patch_states, key_weight).reshape(NPATCH, HEADS, HEAD)
    value_proj = matmul_plain(patch_states, value_weight).astype(jnp.bfloat16)
    query_normed = norm_forward(query_full, 1.0).astype(jnp.bfloat16)
    key_normed = norm_forward(key_full, 1.0).astype(jnp.bfloat16)
    query_seq = query_normed.reshape(SEQS, BYTES, HEADS, HEAD).astype(jnp.float32)
    key_seq = key_normed.reshape(SEQS, PATCHES, HEADS, HEAD).astype(jnp.float32)
    value_seq = value_proj.reshape(SEQS, PATCHES, HEADS, HEAD).astype(jnp.float32)
    starts = jnp.cumsum(patch_lengths, axis=1) - patch_lengths
    positions = jnp.arange(BYTES, dtype=jnp.int32)
    visible = (starts[:, None, :] <= positions[None, :, None]).astype(jnp.float32)[:, None]
    scores = score_scale * jnp.einsum('sbhd,sphd->shbp', query_seq, key_seq)
    weights = jnp.exp(scores) * visible
    probabilities = weights / lax.optimization_barrier(jnp.sum(weights, axis=-1, keepdims=True))
    prob_half = rounded(probabilities)
    attended = jnp.einsum('shbp,sphd->sbhd', prob_half, value_seq).astype(jnp.bfloat16).reshape(TOKENS, HEADS * HEAD)
    attention_sum = group_total([matmul_plain(attended[:, group * head_cols:(group + 1) * head_cols], output_weight[group * head_cols:(group + 1) * head_cols]) for group in range(GROUPS)])
    residual = byte_float + attention_sum
    normed_hidden = norm_forward(residual, feedforward_gain).astype(jnp.bfloat16)
    gate = matmul_plain(normed_hidden, gate_weight)
    up_vals = matmul_plain(normed_hidden, up_weight)
    sigmoid = jax.nn.sigmoid(gate)
    activated = gate * sigmoid
    hidden = (activated * up_vals).astype(jnp.bfloat16)
    hidden_grad = matmul_plain(cotangent, down_weight.T)
    gate_grad = (hidden_grad * up_vals * (sigmoid * (1.0 + gate * (1.0 - sigmoid)))).astype(jnp.bfloat16)
    up_grad = (hidden_grad * activated).astype(jnp.bfloat16)
    normed_hidden_grad = group_total([matmul_plain(gate_grad[:, group * unit_cols:(group + 1) * unit_cols], gate_weight[:, group * unit_cols:(group + 1) * unit_cols].T) + matmul_plain(up_grad[:, group * unit_cols:(group + 1) * unit_cols], up_weight[:, group * unit_cols:(group + 1) * unit_cols].T) for group in range(GROUPS)])
    residual_grad = cotangent.astype(jnp.float32) + norm_backward(residual, feedforward_gain, normed_hidden_grad)
    residual_half = residual_grad.astype(jnp.bfloat16)
    attended_grad = matmul_plain(residual_half, output_weight.T).astype(jnp.bfloat16)
    attended_seq = attended_grad.reshape(SEQS, BYTES, HEADS, HEAD).astype(jnp.float32)
    prob_grad = jnp.einsum('sbhd,sphd->shbp', attended_seq, value_seq)
    score_grad = rounded(score_scale * probabilities * (prob_grad - lax.optimization_barrier(jnp.sum(probabilities * prob_grad, axis=-1, keepdims=True))))
    query_normed_grad = jnp.einsum('shbp,sphd->sbhd', score_grad, key_seq).reshape(TOKENS, HEADS, HEAD)
    key_normed_grad = jnp.einsum('shbp,sbhd->sphd', score_grad, query_seq).reshape(NPATCH, HEADS, HEAD)
    value_grad = jnp.einsum('shbp,sbhd->sphd', prob_half, attended_seq).astype(jnp.bfloat16).reshape(NPATCH, HEADS * HEAD)
    query_grad = norm_backward(query_full, 1.0, query_normed_grad).astype(jnp.bfloat16).reshape(TOKENS, HEADS * HEAD)
    key_grad = norm_backward(key_full, 1.0, key_normed_grad).astype(jnp.bfloat16).reshape(NPATCH, HEADS * HEAD)
    normed_bytes_grad = group_total([matmul_plain(query_grad[:, group * head_cols:(group + 1) * head_cols], query_weight[:, group * head_cols:(group + 1) * head_cols].T) for group in range(GROUPS)])
    patch_total = group_total([matmul_plain(key_grad[:, group * head_cols:(group + 1) * head_cols], key_weight[:, group * head_cols:(group + 1) * head_cols].T) + matmul_plain(value_grad[:, group * head_cols:(group + 1) * head_cols], value_weight[:, group * head_cols:(group + 1) * head_cols].T) for group in range(GROUPS)])
    patch_grad = patch_total.astype(jnp.bfloat16)
    input_grad = (residual_grad + norm_backward(byte_float, attention_gain, normed_bytes_grad)).astype(jnp.bfloat16)
    grad_query = matmul_plain(normed_bytes.T, query_grad)
    grad_key = matmul_plain(patch_states.T, key_grad)
    grad_value = matmul_plain(patch_states.T, value_grad)
    grad_output = matmul_plain(attended.T, residual_half)
    grad_gate = matmul_plain(normed_hidden.T, gate_grad)
    grad_up = matmul_plain(normed_hidden.T, up_grad)
    grad_down = matmul_plain(hidden.T, cotangent)
    flat_rows = []
    for group in range(GROUPS):
        head_lo = group * head_cols
        head_hi = head_lo + head_cols
        unit_lo = group * unit_cols
        unit_hi = unit_lo + unit_cols
        pieces = [grad_query[:, head_lo:head_hi], grad_key[:, head_lo:head_hi], grad_value[:, head_lo:head_hi], grad_output[head_lo:head_hi, :], grad_gate[:, unit_lo:unit_hi], grad_up[:, unit_lo:unit_hi], grad_down[unit_lo:unit_hi, :]]
        flat_rows.append(jnp.concatenate([piece.reshape(N_DP, -1) for piece in pieces], axis=1).reshape(-1))
    flat_grad = jnp.stack(flat_rows) * TOKENS ** (-0.5)
    new_first = beta_first * adam_first + (1.0 - beta_first) * flat_grad
    new_second = beta_second * adam_second + (1.0 - beta_second) * flat_grad * flat_grad
    adam_step = new_first / bias_first / (jnp.sqrt(new_second / bias_second) + adam_epsilon)
    return (input_grad, patch_grad, new_first, new_second, adam_step)
```

```python
import functools

import jax
import jax.numpy as jnp
from jax import lax
from jax.experimental import pallas as pl
from jax.experimental.pallas import tpu as pltpu
from jax.sharding import PartitionSpec as P

HEAD = 128
BYTES = 512
PATCHES = 128


norm_epsilon = 1e-05
adam_epsilon = 1e-08
beta_first = 0.9
beta_second = 0.95
score_scale = 0.125
bias_first = 1.0 - 0.9**20
bias_second = 1.0 - 0.95**20


def norm_forward(inputs, gain_vec):
    inverse = lax.rsqrt(jnp.mean(inputs * inputs, axis=-1, keepdims=True) + norm_epsilon)
    return inputs * inverse * gain_vec


def norm_backward(inputs, gain_vec, grad_vec):
    inverse = lax.rsqrt(jnp.mean(inputs * inputs, axis=-1, keepdims=True) + norm_epsilon)
    scaled = grad_vec * gain_vec
    inner = jnp.mean(scaled * inputs, axis=-1, keepdims=True)
    return inverse * scaled - inputs * (inverse * inverse * inverse) * inner


def matmul_plain(left, right):
    return jnp.dot(left, right, preferred_element_type=jnp.float32)


def matmul_right_t(left, right):
    return lax.dot_general(
        left, right, (((1,), (1,)), ((), ())), preferred_element_type=jnp.float32
    )


def matmul_left_t(left, right):
    return lax.dot_general(
        left, right, (((0,), (0,)), ((), ())), preferred_element_type=jnp.float32
    )


BF16 = jnp.bfloat16
F32 = jnp.float32
MESH_ID = pl.DeviceIdType.MESH
MIB = 1 << 20

GU1, GU2, DN, KK, VV, QO = range(6)
PIECES = (
    (80, 640, True),
    (80, 256, False),
    (32, 1280, False),
    (128, 256, True),
    (128, 256, False),
    (80, 256, True),
)
FLAT = 1512


def place():
    dp = lax.axis_index("dp")
    return lax.div(dp, 8), lax.rem(lax.div(dp, 2), 4), lax.rem(dp, 2), lax.axis_index("heads")


def device_at(z, x, y, g):
    return (z * 8 + x * 2 + y, g)


def scatter_scratch(items):
    shapes = []
    for item in items:
        rows, cols, _ = PIECES[item]
        shapes += [
            pltpu.VMEM((2, 2, 2, rows, cols), BF16),
            pltpu.VMEM((2, 2, 2, rows, cols), BF16),
            pltpu.VMEM((2, 4, 2, rows, cols), BF16),
            pltpu.VMEM((4, 2, rows, cols), BF16),
            pltpu.VMEM((2, rows, cols), BF16),
            pltpu.VMEM((2, rows, cols), BF16),
            pltpu.VMEM((2, 2, rows, cols), BF16),
            pltpu.VMEM((2, rows, cols), BF16),
            pltpu.VMEM((rows, cols), BF16),
            pltpu.SemaphoreType.DMA((13,)),
            pltpu.SemaphoreType.DMA((13,)),
        ]
    return shapes


SCATTER_REFS = 11


class Scatter:
    def __init__(self, item, grad, refs):
        self.grad = grad
        self.zfirst = PIECES[item][2]
        (self.near, self.carry, self.got, self.part, self.near2, self.carry2, self.got2, self.pair, self.last,
         self.send, self.recv) = refs
        z, x, y, g = place()
        self.y = y
        self.f, self.s = (z, x) if self.zfirst else (x, z)
        self.g = g
        self.live = {}

    def at(self, f, s):
        return (f, s) if self.zfirst else (s, f)

    def who(self, f, s, y):
        z, x = self.at(f, s)
        return device_at(z, x, y, self.g)

    def copy(self, n, src, dst, dev):
        c = pltpu.make_async_remote_copy(
            src_ref=src, dst_ref=dst, send_sem=self.send.at[n], recv_sem=self.recv.at[n],
            device_id=dev, device_id_type=MESH_ID,
        )
        c.start()
        self.live[n] = c

    def start1(self):
        for i, d in enumerate((1, 3)):
            dev = self.who(lax.rem(self.f + d, 4), self.s, self.y)
            far = lax.rem(self.f + 2, 4)
            self.copy(i, self.grad.at[self.at(far, pl.ds(2 * i, 2))], self.near.at[i], dev)
        for i, d in enumerate((1, 3)):
            nxt = lax.rem(self.f + d, 4)
            dev = self.who(nxt, self.s, self.y)
            self.copy(2 + i, self.grad.at[self.at(nxt, pl.ds(2 * (1 - i), 2))], self.got.at[i, pl.ds(2 * (1 - i), 2)], dev)

    def relay1(self):
        for i, d in enumerate((1, 3)):
            nxt = lax.rem(self.f + d, 4)
            dev = self.who(nxt, self.s, self.y)
            self.live[i].wait_recv()

            @pl.loop(0, 4)
            def _(k):
                a, b = lax.div(k, 2), lax.rem(k, 2)
                own = self.grad[(*self.at(nxt, 2 * i + a), b)].astype(F32)
                self.carry[i, a, b] = (own + self.near[i, a, b].astype(F32)).astype(BF16)

            self.copy(4 + i, self.carry.at[i], self.got.at[i, pl.ds(2 * i, 2)], dev)

    def start2(self):
        for n in (2, 3, 4, 5):
            self.live[n].wait_recv()

        @pl.loop(0, 8)
        def _(k):
            a, b = lax.div(k, 2), lax.rem(k, 2)
            own = self.grad[(*self.at(self.f, a), b)].astype(F32)
            self.part[a, b] = (own + self.got[0, a, b].astype(F32) + self.got[1, a, b].astype(F32)).astype(BF16)

        for i, d in enumerate((1, 3)):
            dev = self.who(self.f, lax.rem(self.s + d, 4), self.y)
            self.copy(6 + i, self.part.at[lax.rem(self.s + 2, 4), i], self.near2.at[i], dev)
        for i, d in enumerate((1, 3)):
            nxt = lax.rem(self.s + d, 4)
            dev = self.who(self.f, nxt, self.y)
            self.copy(8 + i, self.part.at[nxt, 1 - i], self.got2.at[i, 1 - i], dev)

    def relay2(self):
        for i, d in enumerate((1, 3)):
            nxt = lax.rem(self.s + d, 4)
            dev = self.who(self.f, nxt, self.y)
            self.live[6 + i].wait_recv()
            self.carry2[i] = (self.part[nxt, i].astype(F32) + self.near2[i].astype(F32)).astype(BF16)
            self.copy(10 + i, self.carry2.at[i], self.got2.at[i, i], dev)

    def start3(self):
        for n in (8, 9, 10, 11):
            self.live[n].wait_recv()
        for b in range(2):
            own = self.part[self.s, b].astype(F32)
            self.pair[b] = (own + self.got2[0, b].astype(F32) + self.got2[1, b].astype(F32)).astype(BF16)
        other = 1 - self.y
        self.copy(12, self.pair.at[other], self.last, self.who(self.f, self.s, other))

    def finish(self):
        self.live[12].wait_recv()
        return self.pair[self.y].astype(F32) + self.last[...].astype(F32)

    def drain(self):
        for n in range(13):
            self.live[n].wait_send()


def spread_rows(flat, base, per_row, first, block):
    rows, cols = block.shape
    for c in range(cols // 128):
        flat[pl.ds(base + first + c, rows, per_row), :] = block[:, c * 128 : (c + 1) * 128]


def place_piece(item, total, flat):
    if item == QO:
        spread_rows(flat, 0, 2, 0, total[0:40])
        for j in range(5):
            spread_rows(flat, 592, 10, 2 * j, total[40 + 8 * j : 48 + 8 * j])
    elif item == KK:
        spread_rows(flat, 80, 2, 0, total)
    elif item == VV:
        spread_rows(flat, 336, 2, 0, total)
    elif item == DN:
        spread_rows(flat, 1232, 10, 0, total[0:28])
    else:
        first = 0 if item == GU1 else 5
        spread_rows(flat, 672, 7, first, total[0:40])
        spread_rows(flat, 952, 7, first, total[40:80])


def greet(devices):
    barrier = pltpu.get_barrier_semaphore()
    for dev in devices:
        pl.semaphore_signal(barrier, inc=1, device_id=dev, device_id_type=MESH_ID)
    pl.semaphore_wait(barrier, len(devices))


def dp_partners():
    z, x, y, g = place()
    return [
        device_at(lax.rem(z + 1, 4), x, y, g),
        device_at(lax.rem(z + 3, 4), x, y, g),
        device_at(z, lax.rem(x + 1, 4), y, g),
        device_at(z, lax.rem(x + 3, 4), y, g),
        device_at(z, x, 1 - y, g),
    ]


def scatter_kernel(*refs):
    count = len(PIECES)
    grads, flat, rest = refs[:count], refs[count], refs[count + 1 :]
    jobs = [Scatter(i, grads[i], rest[SCATTER_REFS * i : SCATTER_REFS * (i + 1)]) for i in range(count)]
    greet(dp_partners())
    for job in jobs:
        job.start1()
    for job in jobs:
        job.relay1()
    for i in range(count + 2):
        if i < count:
            jobs[i].start2()
        if 0 <= i - 1 < count:
            jobs[i - 1].relay2()
        if 0 <= i - 2 < count:
            jobs[i - 2].start3()
    for i in range(count):
        place_piece(i, jobs[i].finish(), flat)
    for job in jobs:
        job.drain()


def scatter_grads(grads):
    return pl.pallas_call(
        scatter_kernel,
        out_shape=jax.ShapeDtypeStruct((FLAT, 128), F32),
        in_specs=[pl.BlockSpec(memory_space=pltpu.VMEM)] * len(PIECES),
        out_specs=pl.BlockSpec(memory_space=pltpu.VMEM),
        scratch_shapes=scatter_scratch(range(len(PIECES))),
        compiler_params=pltpu.CompilerParams(
            collective_id=0, has_side_effects=True, vmem_limit_bytes=56 * MIB
        ),
    )(*grads)


def shards(
    byte_states,
    patch_states,
    patch_lengths,
    cotangent,
    attention_gain,
    feedforward_gain,
    query_weight,
    key_weight,
    value_weight,
    output_weight,
    gate_weight,
    up_weight,
    down_weight,
    adam_first,
    adam_second,
):
    row_count = byte_states.shape[0]
    seq_count = patch_lengths.shape[0]
    piece_count = lax.axis_size("dp")
    group_count = lax.axis_size("heads")
    share_rows = row_count // group_count
    group_index = lax.axis_index("heads")
    heads_here = query_weight.shape[1] // HEAD
    byte_float = byte_states.astype(jnp.float32)
    byte_share = lax.dynamic_slice_in_dim(byte_float, group_index * share_rows, share_rows, 0)
    normed_bytes = norm_forward(byte_float, attention_gain).astype(jnp.bfloat16)
    query_full = matmul_plain(normed_bytes, query_weight).reshape(row_count, heads_here, HEAD)
    key_full = matmul_plain(patch_states, key_weight).reshape(-1, heads_here, HEAD)
    value_proj = matmul_plain(patch_states, value_weight).astype(jnp.bfloat16)
    query_seq = (
        norm_forward(query_full, 1.0)
        .astype(jnp.bfloat16)
        .reshape(seq_count, BYTES, heads_here, HEAD)
    )
    key_seq = (
        norm_forward(key_full, 1.0)
        .astype(jnp.bfloat16)
        .reshape(seq_count, PATCHES, heads_here, HEAD)
    )
    value_seq = value_proj.reshape(seq_count, PATCHES, heads_here, HEAD)
    before = jnp.arange(PATCHES)[None, :] < jnp.arange(PATCHES)[:, None]
    starts = jnp.sum(jnp.where(before[None], patch_lengths[:, None, :], 0), axis=-1)
    positions = jnp.arange(BYTES, dtype=jnp.int32)
    visible = (starts[:, None, :] <= positions[None, :, None]).astype(jnp.float32)[:, None]
    scores = score_scale * jnp.einsum(
        "sbhd,sphd->shbp", query_seq, key_seq, preferred_element_type=jnp.float32
    )
    weights = jnp.exp(scores) * visible
    probabilities = weights / jnp.sum(weights, axis=-1, keepdims=True)
    prob_half = probabilities.astype(jnp.bfloat16)
    attended = (
        jnp.einsum("shbp,sphd->sbhd", prob_half, value_seq, preferred_element_type=jnp.float32)
        .astype(jnp.bfloat16)
        .reshape(row_count, -1)
    )
    attention_part = matmul_plain(attended, output_weight)
    attention_piece = lax.psum_scatter(
        attention_part.astype(jnp.bfloat16), "heads", scatter_dimension=0, tiled=True
    ).astype(jnp.float32)
    residual_share = byte_share + attention_piece
    normed_share = norm_forward(residual_share, feedforward_gain).astype(jnp.bfloat16)
    normed_hidden = lax.all_gather(normed_share, "heads", axis=0, tiled=True)
    gate = matmul_plain(normed_hidden, gate_weight)
    up_vals = matmul_plain(normed_hidden, up_weight)
    sigmoid = jax.nn.sigmoid(gate)
    activated = gate * sigmoid
    hidden = (activated * up_vals).astype(jnp.bfloat16)
    hidden_grad = matmul_right_t(cotangent, down_weight)
    gate_grad = (hidden_grad * up_vals * (sigmoid * (1.0 + gate * (1.0 - sigmoid)))).astype(
        jnp.bfloat16
    )
    up_grad = (hidden_grad * activated).astype(jnp.bfloat16)
    normed_grad_part = matmul_right_t(gate_grad, gate_weight) + matmul_right_t(up_grad, up_weight)
    grad_gate = matmul_left_t(normed_hidden, gate_grad)
    grad_up = matmul_left_t(normed_hidden, up_grad)
    grad_down = matmul_left_t(hidden, cotangent)
    normed_grad_piece = lax.psum_scatter(
        normed_grad_part.astype(jnp.bfloat16), "heads", scatter_dimension=0, tiled=True
    ).astype(jnp.float32)
    cotangent_share = lax.dynamic_slice_in_dim(cotangent, group_index * share_rows, share_rows, 0)
    residual_grad_share = cotangent_share.astype(jnp.float32) + norm_backward(
        residual_share, feedforward_gain, normed_grad_piece
    )
    residual_half = lax.all_gather(
        residual_grad_share.astype(jnp.bfloat16), "heads", axis=0, tiled=True
    )
    attended_grad = matmul_right_t(residual_half, output_weight).astype(jnp.bfloat16)
    attended_seq = attended_grad.reshape(seq_count, BYTES, heads_here, HEAD)
    prob_grad = jnp.einsum(
        "sbhd,sphd->shbp", attended_seq, value_seq, preferred_element_type=jnp.float32
    )
    score_grad = (
        score_scale
        * probabilities
        * (prob_grad - jnp.sum(probabilities * prob_grad, axis=-1, keepdims=True))
    ).astype(jnp.bfloat16)
    query_normed_grad = jnp.einsum(
        "shbp,sphd->sbhd", score_grad, key_seq, preferred_element_type=jnp.float32
    ).reshape(row_count, heads_here, HEAD)
    key_normed_grad = jnp.einsum(
        "shbp,sbhd->sphd", score_grad, query_seq, preferred_element_type=jnp.float32
    ).reshape(-1, heads_here, HEAD)
    value_grad = (
        jnp.einsum("shbp,sbhd->sphd", prob_half, attended_seq, preferred_element_type=jnp.float32)
        .astype(jnp.bfloat16)
        .reshape(-1, heads_here * HEAD)
    )
    query_grad = (
        norm_backward(query_full, 1.0, query_normed_grad)
        .astype(jnp.bfloat16)
        .reshape(row_count, -1)
    )
    key_grad = (
        norm_backward(key_full, 1.0, key_normed_grad)
        .astype(jnp.bfloat16)
        .reshape(-1, heads_here * HEAD)
    )
    bytes_grad_part = matmul_right_t(query_grad, query_weight)
    patch_grad_part = matmul_right_t(key_grad, key_weight) + matmul_right_t(
        value_grad, value_weight
    )
    bytes_grad_piece, patch_grad_piece = (
        lax.psum_scatter(
            bytes_grad_part.astype(jnp.bfloat16), "heads", scatter_dimension=0, tiled=True
        ).astype(jnp.float32),
        lax.psum_scatter(
            patch_grad_part.astype(jnp.bfloat16), "heads", scatter_dimension=0, tiled=True
        ).astype(jnp.float32),
    )
    input_grad = (
        residual_grad_share + norm_backward(byte_share, attention_gain, bytes_grad_piece)
    ).astype(jnp.bfloat16)
    patch_grad = patch_grad_piece.astype(jnp.bfloat16)
    grad_query = matmul_left_t(normed_bytes, query_grad)
    grad_key = matmul_left_t(patch_states, key_grad)
    grad_value = matmul_left_t(patch_states, value_grad)
    grad_output = matmul_left_t(attended, residual_half)
    gate_up = jnp.concatenate([grad_gate.reshape(32, 40, -1), grad_up.reshape(32, 40, -1)], axis=1).astype(BF16)
    down = jnp.pad(grad_down.reshape(32, 28, -1).astype(BF16), ((0, 0), (0, 4), (0, 0)))
    out_blocks = jnp.swapaxes(grad_output.reshape(32, 8, 5, 256), 1, 2).reshape(32, 40, 256)
    query_out = jnp.concatenate([grad_query.reshape(32, 40, 256), out_blocks], axis=1).astype(BF16)
    grads = [None] * 6
    grads[GU1] = gate_up[:, :, :640]
    grads[GU2] = gate_up[:, :, 640:]
    grads[DN] = down
    grads[KK] = grad_key.astype(BF16)
    grads[VV] = grad_value.astype(BF16)
    grads[QO] = query_out
    summed = scatter_grads([m.reshape(4, 4, 2, r, c) for m, (r, c, _) in zip(grads, PIECES)])
    gradient = summed * float(row_count * piece_count) ** (-0.5)
    adam_first = adam_first.reshape(FLAT, 128)
    adam_second = adam_second.reshape(FLAT, 128)
    new_first = beta_first * adam_first + (1.0 - beta_first) * gradient
    new_second = beta_second * adam_second + (1.0 - beta_second) * gradient * gradient
    adam_step = new_first / bias_first / (jnp.sqrt(new_second / bias_second) + adam_epsilon)
    return (
        input_grad,
        patch_grad,
        new_first.reshape(1, -1),
        new_second.reshape(1, -1),
        adam_step.reshape(1, -1),
    )


def solution(mesh):
    placed = (
        P("dp", None),
        P("dp", None),
        P("dp", None),
        P("dp", None),
        P(),
        P(),
        P(None, "heads"),
        P(None, "heads"),
        P(None, "heads"),
        P("heads", None),
        P(None, "heads"),
        P(None, "heads"),
        P("heads", None),
        P("heads", "dp"),
        P("heads", "dp"),
    )
    return jax.shard_map(
        shards,
        mesh=mesh,
        in_specs=placed,
        out_specs=(
            P(("dp", "heads"), None),
            P(("dp", "heads"), None),
            P("heads", "dp"),
            P("heads", "dp"),
            P("heads", "dp"),
        ),
        check_vma=False,
    )
```

```python
import jax
import jax.numpy as jnp
from jax import lax
from jax.experimental import pallas as pl
from jax.experimental.pallas import tpu as pltpu
from jax.sharding import PartitionSpec as P

HEAD = 128

norm_epsilon = 1e-05
adam_epsilon = 1e-08
beta_first = 0.9
beta_second = 0.95
score_scale = 0.125
bias_first = 1.0 - 0.9**20
bias_second = 1.0 - 0.95**20

BF16 = jnp.bfloat16
F32 = jnp.float32
MESH_ID = pl.DeviceIdType.MESH
MIB = 1 << 20

D = 1280
DG = 4096
UNITS = 896
UNIT_TILES = ((0, 256), (256, 512), (512, 768), (768, 896))
WIDE_TILES = tuple((n, n + 256) for n in range(0, D, 256))
FLAT = 1512

GU1, GU2, DN, KK, VV, QO = range(6)
PIECES = (
    (80, 640, True),
    (80, 256, False),
    (32, 1280, False),
    (128, 256, True),
    (128, 256, False),
    (160, 128, True),
)


def nn(left, right):
    return lax.dot_general(left, right, (((1,), (0,)), ((), ())), preferred_element_type=F32)


def nt(left, right):
    return lax.dot_general(left, right, (((1,), (1,)), ((), ())), preferred_element_type=F32)


def tn(left, right):
    return lax.dot_general(left, right, (((0,), (0,)), ((), ())), preferred_element_type=F32)


def inverse_rms(x):
    return lax.rsqrt(jnp.mean(x * x, axis=-1, keepdims=True) + norm_epsilon)


def norm_backward(x, inverse, scaled):
    inner = jnp.mean(scaled * x, axis=-1, keepdims=True)
    return inverse * scaled - x * (inverse * inverse * inverse) * inner


def place():
    dp = lax.axis_index("dp")
    return lax.div(dp, 8), lax.rem(lax.div(dp, 2), 4), lax.rem(dp, 2), lax.axis_index("heads")


def device_at(z, x, y, g):
    return (z * 8 + x * 2 + y, g)


def remote(src, dst, send, recv, dev):
    return pltpu.make_async_remote_copy(
        src_ref=src, dst_ref=dst, send_sem=send, recv_sem=recv, device_id=dev, device_id_type=MESH_ID
    )


def scatter_scratch(item):
    rows, cols, _ = PIECES[item]
    return [
        pltpu.VMEM((4, 4, 2, rows, cols), BF16),
        pltpu.VMEM((2, 2, 2, rows, cols), BF16),
        pltpu.VMEM((2, 4, 2, rows, cols), BF16),
        pltpu.VMEM((2, rows, cols), BF16),
        pltpu.VMEM((2, 2, rows, cols), BF16),
        pltpu.VMEM((rows, cols), BF16),
        pltpu.SemaphoreType.DMA((13,)),
        pltpu.SemaphoreType.DMA((13,)),
    ]


class Scatter:
    def __init__(self, item, refs):
        self.zfirst = PIECES[item][2]
        self.grad, self.near, self.got, self.near2, self.got2, self.last, self.send, self.recv = refs
        z, x, self.y, self.g = place()
        self.f, self.s = (z, x) if self.zfirst else (x, z)
        self.live = {}

    def at(self, f, s):
        return (f, s) if self.zfirst else (s, f)

    def mine(self, s, y):
        return (*self.at(self.f, s), y)

    def who(self, f, s, y):
        z, x = self.at(f, s)
        return device_at(z, x, y, self.g)

    def copy(self, n, src, dst, dev):
        c = remote(src, dst, self.send.at[n], self.recv.at[n], dev)
        c.start()
        self.live[n] = c

    def start1(self):
        far = lax.rem(self.f + 2, 4)
        for i, d in enumerate((1, 3)):
            dev = self.who(lax.rem(self.f + d, 4), self.s, self.y)
            self.copy(i, self.grad.at[self.at(far, pl.ds(2 * i, 2))], self.near.at[i], dev)
        for i, d in enumerate((1, 3)):
            nxt = lax.rem(self.f + d, 4)
            dev = self.who(nxt, self.s, self.y)
            rest = pl.ds(2 * (1 - i), 2)
            self.copy(2 + i, self.grad.at[self.at(nxt, rest)], self.got.at[i, rest], dev)

    def relay1(self):
        for i, d in enumerate((1, 3)):
            nxt = lax.rem(self.f + d, 4)
            dev = self.who(nxt, self.s, self.y)
            self.live[i].wait_recv()

            @pl.loop(0, 4)
            def _(k):
                a, b = lax.div(k, 2), lax.rem(k, 2)
                own = self.grad[(*self.at(nxt, 2 * i + a), b)].astype(F32)
                self.near[i, a, b] = (own + self.near[i, a, b].astype(F32)).astype(BF16)

            self.copy(4 + i, self.near.at[i], self.got.at[i, pl.ds(2 * i, 2)], dev)

    def start2(self):
        for n in (2, 3, 4, 5):
            self.live[n].wait_recv()

        @pl.loop(0, 8)
        def _(k):
            a, b = lax.div(k, 2), lax.rem(k, 2)
            own = self.grad[self.mine(a, b)].astype(F32)
            total = own + self.got[0, a, b].astype(F32) + self.got[1, a, b].astype(F32)
            self.grad[self.mine(a, b)] = total.astype(BF16)

        for i, d in enumerate((1, 3)):
            dev = self.who(self.f, lax.rem(self.s + d, 4), self.y)
            self.copy(6 + i, self.grad.at[self.mine(lax.rem(self.s + 2, 4), i)], self.near2.at[i], dev)
        for i, d in enumerate((1, 3)):
            nxt = lax.rem(self.s + d, 4)
            dev = self.who(self.f, nxt, self.y)
            self.copy(8 + i, self.grad.at[self.mine(nxt, 1 - i)], self.got2.at[i, 1 - i], dev)

    def relay2(self):
        for i, d in enumerate((1, 3)):
            nxt = lax.rem(self.s + d, 4)
            dev = self.who(self.f, nxt, self.y)
            self.live[6 + i].wait_recv()
            own = self.grad[self.mine(nxt, i)].astype(F32)
            self.near2[i] = (own + self.near2[i].astype(F32)).astype(BF16)
            self.copy(10 + i, self.near2.at[i], self.got2.at[i, i], dev)

    def start3(self):
        for n in (8, 9, 10, 11):
            self.live[n].wait_recv()
        for b in range(2):
            own = self.grad[self.mine(self.s, b)].astype(F32)
            total = own + self.got2[0, b].astype(F32) + self.got2[1, b].astype(F32)
            self.grad[self.mine(self.s, b)] = total.astype(BF16)
        other = 1 - self.y
        self.copy(12, self.grad.at[self.mine(self.s, other)], self.last, self.who(self.f, self.s, other))

    def finish(self):
        self.live[12].wait_recv()
        return self.grad[self.mine(self.s, self.y)].astype(F32) + self.last[...].astype(F32)

    def drain(self):
        for c in self.live.values():
            c.wait_send()


def heads_place():
    g = lax.axis_index("heads")
    y, core = lax.div(g, 2), lax.rem(g, 2)
    return g, y * 2 + 1 - core, (1 - y) * 2 + core, (1 - y) * 2 + 1 - core


def sum_scratch(rows, cols):
    return [
        pltpu.VMEM((2, rows, cols), BF16),
        pltpu.VMEM((rows, cols), BF16),
        pltpu.SemaphoreType.DMA((4,)),
        pltpu.SemaphoreType.DMA((4,)),
    ]


class HeadsSum:
    def __init__(self, parts, rows, refs):
        self.parts, self.rows = parts, rows
        self.near, self.far, self.send, self.recv = refs
        self.live = {}
        self.dp = lax.axis_index("dp")
        self.g, self.mate, self.over, self.over_mate = heads_place()

    def send_near(self, slot):
        quarter = (self.over_mate, self.mate)[slot]
        c = remote(self.parts.at[quarter], self.near.at[slot], self.send.at[slot], self.recv.at[slot], (self.dp, self.mate))
        c.start()
        self.live[slot] = c

    def relay(self):
        self.live[0].wait_recv()
        half = self.rows // 2
        for c in range(2):

            @pl.loop(0, half // 16)
            def _(k):
                at = pl.ds(pl.multiple_of(c * half + 16 * k, 16), 16)
                total = self.near[0, at].astype(F32) + self.parts[self.over, at].astype(F32)
                self.near[0, at] = total.astype(BF16)

            at = pl.ds(c * half, half)
            copy = remote(
                self.near.at[0, at], self.far.at[at], self.send.at[2 + c], self.recv.at[2 + c], (self.dp, self.over)
            )
            copy.start()
            self.live[2 + c] = copy

    def arrive(self, c):
        if c == 0:
            self.live[1].wait_recv()
        self.live[2 + c].wait_recv()

    def total(self, *at):
        return (
            self.parts[(self.g, *at)].astype(F32) + self.near[(1, *at)].astype(F32) + self.far[at].astype(F32)
        )

    def drain(self):
        for c in self.live.values():
            c.wait_send()


class HeadsGather:
    def __init__(self, whole, send, recv):
        self.whole, self.send_sem, self.recv_sem = whole, send, recv
        self.live = {}
        self.dp = lax.axis_index("dp")
        self.g, self.mate, self.over, self.over_mate = heads_place()

    def copy(self, n, quarter, c, dev):
        ref = self.whole.at[quarter, pl.ds(64 * c, 64)]
        copy = remote(ref, ref, self.send_sem.at[n], self.recv_sem.at[n], (self.dp, dev))
        copy.start()
        self.live[n] = copy

    def send(self, c):
        self.copy(c, self.g, c, self.over)
        self.copy(2 + c, self.g, c, self.mate)

    def chip_ready(self):
        for c in range(2):
            self.live[2 + c].wait_recv()

    def forward(self):
        for c in range(2):
            self.live[c].wait_recv()
            self.copy(4 + c, self.over, c, self.mate)

    def all_ready(self):
        for c in range(2):
            self.live[4 + c].wait_recv()

    def drain(self):
        for c in self.live.values():
            c.wait_send()


def spread_rows(flat, start, per_row, block):
    rows, cols = block.shape
    for c in range(cols // 128):
        flat[pl.ds(start + c, rows, per_row), :] = block[:, c * 128 : (c + 1) * 128]


def place_piece(item, total, flat):
    if item == QO:
        for c in range(2):
            spread_rows(flat, c, 2, total[40 * c : 40 * c + 40])
        for c in range(10):
            spread_rows(flat, 592 + c, 10, total[80 + 8 * c : 88 + 8 * c])
    elif item == KK:
        spread_rows(flat, 80, 2, total)
    elif item == VV:
        spread_rows(flat, 336, 2, total)
    elif item == DN:
        spread_rows(flat, 1232, 10, total[0:28])
    else:
        first = 0 if item == GU1 else 5
        spread_rows(flat, 672 + first, 7, total[0:40])
        spread_rows(flat, 952 + first, 7, total[40:80])


def greet():
    z, x, y, g = place()
    dp = lax.axis_index("dp")
    _, mate, over, _ = heads_place()
    partners = [
        (dp, mate),
        (dp, over),
        device_at(lax.rem(z + 1, 4), x, y, g),
        device_at(lax.rem(z + 3, 4), x, y, g),
        device_at(z, lax.rem(x + 1, 4), y, g),
        device_at(z, lax.rem(x + 3, 4), y, g),
        device_at(z, x, 1 - y, g),
    ]
    barrier = pltpu.get_barrier_semaphore()
    for dev in partners:
        pl.semaphore_signal(barrier, inc=1, device_id=dev, device_id_type=MESH_ID)
    pl.semaphore_wait(barrier, len(partners))


def rows_at(first, k, size):
    return pl.ds(pl.multiple_of(first + size * k, size), size)


def layer_scratch():
    quarters = lambda cols, kind: pltpu.VMEM((4, 128, cols), kind)
    plain = dict(
        states=quarters(D, BF16),
        patches=pltpu.VMEM((128, DG), BF16),
        cot=quarters(D, BF16),
        wq=pltpu.VMEM((D, 256), BF16),
        wk=pltpu.VMEM((DG, 256), BF16),
        wv=pltpu.VMEM((DG, 256), BF16),
        wo=pltpu.VMEM((256, D), BF16),
        wg=pltpu.VMEM((D, UNITS), BF16),
        wu=pltpu.VMEM((D, UNITS), BF16),
        wd=pltpu.VMEM((UNITS, D), BF16),
        loads=pltpu.SemaphoreType.DMA((10,)),
        normed=quarters(D, BF16),
        query=quarters(256, F32),
        key=pltpu.VMEM((128, 256), F32),
        keyn=pltpu.VMEM((128, 256), BF16),
        value=pltpu.VMEM((128, 256), BF16),
        att=quarters(256, BF16),
        part1=quarters(D, BF16),
        part2=quarters(D, BF16),
        part4=pltpu.VMEM((4, 32, DG), BF16),
        res=pltpu.VMEM((128, D), F32),
        resg=pltpu.VMEM((128, D), F32),
        nh=quarters(D, BF16),
        rh=quarters(D, BF16),
        turned=pltpu.VMEM((D, 512), BF16),
        attt=pltpu.VMEM((256, 512), BF16),
        hgrad=pltpu.VMEM((512, UNITS), F32),
        gg=pltpu.VMEM((512, UNITS), BF16),
        ug=pltpu.VMEM((512, UNITS), BF16),
        hid=pltpu.VMEM((512, UNITS), BF16),
        qgrad=quarters(256, BF16),
        keyg=pltpu.VMEM((128, 256), F32),
        valg=pltpu.VMEM((128, 256), F32),
        kg=pltpu.VMEM((128, 256), BF16),
        vg=pltpu.VMEM((128, 256), BF16),
        down=pltpu.VMEM((120, D), F32),
        g1s=pltpu.SemaphoreType.DMA((6,)),
        g1r=pltpu.SemaphoreType.DMA((6,)),
        g2s=pltpu.SemaphoreType.DMA((6,)),
        g2r=pltpu.SemaphoreType.DMA((6,)),
    )
    sums = [sum_scratch(128, D), sum_scratch(128, D), sum_scratch(128, D), sum_scratch(32, DG)]
    jobs = [scatter_scratch(i) for i in range(len(PIECES))]
    return plain, sums, jobs


class Refs:
    pass


def layer_kernel(*refs):
    (lengths, again, fgain, states_h, patches_h, cot_h, wq_h, wk_h, wv_h, wo_h, wg_h, wu_h, wd_h,
     flat, out_bytes, out_patches) = refs[:16]
    plain, sums, jobs = layer_scratch()
    rest = list(refs[16:])
    r = Refs()
    for name in plain:
        setattr(r, name, rest.pop(0))
    sum_refs = [[rest.pop(0) for _ in s] for s in sums]
    jobs = [Scatter(i, [rest.pop(0) for _ in s]) for i, s in enumerate(jobs)]
    g, mate, over, over_mate = heads_place()
    own_pair = lax.div(g, 2)

    moves = {}
    order = [
        ("patches", patches_h), ("wk", wk_h), ("wv", wv_h), ("states", states_h), ("wq", wq_h), ("wo", wo_h),
        ("cot", cot_h), ("wd", wd_h), ("wg", wg_h), ("wu", wu_h),
    ]
    for i, (name, src) in enumerate(order):
        moves[name] = pltpu.make_async_copy(src, getattr(r, name), r.loads.at[i])
        moves[name].start()
    greet()

    sum1 = HeadsSum(r.part1, 128, sum_refs[0])
    sum2 = HeadsSum(r.part2, 128, sum_refs[1])
    sum3 = HeadsSum(r.part1, 128, sum_refs[2])
    sum4 = HeadsSum(r.part4, 32, sum_refs[3])
    gather1 = HeadsGather(r.nh, r.g1s, r.g1r)
    gather2 = HeadsGather(r.rh, r.g2s, r.g2r)

    moves["patches"].wait()
    moves["wk"].wait()
    key = nn(r.patches[...], r.wk[...])
    r.key[...] = key
    for h in range(2):
        cols = slice(HEAD * h, HEAD * h + HEAD)
        one = key[:, cols]
        r.keyn[:, cols] = (one * inverse_rms(one)).astype(BF16)
    moves["wv"].wait()
    r.value[...] = nn(r.patches[...], r.wv[...]).astype(BF16)
    earlier = lax.broadcasted_iota(jnp.int32, (128, 128), 0) < lax.broadcasted_iota(jnp.int32, (128, 128), 1)
    spans = jnp.broadcast_to(lengths[...].astype(F32), (16, 128)).astype(BF16)
    starts = nn(spans, earlier.astype(F32).astype(BF16))[0:1]

    def head_probabilities(qi, h):
        cols = slice(HEAD * h, HEAD * h + HEAD)
        full = r.query[qi, :, cols]
        inverse = inverse_rms(full)
        query = (full * inverse).astype(BF16)
        scores = score_scale * nt(query, r.keyn[:, cols])
        position = (lax.broadcasted_iota(jnp.int32, (128, 128), 0) + qi * 128).astype(F32)
        weights = jnp.where(starts <= position, jnp.exp(scores), 0.0)
        return full, inverse, query, weights / jnp.sum(weights, axis=-1, keepdims=True)

    moves["states"].wait()
    moves["wq"].wait()
    moves["wo"].wait()

    def attend(qi):
        @pl.loop(0, 4)
        def _(k):
            at = rows_at(0, k, 32)
            x = r.states[qi, at].astype(F32)
            r.normed[qi, at] = (x * inverse_rms(x) * again[...]).astype(BF16)

        r.query[qi] = nn(r.normed[qi], r.wq[...])
        for h in range(2):
            cols = slice(HEAD * h, HEAD * h + HEAD)
            prob = head_probabilities(qi, h)[3]
            r.att[qi, :, cols] = nn(prob.astype(BF16), r.value[:, cols]).astype(BF16)
        for lo, hi in WIDE_TILES:
            r.part1[qi, :, lo:hi] = nn(r.att[qi], r.wo[:, lo:hi]).astype(BF16)

    attend(over_mate)
    sum1.send_near(0)
    attend(mate)
    sum1.send_near(1)
    attend(over)
    sum1.relay()
    attend(g)

    moves["cot"].wait()
    moves["wd"].wait()

    @pl.loop(0, 2)
    def _(p):
        at = rows_at(0, p, 256)
        cot = r.cot[pl.ds(2 * p, 2)].reshape(256, D)
        for lo, hi in UNIT_TILES:
            r.hgrad[at, lo:hi] = nt(cot, r.wd[lo:hi, :])

    for c in range(2):
        sum1.arrive(c)

        @pl.loop(0, 2)
        def _(k):
            at = rows_at(64 * c, k, 32)
            res = r.states[g, at].astype(F32) + sum1.total(at)
            r.res[at] = res
            r.nh[g, at] = (res * inverse_rms(res) * fgain[...]).astype(BF16)

        gather1.send(c)
    sum1.drain()
    moves["wg"].wait()
    moves["wu"].wait()

    def feed(p):
        at = rows_at(0, p, 256)
        normed = r.nh[pl.ds(2 * p, 2)].reshape(256, D)
        for lo, hi in UNIT_TILES:
            gate = nn(normed, r.wg[:, lo:hi])
            up = nn(normed, r.wu[:, lo:hi])
            back = r.hgrad[at, lo:hi]
            sigma = jax.nn.sigmoid(gate)
            active = gate * sigma
            r.hid[at, lo:hi] = (active * up).astype(BF16)
            r.gg[at, lo:hi] = (back * up * (sigma * (1.0 + gate * (1.0 - sigma)))).astype(BF16)
            r.ug[at, lo:hi] = (back * active).astype(BF16)
        for lo, hi in WIDE_TILES:
            part = nt(r.gg[at], r.wg[lo:hi, :]) + nt(r.ug[at], r.wu[lo:hi, :])
            r.part2[pl.ds(2 * p, 2), :, lo:hi] = part.astype(BF16).reshape(2, 128, hi - lo)

    gather1.chip_ready()
    feed(own_pair)
    sum2.send_near(1)
    gather1.forward()
    gather1.all_ready()
    feed(1 - own_pair)
    sum2.send_near(0)
    sum2.relay()

    for q in range(4):
        r.turned[:, 128 * q : 128 * q + 128] = r.nh[q].T

    @pl.loop(0, 8)
    def _(c):
        rows = r.turned[rows_at(0, c, 160)]
        z, x = lax.div(c, 2), 2 * lax.rem(c, 2)
        for grad, row in ((r.gg, 0), (r.ug, 40)):
            for job, lo, hi in ((GU1, 0, 256), (GU1, 256, 512), (GU1, 512, 640), (GU2, 640, 896)):
                got = nn(rows, grad[:, lo:hi])
                col = lo if job == GU1 else 0
                for j in range(4):
                    jobs[job].grad[z, x + j // 2, j % 2, row : row + 40, col : col + hi - lo] = got[
                        40 * j : 40 * j + 40
                    ].astype(BF16)

    jobs[GU1].start1()
    jobs[GU2].start1()

    for c in range(2):
        sum2.arrive(c)

        @pl.loop(0, 2)
        def _(k):
            at = rows_at(64 * c, k, 32)
            res = r.res[at]
            grad = r.cot[g, at].astype(F32) + norm_backward(res, inverse_rms(res), sum2.total(at) * fgain[...])
            r.resg[at] = grad
            r.rh[g, at] = grad.astype(BF16)

        gather2.send(c)
    sum2.drain()

    for q in range(4):
        r.turned[0:UNITS, 128 * q : 128 * q + 128] = r.hid[128 * q : 128 * q + 128].T
    r.down[112:120] = jnp.zeros((8, D), F32)

    @pl.loop(0, 8)
    def _(c):
        rows = r.turned[rows_at(0, c, 112)]
        for lo, hi in WIDE_TILES:
            r.down[0:112, lo:hi] = nn(rows, r.cot[:, :, lo:hi].reshape(512, hi - lo))
        z, x = lax.div(c, 2), 2 * lax.rem(c, 2)
        for j in range(4):
            jobs[DN].grad[z, x + j // 2, j % 2] = r.down[28 * j : 28 * j + 32].astype(BF16)

    jobs[DN].start1()

    r.keyg[...] = jnp.zeros((128, 256), F32)
    r.valg[...] = jnp.zeros((128, 256), F32)

    def attend_back(qi):
        agrad = nt(r.rh[qi], r.wo[...]).astype(BF16)
        for h in range(2):
            cols = slice(HEAD * h, HEAD * h + HEAD)
            full, inverse, query, prob = head_probabilities(qi, h)
            back = nt(agrad[:, cols], r.value[:, cols])
            inner = jnp.sum(prob * back, axis=-1, keepdims=True)
            score = (score_scale * prob * (back - inner)).astype(BF16)
            grad = nn(score, r.keyn[:, cols])
            r.keyg[:, cols] += tn(score, query)
            r.valg[:, cols] += tn(prob.astype(BF16), agrad[:, cols])
            r.qgrad[qi, :, cols] = norm_backward(full, inverse, grad).astype(BF16)

    attend_back(g)
    gather2.chip_ready()
    attend_back(mate)
    gather2.forward()
    jobs[GU1].relay1()
    jobs[GU2].relay1()
    attend_back(over)
    gather2.all_ready()
    attend_back(over_mate)
    for h in range(2):
        cols = slice(HEAD * h, HEAD * h + HEAD)
        full = r.key[:, cols]
        r.kg[:, cols] = norm_backward(full, inverse_rms(full), r.keyg[:, cols]).astype(BF16)
    r.vg[...] = r.valg[...].astype(BF16)

    @pl.loop(0, 32)
    def _(p):
        rows = r.patches[:, rows_at(0, p, 128)].T
        at = (lax.div(p, 8), lax.rem(lax.div(p, 2), 4), lax.rem(p, 2))
        jobs[KK].grad[at] = nn(rows, r.kg[...]).astype(BF16)
        jobs[VV].grad[at] = nn(rows, r.vg[...]).astype(BF16)

    jobs[KK].start1()
    jobs[VV].start1()
    jobs[DN].relay1()

    for q in range(4):
        r.turned[:, 128 * q : 128 * q + 128] = r.normed[q].T
        r.attt[:, 128 * q : 128 * q + 128] = r.att[q].T
    for half in range(2):
        for lo, hi in ((0, 256), (256, 512), (512, 640)):
            cols = slice(640 * half + lo, 640 * half + hi)
            r.hgrad[256 * half : 256 * half + 256, lo:hi] = nn(
                r.attt[...], r.rh[:, :, cols].reshape(512, hi - lo)
            )

    @pl.loop(0, 4)
    def _(c):
        got = nn(r.turned[rows_at(0, c, 320)], r.qgrad[...].reshape(512, 256))
        for j in range(8):
            mine = got[40 * j : 40 * j + 40]
            halves = [r.hgrad[rows_at(256 * half + 8 * j, c * 8, 8), 0:640] for half in range(2)]
            blocks = [mine[:, :128], mine[:, 128:]]
            blocks += [m[:, 128 * n : 128 * n + 128] for m in halves for n in range(5)]
            jobs[QO].grad[c, j // 2, j % 2] = jnp.concatenate(blocks, axis=0).astype(BF16)

    jobs[QO].start1()

    @pl.loop(0, 2)
    def _(p):
        grad = r.qgrad[pl.ds(2 * p, 2)].reshape(256, 256)
        for lo, hi in WIDE_TILES:
            r.part1[pl.ds(2 * p, 2), :, lo:hi] = nt(grad, r.wq[lo:hi, :]).astype(BF16).reshape(2, 128, hi - lo)

    sum3.send_near(0)
    sum3.send_near(1)

    @pl.loop(0, 16)
    def _(n):
        at = rows_at(0, n, 256)
        part = nt(r.kg[...], r.wk[at]) + nt(r.vg[...], r.wv[at])
        r.part4[:, :, at] = part.astype(BF16).reshape(4, 32, 256)

    sum4.send_near(0)
    sum4.send_near(1)
    sum3.relay()
    sum4.relay()
    for n in (GU1, GU2, DN):
        jobs[n].start2()
    for n in (KK, VV, QO):
        jobs[n].relay1()
    for n in (GU1, GU2, DN):
        jobs[n].relay2()

    for c in range(2):
        sum3.arrive(c)

        @pl.loop(0, 2)
        def _(k):
            at = rows_at(64 * c, k, 32)
            x = r.states[g, at].astype(F32)
            grad = r.resg[at] + norm_backward(x, inverse_rms(x), sum3.total(at) * again[...])
            out_bytes[at] = grad.astype(BF16)

    for c in range(2):
        sum4.arrive(c)

        @pl.loop(0, 4)
        def _(k):
            at = (pl.ds(16 * c, 16), rows_at(0, k, 1024))
            out_patches[at] = sum4.total(*at).astype(BF16)

    for n in (KK, VV, QO):
        jobs[n].start2()
    for n in (GU1, GU2, DN):
        jobs[n].start3()
    for n in (KK, VV, QO):
        jobs[n].relay2()
    for n in (GU1, GU2, DN):
        place_piece(n, jobs[n].finish(), flat)
    for n in (KK, VV, QO):
        jobs[n].start3()
    for n in (KK, VV, QO):
        place_piece(n, jobs[n].finish(), flat)
    for item in (*jobs, sum3, sum4, gather1, gather2):
        item.drain()


def shards(
    byte_states,
    patch_states,
    patch_lengths,
    cotangent,
    attention_gain,
    feedforward_gain,
    query_weight,
    key_weight,
    value_weight,
    output_weight,
    gate_weight,
    up_weight,
    down_weight,
    adam_first,
    adam_second,
):
    row_count = byte_states.shape[0]
    piece_count = lax.axis_size("dp")
    plain, sums, jobs = layer_scratch()
    vmem = pl.BlockSpec(memory_space=pltpu.VMEM)
    summed, input_grad, patch_grad = pl.pallas_call(
        layer_kernel,
        out_shape=(
            jax.ShapeDtypeStruct((FLAT, 128), F32),
            jax.ShapeDtypeStruct((128, D), BF16),
            jax.ShapeDtypeStruct((32, DG), BF16),
        ),
        in_specs=[vmem] * 3 + [pl.BlockSpec(memory_space=pl.ANY)] * 10,
        out_specs=(vmem, vmem, vmem),
        scratch_shapes=[*plain.values(), *(s for group in (*sums, *jobs) for s in group)],
        compiler_params=pltpu.CompilerParams(
            collective_id=0, has_side_effects=True, vmem_limit_bytes=63 * MIB
        ),
    )(
        patch_lengths,
        attention_gain.reshape(1, D),
        feedforward_gain.reshape(1, D),
        byte_states.reshape(4, 128, D),
        patch_states,
        cotangent.reshape(4, 128, D),
        query_weight,
        key_weight,
        value_weight,
        output_weight,
        gate_weight,
        up_weight,
        down_weight,
    )
    gradient = summed * float(row_count * piece_count) ** (-0.5)
    new_first = beta_first * adam_first.reshape(FLAT, 128) + (1.0 - beta_first) * gradient
    new_second = beta_second * adam_second.reshape(FLAT, 128) + (1.0 - beta_second) * gradient * gradient
    adam_step = new_first / bias_first / (jnp.sqrt(new_second / bias_second) + adam_epsilon)
    return (
        input_grad,
        patch_grad,
        new_first.reshape(1, -1),
        new_second.reshape(1, -1),
        adam_step.reshape(1, -1),
    )


def solution(mesh):
    placed = (
        P("dp", None),
        P("dp", None),
        P("dp", None),
        P("dp", None),
        P(),
        P(),
        P(None, "heads"),
        P(None, "heads"),
        P(None, "heads"),
        P("heads", None),
        P(None, "heads"),
        P(None, "heads"),
        P("heads", None),
        P("heads", "dp"),
        P("heads", "dp"),
    )
    return jax.shard_map(
        shards,
        mesh=mesh,
        in_specs=placed,
        out_specs=(
            P(("dp", "heads"), None),
            P(("dp", "heads"), None),
            P("heads", "dp"),
            P("heads", "dp"),
            P("heads", "dp"),
        ),
        check_vma=False,
    )
```

```python
import jax
import jax.numpy as jnp
from jax import lax
from jax.experimental import pallas as pl
from jax.experimental.pallas import tpu as pltpu
from jax.sharding import PartitionSpec as P

HEAD = 128

norm_epsilon = 1e-05
adam_epsilon = 1e-08
beta_first = 0.9
beta_second = 0.95
score_scale = 0.125
bias_first = 1.0 - 0.9**20
bias_second = 1.0 - 0.95**20

BF16 = jnp.bfloat16
F32 = jnp.float32
MESH_ID = pl.DeviceIdType.MESH
MIB = 1 << 20

D = 1280
DG = 4096
UNITS = 896
UNIT_TILES = ((0, 256), (256, 512), (512, 768), (768, 896))
WIDE_TILES = tuple((n, n + 256) for n in range(0, D, 256))
FLAT = 1512

GU1, GU2, DN, KK, VV, QO = range(6)
PIECES = (
    (80, 640, True),
    (80, 256, False),
    (32, 1280, False),
    (128, 256, True),
    (128, 256, False),
    (160, 128, True),
)


def nn(left, right):
    return lax.dot_general(left, right, (((1,), (0,)), ((), ())), preferred_element_type=F32)


def nt(left, right):
    return lax.dot_general(left, right, (((1,), (1,)), ((), ())), preferred_element_type=F32)


def tn(left, right):
    return lax.dot_general(left, right, (((0,), (0,)), ((), ())), preferred_element_type=F32)


def inverse_rms(x):
    return lax.rsqrt(jnp.mean(x * x, axis=-1, keepdims=True) + norm_epsilon)


def norm_backward(x, inverse, scaled):
    inner = jnp.mean(scaled * x, axis=-1, keepdims=True)
    return inverse * scaled - x * (inverse * inverse * inverse) * inner


def place():
    dp = lax.axis_index("dp")
    return lax.div(dp, 8), lax.rem(lax.div(dp, 2), 4), lax.rem(dp, 2), lax.axis_index("heads")


def device_at(z, x, y, g):
    return (z * 8 + x * 2 + y, g)


def remote(src, dst, send, recv, dev):
    return pltpu.make_async_remote_copy(
        src_ref=src, dst_ref=dst, send_sem=send, recv_sem=recv, device_id=dev, device_id_type=MESH_ID
    )


def scatter_scratch(item):
    rows, cols, _ = PIECES[item]
    return [
        pltpu.VMEM((4, 4, 2, rows, cols), BF16),
        pltpu.VMEM((2, 2, 2, rows, cols), BF16),
        pltpu.VMEM((2, 4, 2, rows, cols), BF16),
        pltpu.VMEM((2, rows, cols), BF16),
        pltpu.VMEM((2, 2, rows, cols), BF16),
        pltpu.VMEM((rows, cols), BF16),
        pltpu.SemaphoreType.DMA((13,)),
        pltpu.SemaphoreType.DMA((13,)),
    ]


class Scatter:
    def __init__(self, item, refs):
        self.zfirst = PIECES[item][2]
        self.grad, self.near, self.got, self.near2, self.got2, self.last, self.send, self.recv = refs
        z, x, self.y, self.g = place()
        self.f, self.s = (z, x) if self.zfirst else (x, z)
        self.live = {}

    def at(self, f, s):
        return (f, s) if self.zfirst else (s, f)

    def mine(self, s, y):
        return (*self.at(self.f, s), y)

    def who(self, f, s, y):
        z, x = self.at(f, s)
        return device_at(z, x, y, self.g)

    def copy(self, n, src, dst, dev):
        c = remote(src, dst, self.send.at[n], self.recv.at[n], dev)
        c.start()
        self.live[n] = c

    def start1(self):
        far = lax.rem(self.f + 2, 4)
        for i, d in enumerate((1, 3)):
            dev = self.who(lax.rem(self.f + d, 4), self.s, self.y)
            self.copy(i, self.grad.at[self.at(far, pl.ds(2 * i, 2))], self.near.at[i], dev)
        for i, d in enumerate((1, 3)):
            nxt = lax.rem(self.f + d, 4)
            dev = self.who(nxt, self.s, self.y)
            rest = pl.ds(2 * (1 - i), 2)
            self.copy(2 + i, self.grad.at[self.at(nxt, rest)], self.got.at[i, rest], dev)

    def relay1(self):
        for i, d in enumerate((1, 3)):
            nxt = lax.rem(self.f + d, 4)
            dev = self.who(nxt, self.s, self.y)
            self.live[i].wait_recv()

            @pl.loop(0, 4)
            def _(k):
                a, b = lax.div(k, 2), lax.rem(k, 2)
                own = self.grad[(*self.at(nxt, 2 * i + a), b)].astype(F32)
                self.near[i, a, b] = (own + self.near[i, a, b].astype(F32)).astype(BF16)

            self.copy(4 + i, self.near.at[i], self.got.at[i, pl.ds(2 * i, 2)], dev)

    def start2(self):
        for n in (2, 3, 4, 5):
            self.live[n].wait_recv()

        @pl.loop(0, 8)
        def _(k):
            a, b = lax.div(k, 2), lax.rem(k, 2)
            own = self.grad[self.mine(a, b)].astype(F32)
            total = own + self.got[0, a, b].astype(F32) + self.got[1, a, b].astype(F32)
            self.grad[self.mine(a, b)] = total.astype(BF16)

        for i, d in enumerate((1, 3)):
            dev = self.who(self.f, lax.rem(self.s + d, 4), self.y)
            self.copy(6 + i, self.grad.at[self.mine(lax.rem(self.s + 2, 4), i)], self.near2.at[i], dev)
        for i, d in enumerate((1, 3)):
            nxt = lax.rem(self.s + d, 4)
            dev = self.who(self.f, nxt, self.y)
            self.copy(8 + i, self.grad.at[self.mine(nxt, 1 - i)], self.got2.at[i, 1 - i], dev)

    def relay2(self):
        for i, d in enumerate((1, 3)):
            nxt = lax.rem(self.s + d, 4)
            dev = self.who(self.f, nxt, self.y)
            self.live[6 + i].wait_recv()
            own = self.grad[self.mine(nxt, i)].astype(F32)
            self.near2[i] = (own + self.near2[i].astype(F32)).astype(BF16)
            self.copy(10 + i, self.near2.at[i], self.got2.at[i, i], dev)

    def start3(self):
        for n in (8, 9, 10, 11):
            self.live[n].wait_recv()
        for b in range(2):
            own = self.grad[self.mine(self.s, b)].astype(F32)
            total = own + self.got2[0, b].astype(F32) + self.got2[1, b].astype(F32)
            self.grad[self.mine(self.s, b)] = total.astype(BF16)
        other = 1 - self.y
        self.copy(12, self.grad.at[self.mine(self.s, other)], self.last, self.who(self.f, self.s, other))

    def finish(self):
        self.live[12].wait_recv()
        return self.grad[self.mine(self.s, self.y)].astype(F32) + self.last[...].astype(F32)

    def drain(self):
        for c in self.live.values():
            c.wait_send()


def heads_place():
    g = lax.axis_index("heads")
    y, core = lax.div(g, 2), lax.rem(g, 2)
    return g, y * 2 + 1 - core, (1 - y) * 2 + core, (1 - y) * 2 + 1 - core


def sum_scratch(rows, cols):
    return [
        pltpu.VMEM((2, rows, cols), BF16),
        pltpu.VMEM((rows, cols), BF16),
        pltpu.SemaphoreType.DMA((4,)),
        pltpu.SemaphoreType.DMA((4,)),
    ]


def pair_scratch():
    return [
        pltpu.VMEM((2, 128, D), BF16),
        pltpu.VMEM((2, 128, D), BF16),
        pltpu.SemaphoreType.DMA((6,)),
        pltpu.SemaphoreType.DMA((6,)),
    ]


class HeadsSum:
    def __init__(self, parts, rows, refs):
        self.parts, self.rows = parts, rows
        self.near, self.far, self.send, self.recv = refs
        self.live = {}
        self.dp = lax.axis_index("dp")
        self.g, self.mate, self.over, self.over_mate = heads_place()

    def send_near(self, slot):
        quarter = (self.over_mate, self.mate)[slot]
        c = remote(self.parts.at[quarter], self.near.at[slot], self.send.at[slot], self.recv.at[slot], (self.dp, self.mate))
        c.start()
        self.live[slot] = c

    def relay(self):
        self.live[0].wait_recv()
        half = self.rows // 2
        for c in range(2):

            @pl.loop(0, half // 16)
            def _(k):
                at = pl.ds(pl.multiple_of(c * half + 16 * k, 16), 16)
                total = self.near[0, at].astype(F32) + self.parts[self.over, at].astype(F32)
                self.near[0, at] = total.astype(BF16)

            at = pl.ds(c * half, half)
            copy = remote(
                self.near.at[0, at], self.far.at[at], self.send.at[2 + c], self.recv.at[2 + c], (self.dp, self.over)
            )
            copy.start()
            self.live[2 + c] = copy

    def arrive(self, c):
        if c == 0:
            self.live[1].wait_recv()
        self.live[2 + c].wait_recv()

    def total(self, *at):
        return (
            self.parts[(self.g, *at)].astype(F32) + self.near[(1, *at)].astype(F32) + self.far[at].astype(F32)
        )

    def drain(self):
        for c in self.live.values():
            c.wait_send()


class PairSum:
    def __init__(self, parts, refs):
        self.parts = parts
        self.near, self.far, self.send, self.recv = refs
        self.live = {}
        self.dp = lax.axis_index("dp")
        self.g, self.mate, self.over, _ = heads_place()
        self.core = lax.rem(self.g, 2)

    def copy(self, n, src, dst, dev):
        c = remote(src, dst, self.send.at[n], self.recv.at[n], (self.dp, dev))
        c.start()
        self.live[n] = c

    def send_near(self, b):
        self.copy(b, self.parts.at[2 * b + 1 - self.core], self.near.at[b], self.mate)

    def relay(self, b):
        self.live[b].wait_recv()
        for c in range(2):

            @pl.loop(0, 4)
            def _(k):
                at = pl.ds(pl.multiple_of(c * 64 + 16 * k, 16), 16)
                total = self.near[b, at].astype(F32) + self.parts[2 * b + self.core, at].astype(F32)
                self.near[b, at] = total.astype(BF16)

            at = pl.ds(c * 64, 64)
            self.copy(2 + 2 * b + c, self.near.at[b, at], self.far.at[b, at], self.over)

    def arrive(self, b, c):
        self.live[2 + 2 * b + c].wait_recv()

    def total(self, b, at):
        return self.near[b, at].astype(F32) + self.far[b, at].astype(F32)

    def drain(self):
        for c in self.live.values():
            c.wait_send()


class CoreSwap:
    def __init__(self, whole, send, recv):
        self.whole, self.send_sem, self.recv_sem = whole, send, recv
        self.live = {}
        self.dp = lax.axis_index("dp")
        self.g, self.mate, _, _ = heads_place()
        self.core = lax.rem(self.g, 2)

    def give(self, b, c):
        n = 2 * b + c
        ref = self.whole.at[2 * b + self.core, pl.ds(64 * c, 64)]
        copy = remote(ref, ref, self.send_sem.at[n], self.recv_sem.at[n], (self.dp, self.mate))
        copy.start()
        self.live[n] = copy

    def take(self, b):
        for c in range(2):
            self.live[2 * b + c].wait_recv()

    def drain(self):
        for c in self.live.values():
            c.wait_send()


def spread_rows(flat, start, per_row, block):
    rows, cols = block.shape
    for c in range(cols // 128):
        flat[pl.ds(start + c, rows, per_row), :] = block[:, c * 128 : (c + 1) * 128]


def place_piece(item, total, flat):
    if item == QO:
        for c in range(2):
            spread_rows(flat, c, 2, total[40 * c : 40 * c + 40])
        for c in range(10):
            spread_rows(flat, 592 + c, 10, total[80 + 8 * c : 88 + 8 * c])
    elif item == KK:
        spread_rows(flat, 80, 2, total)
    elif item == VV:
        spread_rows(flat, 336, 2, total)
    elif item == DN:
        spread_rows(flat, 1232, 10, total[0:28])
    else:
        first = 0 if item == GU1 else 5
        spread_rows(flat, 672 + first, 7, total[0:40])
        spread_rows(flat, 952 + first, 7, total[40:80])


def greet():
    z, x, y, g = place()
    dp = lax.axis_index("dp")
    _, mate, over, _ = heads_place()
    partners = [
        (dp, mate),
        (dp, over),
        device_at(lax.rem(z + 1, 4), x, y, g),
        device_at(lax.rem(z + 3, 4), x, y, g),
        device_at(z, lax.rem(x + 1, 4), y, g),
        device_at(z, lax.rem(x + 3, 4), y, g),
        device_at(z, x, 1 - y, g),
    ]
    barrier = pltpu.get_barrier_semaphore()
    for dev in partners:
        pl.semaphore_signal(barrier, inc=1, device_id=dev, device_id_type=MESH_ID)
    pl.semaphore_wait(barrier, len(partners))


def rows_at(first, k, size):
    return pl.ds(pl.multiple_of(first + size * k, size), size)


def layer_scratch():
    quarters = lambda cols, kind: pltpu.VMEM((4, 128, cols), kind)
    plain = dict(
        states=quarters(D, BF16),
        patches=pltpu.VMEM((128, DG), BF16),
        cot=quarters(D, BF16),
        wq=pltpu.VMEM((D, 256), BF16),
        wk=pltpu.VMEM((DG, 256), BF16),
        wv=pltpu.VMEM((DG, 256), BF16),
        wo=pltpu.VMEM((256, D), BF16),
        wg=pltpu.VMEM((D, UNITS), BF16),
        wu=pltpu.VMEM((D, UNITS), BF16),
        wd=pltpu.VMEM((UNITS, D), BF16),
        loads=pltpu.SemaphoreType.DMA((10,)),
        normed=quarters(D, BF16),
        query=quarters(256, F32),
        key=pltpu.VMEM((128, 256), F32),
        keyn=pltpu.VMEM((128, 256), BF16),
        value=pltpu.VMEM((128, 256), BF16),
        att=quarters(256, BF16),
        part1=quarters(D, BF16),
        part2=quarters(D, BF16),
        part4=pltpu.VMEM((4, 32, DG), BF16),
        res=pltpu.VMEM((2, 128, D), F32),
        gain1=pltpu.VMEM((1, D), F32),
        gain2=pltpu.VMEM((1, D), F32),
        nh=quarters(D, BF16),
        rh=quarters(D, BF16),
        turned=pltpu.VMEM((D, 512), BF16),
        hgrad=pltpu.VMEM((512, UNITS), F32),
        gg=pltpu.VMEM((512, UNITS), BF16),
        ug=pltpu.VMEM((512, UNITS), BF16),
        qgrad=quarters(256, BF16),
        keyg=pltpu.VMEM((128, 256), F32),
        valg=pltpu.VMEM((128, 256), F32),
        kg=pltpu.VMEM((128, 256), BF16),
        vg=pltpu.VMEM((128, 256), BF16),
        down=pltpu.VMEM((120, D), F32),
        g1s=pltpu.SemaphoreType.DMA((4,)),
        g1r=pltpu.SemaphoreType.DMA((4,)),
        g2s=pltpu.SemaphoreType.DMA((4,)),
        g2r=pltpu.SemaphoreType.DMA((4,)),
    )
    sums = [pair_scratch(), pair_scratch(), sum_scratch(128, D), sum_scratch(32, DG)]
    jobs = [scatter_scratch(i) for i in range(len(PIECES))]
    return plain, sums, jobs


class Refs:
    pass


def layer_kernel(*refs):
    (lengths, again, fgain, states_h, patches_h, cot_h, wq_h, wk_h, wv_h, wo_h, wg_h, wu_h, wd_h,
     flat, out_bytes, out_patches) = refs[:16]
    plain, sums, jobs = layer_scratch()
    rest = list(refs[16:])
    r = Refs()
    for name in plain:
        setattr(r, name, rest.pop(0))
    r.hid = r.wd.at[0:512, 0:UNITS]
    r.attt = r.wd.at[512:768, 0:512]
    sum_refs = [[rest.pop(0) for _ in s] for s in sums]
    jobs = [Scatter(i, [rest.pop(0) for _ in s]) for i, s in enumerate(jobs)]
    g, _, _, _ = heads_place()
    core = lax.rem(g, 2)

    moves = {}
    order = [
        ("patches", patches_h), ("wk", wk_h), ("wv", wv_h), ("states", states_h), ("wq", wq_h), ("wo", wo_h),
        ("cot", cot_h), ("wd", wd_h), ("wg", wg_h), ("wu", wu_h),
    ]
    for i, (name, src) in enumerate(order):
        moves[name] = pltpu.make_async_copy(src, getattr(r, name), r.loads.at[i])
    for name in ("patches", "wk", "wv", "states", "wq"):
        moves[name].start()
    r.gain1[...] = again[...].reshape(1, D)
    r.gain2[...] = fgain[...].reshape(1, D)
    greet()

    sum1 = PairSum(r.part1, sum_refs[0])
    sum2 = PairSum(r.part2, sum_refs[1])
    sum3 = HeadsSum(r.part1, 128, sum_refs[2])
    sum4 = HeadsSum(r.part4, 32, sum_refs[3])
    swap1 = CoreSwap(r.nh, r.g1s, r.g1r)
    swap2 = CoreSwap(r.rh, r.g2s, r.g2r)

    moves["patches"].wait()
    moves["wk"].wait()
    for name in ("wo", "cot", "wd", "wg", "wu"):
        moves[name].start()
    key = nn(r.patches[...], r.wk[...])
    r.key[...] = key
    for h in range(2):
        cols = slice(HEAD * h, HEAD * h + HEAD)
        one = key[:, cols]
        r.keyn[:, cols] = (one * inverse_rms(one)).astype(BF16)
    moves["wv"].wait()
    r.value[...] = nn(r.patches[...], r.wv[...]).astype(BF16)
    earlier = lax.broadcasted_iota(jnp.int32, (128, 128), 0) < lax.broadcasted_iota(jnp.int32, (128, 128), 1)
    spans = jnp.broadcast_to(lengths[...].astype(F32), (16, 128)).astype(BF16)
    starts = nn(spans, earlier.astype(F32).astype(BF16))[0:1]

    def head_probabilities(qi, h):
        cols = slice(HEAD * h, HEAD * h + HEAD)
        full = r.query[qi, :, cols]
        inverse = inverse_rms(full)
        query = (full * inverse).astype(BF16)
        scores = score_scale * nt(query, r.keyn[:, cols])
        position = (lax.broadcasted_iota(jnp.int32, (128, 128), 0) + qi * 128).astype(F32)
        weights = jnp.where(starts <= position, jnp.exp(scores), 0.0)
        return full, inverse, query, weights / jnp.sum(weights, axis=-1, keepdims=True)

    moves["states"].wait()
    moves["wq"].wait()
    moves["wo"].wait()

    def attend(qi):
        @pl.loop(0, 4)
        def _(k):
            at = rows_at(0, k, 32)
            x = r.states[qi, at].astype(F32)
            r.normed[qi, at] = (x * inverse_rms(x) * r.gain1[...]).astype(BF16)

        r.query[qi] = nn(r.normed[qi], r.wq[...])
        for h in range(2):
            cols = slice(HEAD * h, HEAD * h + HEAD)
            prob = head_probabilities(qi, h)[3]
            r.att[qi, :, cols] = nn(prob.astype(BF16), r.value[:, cols]).astype(BF16)
        for lo, hi in WIDE_TILES:
            r.part1[qi, :, lo:hi] = nn(r.att[qi], r.wo[:, lo:hi]).astype(BF16)

    for b in range(2):
        attend(2 * b + 1 - core)
        sum1.send_near(b)
        attend(2 * b + core)
        sum1.relay(b)

    moves["cot"].wait()
    moves["wd"].wait()

    @pl.loop(0, 2)
    def _(p):
        at = rows_at(0, p, 256)
        cot = r.cot[pl.ds(2 * p, 2)].reshape(256, D)
        for lo, hi in UNIT_TILES:
            r.hgrad[at, lo:hi] = nt(cot, r.wd[lo:hi, :])

    def residual(b):
        for c in range(2):
            sum1.arrive(b, c)

            @pl.loop(0, 2)
            def _(k):
                at = rows_at(64 * c, k, 32)
                res = r.states[2 * b + core, at].astype(F32) + sum1.total(b, at)
                r.res[b, at] = res
                r.nh[2 * b + core, at] = (res * inverse_rms(res) * r.gain2[...]).astype(BF16)

            swap1.give(b, c)

    def residual_back(b):
        for c in range(2):
            sum2.arrive(b, c)

            @pl.loop(0, 2)
            def _(k):
                at = rows_at(64 * c, k, 32)
                res = r.res[b, at]
                grad = norm_backward(res, inverse_rms(res), sum2.total(b, at) * r.gain2[...])
                grad = grad + r.cot[2 * b + core, at].astype(F32)
                r.res[b, at] = grad
                r.rh[2 * b + core, at] = grad.astype(BF16)

            swap2.give(b, c)

    residual(0)
    moves["wg"].wait()
    moves["wu"].wait()

    def feed(p):
        at = slice(256 * p, 256 * p + 256)
        normed = r.nh[pl.ds(2 * p, 2)].reshape(256, D)
        for lo, hi in UNIT_TILES:
            gate = nn(normed, r.wg[:, lo:hi])
            up = nn(normed, r.wu[:, lo:hi])
            back = r.hgrad[at, lo:hi]
            sigma = jax.nn.sigmoid(gate)
            active = gate * sigma
            r.hid[at, lo:hi] = (active * up).astype(BF16)
            r.gg[at, lo:hi] = (back * up * (sigma * (1.0 + gate * (1.0 - sigma)))).astype(BF16)
            r.ug[at, lo:hi] = (back * active).astype(BF16)
        for lo, hi in WIDE_TILES:
            part = nt(r.gg[at], r.wg[lo:hi, :]) + nt(r.ug[at], r.wu[lo:hi, :])
            r.part2[pl.ds(2 * p, 2), :, lo:hi] = part.astype(BF16).reshape(2, 128, hi - lo)

    def store(ref, at, rows, cols, new, again_):
        at = (*at, rows, cols)
        if again_:
            new = new + ref[at].astype(F32)
        ref[at] = new.astype(BF16)

    def turn(p):
        for q in (2 * p, 2 * p + 1):
            r.turned[:, 128 * q : 128 * q + 128] = r.nh[q].T

    def gate_up_grads(p):
        @pl.loop(0, 8)
        def _(c):
            rows = r.turned[rows_at(0, c, 160), 256 * p : 256 * p + 256]
            z, x = lax.div(c, 2), 2 * lax.rem(c, 2)
            for grad, row in ((r.gg, 0), (r.ug, 40)):
                for job, lo, hi in ((GU1, 0, 256), (GU1, 256, 512), (GU1, 512, 640), (GU2, 640, 896)):
                    got = nn(rows, grad[256 * p : 256 * p + 256, lo:hi])
                    col = lo if job == GU1 else 0
                    for j in range(4):
                        store(
                            jobs[job].grad, (z, x + j // 2, j % 2), slice(row, row + 40), slice(col, col + hi - lo),
                            got[40 * j : 40 * j + 40], p,
                        )

    def down_grads(p):
        for q in (2 * p, 2 * p + 1):
            r.turned[0:UNITS, 128 * q : 128 * q + 128] = r.hid[128 * q : 128 * q + 128].T

        @pl.loop(0, 8)
        def _(c):
            rows = r.turned[rows_at(0, c, 112), 256 * p : 256 * p + 256]
            for lo, hi in WIDE_TILES:
                r.down[0:112, lo:hi] = nn(rows, r.cot[2 * p : 2 * p + 2, :, lo:hi].reshape(256, hi - lo))
            z, x = lax.div(c, 2), 2 * lax.rem(c, 2)
            for j in range(4):
                store(
                    jobs[DN].grad, (z, x + j // 2, j % 2), slice(0, 32), slice(0, D), r.down[28 * j : 28 * j + 32], p
                )

    r.down[112:120] = jnp.zeros((8, D), F32)
    swap1.take(0)
    feed(0)
    sum2.send_near(0)
    turn(0)
    sum2.relay(0)
    gate_up_grads(0)
    residual(1)
    down_grads(0)
    swap1.take(1)
    sum1.drain()
    feed(1)
    sum2.send_near(1)
    turn(1)
    sum2.relay(1)
    gate_up_grads(1)
    jobs[GU1].start1()
    jobs[GU2].start1()
    residual_back(0)
    down_grads(1)
    jobs[DN].start1()

    r.keyg[...] = jnp.zeros((128, 256), F32)
    r.valg[...] = jnp.zeros((128, 256), F32)

    def attend_back(qi):
        agrad = nt(r.rh[qi], r.wo[...]).astype(BF16)
        for h in range(2):
            cols = slice(HEAD * h, HEAD * h + HEAD)
            full, inverse, query, prob = head_probabilities(qi, h)
            back = nt(agrad[:, cols], r.value[:, cols])
            inner = jnp.sum(prob * back, axis=-1, keepdims=True)
            score = (score_scale * prob * (back - inner)).astype(BF16)
            grad = nn(score, r.keyn[:, cols])
            r.keyg[:, cols] += tn(score, query)
            r.valg[:, cols] += tn(prob.astype(BF16), agrad[:, cols])
            r.qgrad[qi, :, cols] = norm_backward(full, inverse, grad).astype(BF16)

    attend_back(core)
    swap2.take(0)
    attend_back(1 - core)
    residual_back(1)
    jobs[GU1].relay1()
    jobs[GU2].relay1()
    attend_back(2 + core)
    swap2.take(1)
    sum2.drain()
    attend_back(3 - core)
    for h in range(2):
        cols = slice(HEAD * h, HEAD * h + HEAD)
        full = r.key[:, cols]
        r.kg[:, cols] = norm_backward(full, inverse_rms(full), r.keyg[:, cols]).astype(BF16)
    r.vg[...] = r.valg[...].astype(BF16)

    @pl.loop(0, 8)
    def _(n):
        rows = r.patches[:, rows_at(0, n, 512)].T
        z, x = lax.div(n, 2), 2 * lax.rem(n, 2)
        for job, grad in ((KK, r.kg), (VV, r.vg)):
            got = nn(rows, grad[...]).astype(BF16)
            for j in range(4):
                jobs[job].grad[z, x + j // 2, j % 2] = got[128 * j : 128 * j + 128]

    jobs[KK].start1()
    jobs[VV].start1()
    jobs[DN].relay1()

    for q in range(4):
        r.turned[:, 128 * q : 128 * q + 128] = r.normed[q].T
        r.attt[:, 128 * q : 128 * q + 128] = r.att[q].T
    for half in range(2):
        for lo, hi in ((0, 256), (256, 512), (512, 640)):
            cols = slice(640 * half + lo, 640 * half + hi)
            r.hgrad[256 * half : 256 * half + 256, lo:hi] = nn(
                r.attt[...], r.rh[:, :, cols].reshape(512, hi - lo)
            )

    @pl.loop(0, 4)
    def _(c):
        got = nn(r.turned[rows_at(0, c, 320)], r.qgrad[...].reshape(512, 256))
        for j in range(8):
            mine = got[40 * j : 40 * j + 40]
            halves = [r.hgrad[rows_at(256 * half + 8 * j, c * 8, 8), 0:640] for half in range(2)]
            blocks = [mine[:, :128], mine[:, 128:]]
            blocks += [m[:, 128 * n : 128 * n + 128] for m in halves for n in range(5)]
            jobs[QO].grad[c, j // 2, j % 2] = jnp.concatenate(blocks, axis=0).astype(BF16)

    jobs[QO].start1()

    @pl.loop(0, 2)
    def _(p):
        grad = r.qgrad[pl.ds(2 * p, 2)].reshape(256, 256)
        for lo, hi in WIDE_TILES:
            r.part1[pl.ds(2 * p, 2), :, lo:hi] = nt(grad, r.wq[lo:hi, :]).astype(BF16).reshape(2, 128, hi - lo)

    sum3.send_near(0)
    sum3.send_near(1)

    @pl.loop(0, 16)
    def _(n):
        at = rows_at(0, n, 256)
        part = nt(r.kg[...], r.wk[at]) + nt(r.vg[...], r.wv[at])
        r.part4[:, :, at] = part.astype(BF16).reshape(4, 32, 256)

    sum4.send_near(0)
    sum4.send_near(1)
    sum3.relay()
    sum4.relay()
    for n in (GU1, GU2, DN):
        jobs[n].start2()
    for n in (KK, VV, QO):
        jobs[n].relay1()
    for n in (GU1, GU2, DN):
        jobs[n].relay2()

    for c in range(2):
        sum3.arrive(c)

        @pl.loop(0, 2)
        def _(k):
            at = rows_at(64 * c, k, 32)
            x = r.states[g, at].astype(F32)
            grad = r.res[lax.div(g, 2), at] + norm_backward(x, inverse_rms(x), sum3.total(at) * r.gain1[...])
            out_bytes[at] = grad.astype(BF16)

    for c in range(2):
        sum4.arrive(c)

        @pl.loop(0, 4)
        def _(k):
            at = (pl.ds(16 * c, 16), rows_at(0, k, 1024))
            out_patches[at] = sum4.total(*at).astype(BF16)

    for n in (KK, VV, QO):
        jobs[n].start2()
    for n in (GU1, GU2, DN):
        jobs[n].start3()
    for n in (KK, VV, QO):
        jobs[n].relay2()
    for n in (GU1, GU2, DN):
        place_piece(n, jobs[n].finish(), flat)
    for n in (KK, VV, QO):
        jobs[n].start3()
    for n in (KK, VV, QO):
        place_piece(n, jobs[n].finish(), flat)
    for item in (*jobs, sum3, sum4, swap1, swap2):
        item.drain()


def shards(
    byte_states,
    patch_states,
    patch_lengths,
    cotangent,
    attention_gain,
    feedforward_gain,
    query_weight,
    key_weight,
    value_weight,
    output_weight,
    gate_weight,
    up_weight,
    down_weight,
    adam_first,
    adam_second,
):
    row_count = byte_states.shape[0]
    piece_count = lax.axis_size("dp")
    plain, sums, jobs = layer_scratch()
    vmem = pl.BlockSpec(memory_space=pltpu.VMEM)
    summed, input_grad, patch_grad = pl.pallas_call(
        layer_kernel,
        out_shape=(
            jax.ShapeDtypeStruct((FLAT, 128), F32),
            jax.ShapeDtypeStruct((128, D), BF16),
            jax.ShapeDtypeStruct((32, DG), BF16),
        ),
        in_specs=[vmem] * 3 + [pl.BlockSpec(memory_space=pl.ANY)] * 10,
        out_specs=(vmem, vmem, vmem),
        scratch_shapes=[*plain.values(), *(s for group in (*sums, *jobs) for s in group)],
        compiler_params=pltpu.CompilerParams(
            collective_id=0, has_side_effects=True, vmem_limit_bytes=63 * MIB
        ),
    )(
        patch_lengths,
        attention_gain,
        feedforward_gain,
        byte_states.reshape(4, 128, D),
        patch_states,
        cotangent.reshape(4, 128, D),
        query_weight,
        key_weight,
        value_weight,
        output_weight,
        gate_weight,
        up_weight,
        down_weight,
    )
    summed, adam_first, adam_second = lax.optimization_barrier((summed, adam_first, adam_second))
    gradient = summed * float(row_count * piece_count) ** (-0.5)
    new_first = beta_first * adam_first.reshape(FLAT, 128) + (1.0 - beta_first) * gradient
    new_second = beta_second * adam_second.reshape(FLAT, 128) + (1.0 - beta_second) * gradient * gradient
    adam_step = new_first / bias_first / (jnp.sqrt(new_second / bias_second) + adam_epsilon)
    return (
        input_grad,
        patch_grad,
        new_first.reshape(1, -1),
        new_second.reshape(1, -1),
        adam_step.reshape(1, -1),
    )


def solution(mesh):
    placed = (
        P("dp", None),
        P("dp", None),
        P("dp", None),
        P("dp", None),
        P(),
        P(),
        P(None, "heads"),
        P(None, "heads"),
        P(None, "heads"),
        P("heads", None),
        P(None, "heads"),
        P(None, "heads"),
        P("heads", None),
        P("heads", "dp"),
        P("heads", "dp"),
    )
    return jax.shard_map(
        shards,
        mesh=mesh,
        in_specs=placed,
        out_specs=(
            P(("dp", "heads"), None),
            P(("dp", "heads"), None),
            P("heads", "dp"),
            P("heads", "dp"),
            P("heads", "dp"),
        ),
        check_vma=False,
    )
```

```python
import jax
import jax.numpy as jnp
from jax import lax
from jax.experimental import pallas as pl
from jax.experimental.pallas import tpu as pltpu
from jax.sharding import PartitionSpec as P

HEAD = 128

norm_epsilon = 1e-05
adam_epsilon = 1e-08
beta_first = 0.9
beta_second = 0.95
score_scale = 0.125
bias_first = 1.0 - 0.9**20
bias_second = 1.0 - 0.95**20

BF16 = jnp.bfloat16
F32 = jnp.float32
MESH_ID = pl.DeviceIdType.MESH
MIB = 1 << 20

D = 1280
DG = 4096
UNITS = 896
UNIT_TILES = ((0, 256), (256, 512), (512, 768), (768, 896))
WIDE_TILES = tuple((n, n + 256) for n in range(0, D, 256))
FLAT = 1512
TOKEN_SCALE = 16384.0**-0.5

GU1, GU2, DN, KK, VV, QO = range(6)
PIECES = (
    (80, 640, True),
    (80, 256, False),
    (32, 1280, False),
    (128, 256, True),
    (128, 256, False),
    (160, 128, True),
)


def nn(left, right):
    return lax.dot_general(left, right, (((1,), (0,)), ((), ())), preferred_element_type=F32)


def nt(left, right):
    return lax.dot_general(left, right, (((1,), (1,)), ((), ())), preferred_element_type=F32)


def tn(left, right):
    return lax.dot_general(left, right, (((0,), (0,)), ((), ())), preferred_element_type=F32)


def inverse_rms(x):
    return lax.rsqrt(jnp.mean(x * x, axis=-1, keepdims=True) + norm_epsilon)


def norm_backward(x, inverse, scaled):
    inner = jnp.mean(scaled * x, axis=-1, keepdims=True)
    return inverse * scaled - x * (inverse * inverse * inverse) * inner


def place():
    dp = lax.axis_index("dp")
    return lax.div(dp, 8), lax.rem(lax.div(dp, 2), 4), lax.rem(dp, 2), lax.axis_index("heads")


def device_at(z, x, y, g):
    return (z * 8 + x * 2 + y, g)


def remote(src, dst, send, recv, dev):
    return pltpu.make_async_remote_copy(
        src_ref=src, dst_ref=dst, send_sem=send, recv_sem=recv, device_id=dev, device_id_type=MESH_ID
    )


def scatter_scratch(item):
    rows, cols, _ = PIECES[item]
    return [
        pltpu.VMEM((4, 4, 2, rows, cols), BF16),
        pltpu.VMEM((2, 2, 2, rows, cols), BF16),
        pltpu.VMEM((2, 4, 2, rows, cols), BF16),
        pltpu.VMEM((4, rows, cols), BF16),
        pltpu.VMEM((rows, cols), BF16),
        pltpu.VMEM((2, rows, cols), BF16),
        pltpu.SemaphoreType.DMA((13,)),
        pltpu.SemaphoreType.DMA((13,)),
    ]


class Scatter:
    def __init__(self, item, refs):
        rows, _, self.zfirst = PIECES[item]
        cut = 16 * ((rows // 16 + 1) // 2)
        self.halves = (slice(0, cut), slice(cut, rows))
        self.grad, self.near, self.got, self.pairs, self.near2, self.got2, self.send, self.recv = refs
        z, x, self.y, self.g = place()
        self.f, self.s = (z, x) if self.zfirst else (x, z)
        self.live = {}

    def at(self, f, s):
        return (f, s) if self.zfirst else (s, f)

    def mine(self, s, y):
        return (*self.at(self.f, s), y)

    def who(self, f, s, y):
        z, x = self.at(f, s)
        return device_at(z, x, y, self.g)

    def copy(self, n, src, dst, dev):
        c = remote(src, dst, self.send.at[n], self.recv.at[n], dev)
        c.start()
        self.live[n] = c

    def start1(self):
        far = lax.rem(self.f + 2, 4)
        for i, d in enumerate((1, 3)):
            dev = self.who(lax.rem(self.f + d, 4), self.s, self.y)
            self.copy(i, self.grad.at[self.at(far, pl.ds(2 * i, 2))], self.near.at[i], dev)
        for i, d in enumerate((1, 3)):
            nxt = lax.rem(self.f + d, 4)
            dev = self.who(nxt, self.s, self.y)
            rest = pl.ds(2 * (1 - i), 2)
            self.copy(2 + i, self.grad.at[self.at(nxt, rest)], self.got.at[i, rest], dev)

    def relay1(self):
        for i, d in enumerate((1, 3)):
            nxt = lax.rem(self.f + d, 4)
            dev = self.who(nxt, self.s, self.y)
            self.live[i].wait_recv()

            @pl.loop(0, 4)
            def _(k):
                a, b = lax.div(k, 2), lax.rem(k, 2)
                own = self.grad[(*self.at(nxt, 2 * i + a), b)].astype(F32)
                self.near[i, a, b] = (own + self.near[i, a, b].astype(F32)).astype(BF16)

            self.copy(4 + i, self.near.at[i], self.got.at[i, pl.ds(2 * i, 2)], dev)

    def sum_mine(self, y):
        @pl.loop(0, 4)
        def _(a):
            own = self.grad[self.mine(a, y)].astype(F32)
            total = own + self.got[0, a, y].astype(F32) + self.got[1, a, y].astype(F32)
            self.grad[self.mine(a, y)] = total.astype(BF16)

    def swap(self):
        for n in (2, 3, 4, 5):
            self.live[n].wait_recv()
        other = 1 - self.y
        self.sum_mine(other)
        self.copy(12, self.grad.at[self.mine(slice(None), other)], self.pairs, self.who(self.f, self.s, other))
        self.sum_mine(self.y)

    def start2(self):
        self.live[12].wait_recv()

        @pl.loop(0, 4)
        def _(a):
            at = self.mine(a, self.y)
            self.grad[at] = (self.grad[at].astype(F32) + self.pairs[a].astype(F32)).astype(BF16)

        for i, d in enumerate((1, 3)):
            dev = self.who(self.f, lax.rem(self.s + d, 4), self.y)
            at = self.halves[i]
            self.copy(6 + i, self.grad.at[(*self.mine(lax.rem(self.s + 2, 4), self.y), at)], self.near2.at[at], dev)
        for i, d in enumerate((1, 3)):
            nxt = lax.rem(self.s + d, 4)
            dev = self.who(self.f, nxt, self.y)
            at = self.halves[1 - i]
            self.copy(8 + i, self.grad.at[(*self.mine(nxt, self.y), at)], self.got2.at[i, at], dev)

    def relay2(self):
        for i, d in enumerate((1, 3)):
            nxt = lax.rem(self.s + d, 4)
            dev = self.who(self.f, nxt, self.y)
            at = self.halves[i]
            self.live[6 + i].wait_recv()
            own = self.grad[(*self.mine(nxt, self.y), at)].astype(F32)
            self.near2[at] = (own + self.near2[at].astype(F32)).astype(BF16)
            self.copy(10 + i, self.near2.at[at], self.got2.at[i, at], dev)

    def finish(self):
        for n in (8, 9, 10, 11):
            self.live[n].wait_recv()
        own = self.grad[self.mine(self.s, self.y)].astype(F32)
        return own + self.got2[0].astype(F32) + self.got2[1].astype(F32)

    def drain(self):
        for c in self.live.values():
            c.wait_send()


def heads_place():
    g = lax.axis_index("heads")
    y, core = lax.div(g, 2), lax.rem(g, 2)
    return g, y * 2 + 1 - core, (1 - y) * 2 + core, (1 - y) * 2 + 1 - core


def sum_scratch(rows, cols):
    return [
        pltpu.VMEM((2, rows, cols), BF16),
        pltpu.VMEM((rows, cols), BF16),
        pltpu.SemaphoreType.DMA((4,)),
        pltpu.SemaphoreType.DMA((4,)),
    ]


def pair_scratch():
    return [
        pltpu.VMEM((2, 128, D), BF16),
        pltpu.VMEM((2, 128, D), BF16),
        pltpu.SemaphoreType.DMA((6,)),
        pltpu.SemaphoreType.DMA((6,)),
    ]


class HeadsSum:
    def __init__(self, parts, rows, refs):
        self.parts, self.rows = parts, rows
        self.near, self.far, self.send, self.recv = refs
        self.live = {}
        self.dp = lax.axis_index("dp")
        self.g, self.mate, self.over, self.over_mate = heads_place()

    def send_near(self, slot):
        quarter = (self.over_mate, self.mate)[slot]
        c = remote(self.parts.at[quarter], self.near.at[slot], self.send.at[slot], self.recv.at[slot], (self.dp, self.mate))
        c.start()
        self.live[slot] = c

    def relay(self):
        self.live[0].wait_recv()
        half = self.rows // 2
        for c in range(2):

            @pl.loop(0, half // 16)
            def _(k):
                at = pl.ds(pl.multiple_of(c * half + 16 * k, 16), 16)
                total = self.near[0, at].astype(F32) + self.parts[self.over, at].astype(F32)
                self.near[0, at] = total.astype(BF16)

            at = pl.ds(c * half, half)
            copy = remote(
                self.near.at[0, at], self.far.at[at], self.send.at[2 + c], self.recv.at[2 + c], (self.dp, self.over)
            )
            copy.start()
            self.live[2 + c] = copy

    def arrive(self, c):
        if c == 0:
            self.live[1].wait_recv()
        self.live[2 + c].wait_recv()

    def total(self, *at):
        return (
            self.parts[(self.g, *at)].astype(F32) + self.near[(1, *at)].astype(F32) + self.far[at].astype(F32)
        )

    def drain(self):
        for c in self.live.values():
            c.wait_send()


class PairSum:
    def __init__(self, parts, refs):
        self.parts = parts
        self.near, self.far, self.send, self.recv = refs
        self.live = {}
        self.dp = lax.axis_index("dp")
        self.g, self.mate, self.over, _ = heads_place()
        self.core = lax.rem(self.g, 2)

    def copy(self, n, src, dst, dev):
        c = remote(src, dst, self.send.at[n], self.recv.at[n], (self.dp, dev))
        c.start()
        self.live[n] = c

    def send_near(self, b):
        self.copy(b, self.parts.at[2 * b + 1 - self.core], self.near.at[b], self.mate)

    def relay(self, b):
        self.live[b].wait_recv()
        for c in range(2):

            @pl.loop(0, 4)
            def _(k):
                at = pl.ds(pl.multiple_of(c * 64 + 16 * k, 16), 16)
                total = self.near[b, at].astype(F32) + self.parts[2 * b + self.core, at].astype(F32)
                self.near[b, at] = total.astype(BF16)

            at = pl.ds(c * 64, 64)
            self.copy(2 + 2 * b + c, self.near.at[b, at], self.far.at[b, at], self.over)

    def arrive(self, b, c):
        self.live[2 + 2 * b + c].wait_recv()

    def total(self, b, at):
        return self.near[b, at].astype(F32) + self.far[b, at].astype(F32)

    def drain(self):
        for c in self.live.values():
            c.wait_send()


class CoreSwap:
    def __init__(self, whole, send, recv):
        self.whole, self.send_sem, self.recv_sem = whole, send, recv
        self.live = {}
        self.dp = lax.axis_index("dp")
        self.g, self.mate, _, _ = heads_place()
        self.core = lax.rem(self.g, 2)

    def give(self, b, c):
        n = 2 * b + c
        ref = self.whole.at[2 * b + self.core, pl.ds(64 * c, 64)]
        copy = remote(ref, ref, self.send_sem.at[n], self.recv_sem.at[n], (self.dp, self.mate))
        copy.start()
        self.live[n] = copy

    def take(self, b):
        for c in range(2):
            self.live[2 * b + c].wait_recv()

    def drain(self):
        for c in self.live.values():
            c.wait_send()


def spread_rows(flat, start, per_row, block):
    rows, cols = block.shape
    for c in range(cols // 128):
        flat[pl.ds(start + c, rows, per_row), :] = block[:, c * 128 : (c + 1) * 128]


def place_piece(item, total, flat):
    if item == QO:
        for c in range(2):
            spread_rows(flat, c, 2, total[40 * c : 40 * c + 40])
        for c in range(10):
            spread_rows(flat, 592 + c, 10, total[80 + 8 * c : 88 + 8 * c])
    elif item == KK:
        spread_rows(flat, 80, 2, total)
    elif item == VV:
        spread_rows(flat, 336, 2, total)
    elif item == DN:
        spread_rows(flat, 1232, 10, total[0:28])
    else:
        first = 0 if item == GU1 else 5
        spread_rows(flat, 672 + first, 7, total[0:40])
        spread_rows(flat, 952 + first, 7, total[40:80])


def greet():
    z, x, y, g = place()
    dp = lax.axis_index("dp")
    _, mate, over, _ = heads_place()
    partners = [
        (dp, mate),
        (dp, over),
        device_at(lax.rem(z + 1, 4), x, y, g),
        device_at(lax.rem(z + 3, 4), x, y, g),
        device_at(z, lax.rem(x + 1, 4), y, g),
        device_at(z, lax.rem(x + 3, 4), y, g),
        device_at(z, x, 1 - y, g),
    ]
    barrier = pltpu.get_barrier_semaphore()
    for dev in partners:
        pl.semaphore_signal(barrier, inc=1, device_id=dev, device_id_type=MESH_ID)
    pl.semaphore_wait(barrier, len(partners))


def rows_at(first, k, size):
    return pl.ds(pl.multiple_of(first + size * k, size), size)


def layer_scratch():
    quarters = lambda cols, kind: pltpu.VMEM((4, 128, cols), kind)
    plain = dict(
        states=quarters(D, BF16),
        patches=pltpu.VMEM((128, DG), BF16),
        cot=quarters(D, BF16),
        wq=pltpu.VMEM((D, 256), BF16),
        wk=pltpu.VMEM((DG, 256), BF16),
        wv=pltpu.VMEM((DG, 256), BF16),
        wo=pltpu.VMEM((256, D), BF16),
        wg=pltpu.VMEM((D, UNITS), BF16),
        wu=pltpu.VMEM((D, UNITS), BF16),
        wd=pltpu.VMEM((UNITS, D), BF16),
        loads=pltpu.SemaphoreType.DMA((10,)),
        normed=quarters(D, BF16),
        query=quarters(256, F32),
        key=pltpu.VMEM((128, 256), F32),
        keyn=pltpu.VMEM((128, 256), BF16),
        value=pltpu.VMEM((128, 256), BF16),
        att=quarters(256, BF16),
        part1=quarters(D, BF16),
        part2=quarters(D, BF16),
        part4=pltpu.VMEM((4, 32, DG), BF16),
        res=pltpu.VMEM((2, 128, D), F32),
        gain1=pltpu.VMEM((1, D), F32),
        gain2=pltpu.VMEM((1, D), F32),
        nh=quarters(D, BF16),
        rh=quarters(D, BF16),
        turned=pltpu.VMEM((D, 512), BF16),
        hgrad=pltpu.VMEM((512, UNITS), F32),
        gg=pltpu.VMEM((512, UNITS), BF16),
        ug=pltpu.VMEM((512, UNITS), BF16),
        qgrad=quarters(256, BF16),
        keyg=pltpu.VMEM((128, 256), F32),
        valg=pltpu.VMEM((128, 256), F32),
        kg=pltpu.VMEM((128, 256), BF16),
        vg=pltpu.VMEM((128, 256), BF16),
        down=pltpu.VMEM((120, D), F32),
        g1s=pltpu.SemaphoreType.DMA((4,)),
        g1r=pltpu.SemaphoreType.DMA((4,)),
        g2s=pltpu.SemaphoreType.DMA((4,)),
        g2r=pltpu.SemaphoreType.DMA((4,)),
    )
    sums = [pair_scratch(), pair_scratch(), sum_scratch(128, D), sum_scratch(32, DG)]
    jobs = [scatter_scratch(i) for i in range(len(PIECES))]
    return plain, sums, jobs


class Refs:
    pass


def layer_kernel(*refs):
    (lengths, again, fgain, states_h, patches_h, cot_h, wq_h, wk_h, wv_h, wo_h, wg_h, wu_h, wd_h,
     flat, out_bytes, out_patches) = refs[:16]
    plain, sums, jobs = layer_scratch()
    rest = list(refs[16:])
    r = Refs()
    for name in plain:
        setattr(r, name, rest.pop(0))
    r.hid = r.wd.at[0:512, 0:UNITS]
    r.attt = r.wd.at[512:768, 0:512]
    sum_refs = [[rest.pop(0) for _ in s] for s in sums]
    jobs = [Scatter(i, [rest.pop(0) for _ in s]) for i, s in enumerate(jobs)]
    g, _, _, _ = heads_place()
    core = lax.rem(g, 2)

    moves = {}
    order = [
        ("patches", patches_h), ("wk", wk_h), ("wv", wv_h), ("states", states_h), ("wq", wq_h), ("wo", wo_h),
        ("cot", cot_h), ("wd", wd_h), ("wg", wg_h), ("wu", wu_h),
    ]
    for i, (name, src) in enumerate(order):
        moves[name] = pltpu.make_async_copy(src, getattr(r, name), r.loads.at[i])
    for name in ("patches", "wk", "wv", "states", "wq"):
        moves[name].start()
    r.gain1[...] = again[...].reshape(1, D)
    r.gain2[...] = fgain[...].reshape(1, D)
    greet()

    sum1 = PairSum(r.part1, sum_refs[0])
    sum2 = PairSum(r.part2, sum_refs[1])
    sum3 = HeadsSum(r.part1, 128, sum_refs[2])
    sum4 = HeadsSum(r.part4, 32, sum_refs[3])
    swap1 = CoreSwap(r.nh, r.g1s, r.g1r)
    swap2 = CoreSwap(r.rh, r.g2s, r.g2r)

    moves["patches"].wait()
    moves["wk"].wait()
    for name in ("wo", "cot", "wd", "wg", "wu"):
        moves[name].start()
    key = nn(r.patches[...], r.wk[...])
    r.key[...] = key
    for h in range(2):
        cols = slice(HEAD * h, HEAD * h + HEAD)
        one = key[:, cols]
        r.keyn[:, cols] = (one * inverse_rms(one)).astype(BF16)
    moves["wv"].wait()
    r.value[...] = nn(r.patches[...], r.wv[...]).astype(BF16)
    earlier = lax.broadcasted_iota(jnp.int32, (128, 128), 0) < lax.broadcasted_iota(jnp.int32, (128, 128), 1)
    spans = jnp.broadcast_to(lengths[...].astype(F32), (16, 128)).astype(BF16)
    starts = nn(spans, earlier.astype(F32).astype(BF16))[0:1]

    def head_probabilities(qi, h):
        cols = slice(HEAD * h, HEAD * h + HEAD)
        full = r.query[qi, :, cols]
        inverse = inverse_rms(full)
        query = (full * inverse).astype(BF16)
        scores = score_scale * nt(query, r.keyn[:, cols])
        position = (lax.broadcasted_iota(jnp.int32, (128, 128), 0) + qi * 128).astype(F32)
        weights = jnp.where(starts <= position, jnp.exp(scores), 0.0)
        return full, inverse, query, weights / jnp.sum(weights, axis=-1, keepdims=True)

    moves["states"].wait()
    moves["wq"].wait()
    moves["wo"].wait()

    def attend(qi):
        @pl.loop(0, 4)
        def _(k):
            at = rows_at(0, k, 32)
            x = r.states[qi, at].astype(F32)
            r.normed[qi, at] = (x * inverse_rms(x) * r.gain1[...]).astype(BF16)

        r.query[qi] = nn(r.normed[qi], r.wq[...])
        for h in range(2):
            cols = slice(HEAD * h, HEAD * h + HEAD)
            prob = head_probabilities(qi, h)[3]
            r.att[qi, :, cols] = nn(prob.astype(BF16), r.value[:, cols]).astype(BF16)
        for lo, hi in WIDE_TILES:
            r.part1[qi, :, lo:hi] = nn(r.att[qi], r.wo[:, lo:hi]).astype(BF16)

    for b in range(2):
        attend(2 * b + 1 - core)
        sum1.send_near(b)
        attend(2 * b + core)
        sum1.relay(b)

    moves["cot"].wait()
    moves["wd"].wait()

    @pl.loop(0, 2)
    def _(p):
        at = rows_at(0, p, 256)
        cot = r.cot[pl.ds(2 * p, 2)].reshape(256, D)
        for lo, hi in UNIT_TILES:
            r.hgrad[at, lo:hi] = nt(cot, r.wd[lo:hi, :])

    def residual(b):
        for c in range(2):
            sum1.arrive(b, c)

            @pl.loop(0, 2)
            def _(k):
                at = rows_at(64 * c, k, 32)
                res = r.states[2 * b + core, at].astype(F32) + sum1.total(b, at)
                r.res[b, at] = res
                r.nh[2 * b + core, at] = (res * inverse_rms(res) * r.gain2[...]).astype(BF16)

            swap1.give(b, c)

    def residual_back(b):
        for c in range(2):
            sum2.arrive(b, c)

            @pl.loop(0, 2)
            def _(k):
                at = rows_at(64 * c, k, 32)
                res = r.res[b, at]
                grad = norm_backward(res, inverse_rms(res), sum2.total(b, at) * r.gain2[...])
                grad = grad + r.cot[2 * b + core, at].astype(F32)
                r.res[b, at] = grad
                r.rh[2 * b + core, at] = grad.astype(BF16)

            swap2.give(b, c)

    residual(0)
    moves["wg"].wait()
    moves["wu"].wait()

    def feed(p):
        at = slice(256 * p, 256 * p + 256)
        normed = r.nh[pl.ds(2 * p, 2)].reshape(256, D)
        for lo, hi in UNIT_TILES:
            gate = nn(normed, r.wg[:, lo:hi])
            up = nn(normed, r.wu[:, lo:hi])
            back = r.hgrad[at, lo:hi]
            sigma = jax.nn.sigmoid(gate)
            active = gate * sigma
            r.hid[at, lo:hi] = (active * up).astype(BF16)
            r.gg[at, lo:hi] = (back * up * (sigma * (1.0 + gate * (1.0 - sigma)))).astype(BF16)
            r.ug[at, lo:hi] = (back * active).astype(BF16)
        for lo, hi in WIDE_TILES:
            part = nt(r.gg[at], r.wg[lo:hi, :]) + nt(r.ug[at], r.wu[lo:hi, :])
            r.part2[pl.ds(2 * p, 2), :, lo:hi] = part.astype(BF16).reshape(2, 128, hi - lo)

    def store(ref, at, rows, cols, new, again_):
        at = (*at, rows, cols)
        if again_:
            new = new + ref[at].astype(F32)
        ref[at] = new.astype(BF16)

    def turn(p):
        for q in (2 * p, 2 * p + 1):
            r.turned[:, 128 * q : 128 * q + 128] = r.nh[q].T

    def gate_up_grads(p):
        @pl.loop(0, 8)
        def _(c):
            rows = r.turned[rows_at(0, c, 160), 256 * p : 256 * p + 256]
            z, x = lax.div(c, 2), 2 * lax.rem(c, 2)
            for grad, row in ((r.gg, 0), (r.ug, 40)):
                for job, lo, hi in ((GU1, 0, 256), (GU1, 256, 512), (GU1, 512, 640), (GU2, 640, 896)):
                    got = nn(rows, grad[256 * p : 256 * p + 256, lo:hi])
                    col = lo if job == GU1 else 0
                    for j in range(4):
                        store(
                            jobs[job].grad, (z, x + j // 2, j % 2), slice(row, row + 40), slice(col, col + hi - lo),
                            got[40 * j : 40 * j + 40], p,
                        )

    def down_grads(p):
        for q in (2 * p, 2 * p + 1):
            r.turned[0:UNITS, 128 * q : 128 * q + 128] = r.hid[128 * q : 128 * q + 128].T

        @pl.loop(0, 8)
        def _(c):
            rows = r.turned[rows_at(0, c, 112), 256 * p : 256 * p + 256]
            for lo, hi in WIDE_TILES:
                r.down[0:112, lo:hi] = nn(rows, r.cot[2 * p : 2 * p + 2, :, lo:hi].reshape(256, hi - lo))
            z, x = lax.div(c, 2), 2 * lax.rem(c, 2)
            for j in range(4):
                store(
                    jobs[DN].grad, (z, x + j // 2, j % 2), slice(0, 32), slice(0, D), r.down[28 * j : 28 * j + 32], p
                )

    r.down[112:120] = jnp.zeros((8, D), F32)
    swap1.take(0)
    feed(0)
    sum2.send_near(0)
    turn(0)
    sum2.relay(0)
    gate_up_grads(0)
    residual(1)
    down_grads(0)
    swap1.take(1)
    sum1.drain()
    feed(1)
    sum2.send_near(1)
    turn(1)
    sum2.relay(1)
    gate_up_grads(1)
    jobs[GU1].start1()
    jobs[GU2].start1()
    residual_back(0)
    down_grads(1)
    jobs[DN].start1()

    r.keyg[...] = jnp.zeros((128, 256), F32)
    r.valg[...] = jnp.zeros((128, 256), F32)

    def attend_back(qi):
        agrad = nt(r.rh[qi], r.wo[...]).astype(BF16)
        for h in range(2):
            cols = slice(HEAD * h, HEAD * h + HEAD)
            full, inverse, query, prob = head_probabilities(qi, h)
            back = nt(agrad[:, cols], r.value[:, cols])
            inner = jnp.sum(prob * back, axis=-1, keepdims=True)
            score = (score_scale * prob * (back - inner)).astype(BF16)
            grad = nn(score, r.keyn[:, cols])
            r.keyg[:, cols] += tn(score, query)
            r.valg[:, cols] += tn(prob.astype(BF16), agrad[:, cols])
            r.qgrad[qi, :, cols] = norm_backward(full, inverse, grad).astype(BF16)

    attend_back(core)
    swap2.take(0)
    attend_back(1 - core)
    residual_back(1)
    jobs[GU1].relay1()
    jobs[GU2].relay1()
    attend_back(2 + core)
    swap2.take(1)
    sum2.drain()
    attend_back(3 - core)
    for h in range(2):
        cols = slice(HEAD * h, HEAD * h + HEAD)
        full = r.key[:, cols]
        r.kg[:, cols] = norm_backward(full, inverse_rms(full), r.keyg[:, cols]).astype(BF16)
    r.vg[...] = r.valg[...].astype(BF16)

    @pl.loop(0, 8)
    def _(n):
        rows = r.patches[:, rows_at(0, n, 512)].T
        z, x = lax.div(n, 2), 2 * lax.rem(n, 2)
        for job, grad in ((KK, r.kg), (VV, r.vg)):
            got = nn(rows, grad[...]).astype(BF16)
            for j in range(4):
                jobs[job].grad[z, x + j // 2, j % 2] = got[128 * j : 128 * j + 128]

    jobs[DN].relay1()
    jobs[KK].start1()
    jobs[VV].start1()
    jobs[GU2].swap()

    for q in range(4):
        r.turned[:, 128 * q : 128 * q + 128] = r.normed[q].T
        r.attt[:, 128 * q : 128 * q + 128] = r.att[q].T
    for half in range(2):
        for lo, hi in ((0, 256), (256, 512), (512, 640)):
            cols = slice(640 * half + lo, 640 * half + hi)
            r.hgrad[256 * half : 256 * half + 256, lo:hi] = nn(
                r.attt[...], r.rh[:, :, cols].reshape(512, hi - lo)
            )

    @pl.loop(0, 4)
    def _(c):
        got = nn(r.turned[rows_at(0, c, 320)], r.qgrad[...].reshape(512, 256))
        for j in range(8):
            mine = got[40 * j : 40 * j + 40]
            halves = [r.hgrad[rows_at(256 * half + 8 * j, c * 8, 8), 0:640] for half in range(2)]
            blocks = [mine[:, :128], mine[:, 128:]]
            blocks += [m[:, 128 * n : 128 * n + 128] for m in halves for n in range(5)]
            jobs[QO].grad[c, j // 2, j % 2] = jnp.concatenate(blocks, axis=0).astype(BF16)

    jobs[QO].start1()

    @pl.loop(0, 2)
    def _(p):
        grad = r.qgrad[pl.ds(2 * p, 2)].reshape(256, 256)
        for lo, hi in WIDE_TILES:
            r.part1[pl.ds(2 * p, 2), :, lo:hi] = nt(grad, r.wq[lo:hi, :]).astype(BF16).reshape(2, 128, hi - lo)

    sum3.send_near(0)
    sum3.send_near(1)

    @pl.loop(0, 16)
    def _(n):
        at = rows_at(0, n, 256)
        part = nt(r.kg[...], r.wk[at]) + nt(r.vg[...], r.wv[at])
        r.part4[:, :, at] = part.astype(BF16).reshape(4, 32, 256)

    sum4.send_near(0)
    sum4.send_near(1)
    sum3.relay()
    sum4.relay()
    jobs[GU1].swap()
    jobs[KK].relay1()
    jobs[GU2].start2()
    jobs[DN].swap()
    jobs[VV].relay1()
    jobs[GU2].relay2()
    jobs[QO].relay1()
    jobs[GU1].start2()
    jobs[DN].start2()
    jobs[GU1].relay2()

    for c in range(2):
        sum3.arrive(c)

        @pl.loop(0, 2)
        def _(k):
            at = rows_at(64 * c, k, 32)
            x = r.states[g, at].astype(F32)
            grad = r.res[lax.div(g, 2), at] + norm_backward(x, inverse_rms(x), sum3.total(at) * r.gain1[...])
            out_bytes[at] = grad.astype(BF16)

    for c in range(2):
        sum4.arrive(c)

        @pl.loop(0, 4)
        def _(k):
            at = (pl.ds(16 * c, 16), rows_at(0, k, 1024))
            out_patches[at] = sum4.total(*at).astype(BF16)

    jobs[DN].relay2()
    place_piece(GU2, jobs[GU2].finish(), flat)
    jobs[KK].swap()
    jobs[VV].swap()
    place_piece(GU1, jobs[GU1].finish(), flat)
    place_piece(DN, jobs[DN].finish(), flat)
    jobs[KK].start2()
    jobs[QO].swap()
    jobs[VV].start2()
    for n in (KK, VV):
        jobs[n].relay2()
    jobs[QO].start2()
    jobs[QO].relay2()
    for n in (KK, VV, QO):
        place_piece(n, jobs[n].finish(), flat)
    for item in (*jobs, sum3, sum4, swap1, swap2):
        item.drain()


def adam_kernel(summed, first, second, bytes_in, patches_in, new_first, new_second, step, bytes_out, patches_out):
    @pl.when(pl.program_id(0) == 0)
    def _():
        bytes_out[...] = bytes_in[...]
        patches_out[...] = patches_in[...]

    gradient = summed[...] * TOKEN_SCALE
    moment = beta_first * first[...] + (1.0 - beta_first) * gradient
    spread = beta_second * second[...] + (1.0 - beta_second) * gradient * gradient
    new_first[...] = moment
    new_second[...] = spread
    step[...] = moment / bias_first / (jnp.sqrt(spread / bias_second) + adam_epsilon)


def adam(summed, first, second, input_grad, patch_grad):
    flat = pl.BlockSpec((216, 128), lambda i: (i, 0))
    whole = [pl.BlockSpec(m.shape, lambda i: (0, 0)) for m in (input_grad, patch_grad)]
    return pl.pallas_call(
        adam_kernel,
        grid=(7,),
        out_shape=[jax.ShapeDtypeStruct((FLAT, 128), F32)] * 3
        + [jax.ShapeDtypeStruct(m.shape, m.dtype) for m in (input_grad, patch_grad)],
        in_specs=[flat] * 3 + whole,
        out_specs=[flat] * 3 + whole,
        compiler_params=pltpu.CompilerParams(vmem_limit_bytes=60 * MIB),
    )(summed, first, second, input_grad, patch_grad)


def shards(
    byte_states,
    patch_states,
    patch_lengths,
    cotangent,
    attention_gain,
    feedforward_gain,
    query_weight,
    key_weight,
    value_weight,
    output_weight,
    gate_weight,
    up_weight,
    down_weight,
    adam_first,
    adam_second,
):
    plain, sums, jobs = layer_scratch()
    vmem = pl.BlockSpec(memory_space=pltpu.VMEM)
    summed, input_grad, patch_grad = pl.pallas_call(
        layer_kernel,
        out_shape=(
            jax.ShapeDtypeStruct((FLAT, 128), F32),
            jax.ShapeDtypeStruct((128, D), BF16),
            jax.ShapeDtypeStruct((32, DG), BF16),
        ),
        in_specs=[vmem] * 3 + [pl.BlockSpec(memory_space=pl.ANY)] * 10,
        out_specs=(vmem, vmem, vmem),
        scratch_shapes=[*plain.values(), *(s for group in (*sums, *jobs) for s in group)],
        compiler_params=pltpu.CompilerParams(
            collective_id=0, has_side_effects=True, vmem_limit_bytes=63 * MIB
        ),
    )(
        patch_lengths,
        attention_gain,
        feedforward_gain,
        byte_states.reshape(4, 128, D),
        patch_states,
        cotangent.reshape(4, 128, D),
        query_weight,
        key_weight,
        value_weight,
        output_weight,
        gate_weight,
        up_weight,
        down_weight,
    )
    new_first, new_second, adam_step, input_grad, patch_grad = adam(
        summed, adam_first.reshape(FLAT, 128), adam_second.reshape(FLAT, 128), input_grad, patch_grad
    )
    return (
        input_grad,
        patch_grad,
        new_first.reshape(1, -1),
        new_second.reshape(1, -1),
        adam_step.reshape(1, -1),
    )


def solution(mesh):
    placed = (
        P("dp", None),
        P("dp", None),
        P("dp", None),
        P("dp", None),
        P(),
        P(),
        P(None, "heads"),
        P(None, "heads"),
        P(None, "heads"),
        P("heads", None),
        P(None, "heads"),
        P(None, "heads"),
        P("heads", None),
        P("heads", "dp"),
        P("heads", "dp"),
    )
    return jax.shard_map(
        shards,
        mesh=mesh,
        in_specs=placed,
        out_specs=(
            P(("dp", "heads"), None),
            P(("dp", "heads"), None),
            P("heads", "dp"),
            P("heads", "dp"),
            P("heads", "dp"),
        ),
        check_vma=False,
    )
```

```python
import jax
import jax.numpy as jnp
from jax import lax
from jax.experimental import pallas as pl
from jax.experimental.pallas import tpu as pltpu
from jax.sharding import PartitionSpec as P

HEAD = 128

norm_epsilon = 1e-05
adam_epsilon = 1e-08
beta_first = 0.9
beta_second = 0.95
score_scale = 0.125
bias_first = 1.0 - 0.9**20
bias_second = 1.0 - 0.95**20

BF16 = jnp.bfloat16
F32 = jnp.float32
MESH_ID = pl.DeviceIdType.MESH
MIB = 1 << 20

D = 1280
DG = 4096
UNITS = 896
UNIT_TILES = ((0, 256), (256, 512), (512, 768), (768, 896))
WIDE_TILES = tuple((n, n + 256) for n in range(0, D, 256))
FLAT = 1512
TOKEN_SCALE = 16384.0**-0.5

GU1, GU2, DN, KK, VV, QO = range(6)
PIECES = (
    (80, 640, True),
    (80, 256, False),
    (32, 1280, False),
    (128, 256, True),
    (128, 256, False),
    (160, 128, True),
)
LATE = (KK, VV, QO)


def nn(left, right):
    return lax.dot_general(left, right, (((1,), (0,)), ((), ())), preferred_element_type=F32)


def nt(left, right):
    return lax.dot_general(left, right, (((1,), (1,)), ((), ())), preferred_element_type=F32)


def tn(left, right):
    return lax.dot_general(left, right, (((0,), (0,)), ((), ())), preferred_element_type=F32)


def inverse_rms(x):
    return lax.rsqrt(jnp.mean(x * x, axis=-1, keepdims=True) + norm_epsilon)


def norm_backward(x, inverse, scaled):
    inner = jnp.mean(scaled * x, axis=-1, keepdims=True)
    return inverse * scaled - x * (inverse * inverse * inverse) * inner


def place():
    dp = lax.axis_index("dp")
    return lax.div(dp, 8), lax.rem(lax.div(dp, 2), 4), lax.rem(dp, 2), lax.axis_index("heads")


def device_at(z, x, y, g):
    return (z * 8 + x * 2 + y, g)


def remote(src, dst, send, recv, dev):
    return pltpu.make_async_remote_copy(
        src_ref=src, dst_ref=dst, send_sem=send, recv_sem=recv, device_id=dev, device_id_type=MESH_ID
    )


def scatter_scratch(item):
    rows, cols, _ = PIECES[item]
    shapes = ((2,), (2, 2), ()) if item in LATE else ((4,), (), (2,))
    ends = [pltpu.VMEM((*m, rows, cols), BF16) for m in shapes]
    return [
        pltpu.VMEM((4, 4, 2, rows, cols), BF16),
        pltpu.VMEM((2, 2, 2, rows, cols), BF16),
        pltpu.VMEM((2, 4, 2, rows, cols), BF16),
        *ends,
        pltpu.SemaphoreType.DMA((13,)),
        pltpu.SemaphoreType.DMA((13,)),
    ]


class Scatter:
    def __init__(self, item, refs):
        rows, _, self.zfirst = PIECES[item]
        cut = 16 * ((rows // 16 + 1) // 2)
        self.halves = (slice(0, cut), slice(cut, rows))
        self.unpack(refs)
        z, x, self.y, self.g = place()
        self.f, self.s = (z, x) if self.zfirst else (x, z)
        self.live = {}

    def unpack(self, refs):
        self.grad, self.near, self.got, self.pairs, self.near2, self.got2, self.send, self.recv = refs

    def at(self, f, s):
        return (f, s) if self.zfirst else (s, f)

    def mine(self, s, y):
        return (*self.at(self.f, s), y)

    def who(self, f, s, y):
        z, x = self.at(f, s)
        return device_at(z, x, y, self.g)

    def copy(self, n, src, dst, dev):
        c = remote(src, dst, self.send.at[n], self.recv.at[n], dev)
        c.start()
        self.live[n] = c

    def start1(self):
        far = lax.rem(self.f + 2, 4)
        for i, d in enumerate((1, 3)):
            dev = self.who(lax.rem(self.f + d, 4), self.s, self.y)
            self.copy(i, self.grad.at[self.at(far, pl.ds(2 * i, 2))], self.near.at[i], dev)
        for i, d in enumerate((1, 3)):
            nxt = lax.rem(self.f + d, 4)
            dev = self.who(nxt, self.s, self.y)
            rest = pl.ds(2 * (1 - i), 2)
            self.copy(2 + i, self.grad.at[self.at(nxt, rest)], self.got.at[i, rest], dev)

    def relay1(self):
        for i, d in enumerate((1, 3)):
            nxt = lax.rem(self.f + d, 4)
            dev = self.who(nxt, self.s, self.y)
            self.live[i].wait_recv()

            @pl.loop(0, 4)
            def _(k):
                a, b = lax.div(k, 2), lax.rem(k, 2)
                own = self.grad[(*self.at(nxt, 2 * i + a), b)].astype(F32)
                self.near[i, a, b] = (own + self.near[i, a, b].astype(F32)).astype(BF16)

            self.copy(4 + i, self.near.at[i], self.got.at[i, pl.ds(2 * i, 2)], dev)

    def sum_mine(self, y):
        @pl.loop(0, 4)
        def _(a):
            own = self.grad[self.mine(a, y)].astype(F32)
            total = own + self.got[0, a, y].astype(F32) + self.got[1, a, y].astype(F32)
            self.grad[self.mine(a, y)] = total.astype(BF16)

    def swap(self):
        for n in (2, 3, 4, 5):
            self.live[n].wait_recv()
        other = 1 - self.y
        self.sum_mine(other)
        self.copy(12, self.grad.at[self.mine(slice(None), other)], self.pairs, self.who(self.f, self.s, other))
        self.sum_mine(self.y)

    def start2(self):
        self.live[12].wait_recv()

        @pl.loop(0, 4)
        def _(a):
            at = self.mine(a, self.y)
            self.grad[at] = (self.grad[at].astype(F32) + self.pairs[a].astype(F32)).astype(BF16)

        for i, d in enumerate((1, 3)):
            dev = self.who(self.f, lax.rem(self.s + d, 4), self.y)
            at = self.halves[i]
            self.copy(6 + i, self.grad.at[(*self.mine(lax.rem(self.s + 2, 4), self.y), at)], self.near2.at[at], dev)
        for i, d in enumerate((1, 3)):
            nxt = lax.rem(self.s + d, 4)
            dev = self.who(self.f, nxt, self.y)
            at = self.halves[1 - i]
            self.copy(8 + i, self.grad.at[(*self.mine(nxt, self.y), at)], self.got2.at[i, at], dev)

    def relay2(self):
        for i, d in enumerate((1, 3)):
            nxt = lax.rem(self.s + d, 4)
            dev = self.who(self.f, nxt, self.y)
            at = self.halves[i]
            self.live[6 + i].wait_recv()
            own = self.grad[(*self.mine(nxt, self.y), at)].astype(F32)
            self.near2[at] = (own + self.near2[at].astype(F32)).astype(BF16)
            self.copy(10 + i, self.near2.at[at], self.got2.at[i, at], dev)

    def finish(self):
        for n in (8, 9, 10, 11):
            self.live[n].wait_recv()
        own = self.grad[self.mine(self.s, self.y)].astype(F32)
        return own + self.got2[0].astype(F32) + self.got2[1].astype(F32)

    def drain(self):
        for c in self.live.values():
            c.wait_send()


class ScatterLate(Scatter):
    def unpack(self, refs):
        self.grad, self.near, self.got, self.near2, self.got2, self.last, self.send, self.recv = refs

    def start2(self):
        for n in (2, 3, 4, 5):
            self.live[n].wait_recv()

        @pl.loop(0, 8)
        def _(k):
            a, b = lax.div(k, 2), lax.rem(k, 2)
            own = self.grad[self.mine(a, b)].astype(F32)
            total = own + self.got[0, a, b].astype(F32) + self.got[1, a, b].astype(F32)
            self.grad[self.mine(a, b)] = total.astype(BF16)

        for i, d in enumerate((1, 3)):
            dev = self.who(self.f, lax.rem(self.s + d, 4), self.y)
            self.copy(6 + i, self.grad.at[self.mine(lax.rem(self.s + 2, 4), i)], self.near2.at[i], dev)
        for i, d in enumerate((1, 3)):
            nxt = lax.rem(self.s + d, 4)
            dev = self.who(self.f, nxt, self.y)
            self.copy(8 + i, self.grad.at[self.mine(nxt, 1 - i)], self.got2.at[i, 1 - i], dev)

    def relay2(self):
        for i, d in enumerate((1, 3)):
            nxt = lax.rem(self.s + d, 4)
            dev = self.who(self.f, nxt, self.y)
            self.live[6 + i].wait_recv()
            own = self.grad[self.mine(nxt, i)].astype(F32)
            self.near2[i] = (own + self.near2[i].astype(F32)).astype(BF16)
            self.copy(10 + i, self.near2.at[i], self.got2.at[i, i], dev)

    def start3(self):
        for n in (8, 9, 10, 11):
            self.live[n].wait_recv()
        for b in range(2):
            own = self.grad[self.mine(self.s, b)].astype(F32)
            total = own + self.got2[0, b].astype(F32) + self.got2[1, b].astype(F32)
            self.grad[self.mine(self.s, b)] = total.astype(BF16)
        other = 1 - self.y
        self.copy(12, self.grad.at[self.mine(self.s, other)], self.last, self.who(self.f, self.s, other))

    def finish(self):
        self.live[12].wait_recv()
        return self.grad[self.mine(self.s, self.y)].astype(F32) + self.last[...].astype(F32)


def heads_place():
    g = lax.axis_index("heads")
    y, core = lax.div(g, 2), lax.rem(g, 2)
    return g, y * 2 + 1 - core, (1 - y) * 2 + core, (1 - y) * 2 + 1 - core


def sum_scratch(rows, cols):
    return [
        pltpu.VMEM((2, rows, cols), BF16),
        pltpu.VMEM((rows, cols), BF16),
        pltpu.SemaphoreType.DMA((4,)),
        pltpu.SemaphoreType.DMA((4,)),
    ]


def pair_scratch():
    return [
        pltpu.VMEM((2, 128, D), BF16),
        pltpu.VMEM((2, 128, D), BF16),
        pltpu.SemaphoreType.DMA((6,)),
        pltpu.SemaphoreType.DMA((6,)),
    ]


class HeadsSum:
    def __init__(self, parts, rows, refs):
        self.parts, self.rows = parts, rows
        self.near, self.far, self.send, self.recv = refs
        self.live = {}
        self.dp = lax.axis_index("dp")
        self.g, self.mate, self.over, self.over_mate = heads_place()

    def send_near(self, slot):
        quarter = (self.over_mate, self.mate)[slot]
        c = remote(self.parts.at[quarter], self.near.at[slot], self.send.at[slot], self.recv.at[slot], (self.dp, self.mate))
        c.start()
        self.live[slot] = c

    def relay(self):
        self.live[0].wait_recv()
        half = self.rows // 2
        for c in range(2):

            @pl.loop(0, half // 16)
            def _(k):
                at = pl.ds(pl.multiple_of(c * half + 16 * k, 16), 16)
                total = self.near[0, at].astype(F32) + self.parts[self.over, at].astype(F32)
                self.near[0, at] = total.astype(BF16)

            at = pl.ds(c * half, half)
            copy = remote(
                self.near.at[0, at], self.far.at[at], self.send.at[2 + c], self.recv.at[2 + c], (self.dp, self.over)
            )
            copy.start()
            self.live[2 + c] = copy

    def arrive(self, c):
        if c == 0:
            self.live[1].wait_recv()
        self.live[2 + c].wait_recv()

    def total(self, *at):
        return (
            self.parts[(self.g, *at)].astype(F32) + self.near[(1, *at)].astype(F32) + self.far[at].astype(F32)
        )

    def drain(self):
        for c in self.live.values():
            c.wait_send()


class PairSum:
    def __init__(self, parts, refs):
        self.parts = parts
        self.near, self.far, self.send, self.recv = refs
        self.live = {}
        self.dp = lax.axis_index("dp")
        self.g, self.mate, self.over, _ = heads_place()
        self.core = lax.rem(self.g, 2)

    def copy(self, n, src, dst, dev):
        c = remote(src, dst, self.send.at[n], self.recv.at[n], (self.dp, dev))
        c.start()
        self.live[n] = c

    def send_near(self, b):
        self.copy(b, self.parts.at[2 * b + 1 - self.core], self.near.at[b], self.mate)

    def relay(self, b):
        self.live[b].wait_recv()
        for c in range(2):

            @pl.loop(0, 4)
            def _(k):
                at = pl.ds(pl.multiple_of(c * 64 + 16 * k, 16), 16)
                total = self.near[b, at].astype(F32) + self.parts[2 * b + self.core, at].astype(F32)
                self.near[b, at] = total.astype(BF16)

            at = pl.ds(c * 64, 64)
            self.copy(2 + 2 * b + c, self.near.at[b, at], self.far.at[b, at], self.over)

    def arrive(self, b, c):
        self.live[2 + 2 * b + c].wait_recv()

    def total(self, b, at):
        return self.near[b, at].astype(F32) + self.far[b, at].astype(F32)

    def drain(self):
        for c in self.live.values():
            c.wait_send()


class CoreSwap:
    def __init__(self, whole, send, recv):
        self.whole, self.send_sem, self.recv_sem = whole, send, recv
        self.live = {}
        self.dp = lax.axis_index("dp")
        self.g, self.mate, _, _ = heads_place()
        self.core = lax.rem(self.g, 2)

    def give(self, b, c):
        n = 2 * b + c
        ref = self.whole.at[2 * b + self.core, pl.ds(64 * c, 64)]
        copy = remote(ref, ref, self.send_sem.at[n], self.recv_sem.at[n], (self.dp, self.mate))
        copy.start()
        self.live[n] = copy

    def take(self, b):
        for c in range(2):
            self.live[2 * b + c].wait_recv()

    def drain(self):
        for c in self.live.values():
            c.wait_send()


def spread_rows(flat, start, per_row, block):
    rows, cols = block.shape
    for c in range(cols // 128):
        flat[pl.ds(start + c, rows, per_row), :] = block[:, c * 128 : (c + 1) * 128]


def place_piece(item, total, flat):
    if item == QO:
        for c in range(2):
            spread_rows(flat, c, 2, total[40 * c : 40 * c + 40])
        for c in range(10):
            spread_rows(flat, 592 + c, 10, total[80 + 8 * c : 88 + 8 * c])
    elif item == KK:
        spread_rows(flat, 80, 2, total)
    elif item == VV:
        spread_rows(flat, 336, 2, total)
    elif item == DN:
        spread_rows(flat, 1232, 10, total[0:28])
    else:
        first = 0 if item == GU1 else 5
        spread_rows(flat, 672 + first, 7, total[0:40])
        spread_rows(flat, 952 + first, 7, total[40:80])


def greet():
    z, x, y, g = place()
    dp = lax.axis_index("dp")
    _, mate, over, _ = heads_place()
    partners = [
        (dp, mate),
        (dp, over),
        device_at(lax.rem(z + 1, 4), x, y, g),
        device_at(lax.rem(z + 3, 4), x, y, g),
        device_at(z, lax.rem(x + 1, 4), y, g),
        device_at(z, lax.rem(x + 3, 4), y, g),
        device_at(z, x, 1 - y, g),
    ]
    barrier = pltpu.get_barrier_semaphore()
    for dev in partners:
        pl.semaphore_signal(barrier, inc=1, device_id=dev, device_id_type=MESH_ID)
    pl.semaphore_wait(barrier, len(partners))


def rows_at(first, k, size):
    return pl.ds(pl.multiple_of(first + size * k, size), size)


def layer_scratch():
    quarters = lambda cols, kind: pltpu.VMEM((4, 128, cols), kind)
    plain = dict(
        states=quarters(D, BF16),
        patches=pltpu.VMEM((128, DG), BF16),
        cot=quarters(D, BF16),
        wq=pltpu.VMEM((D, 256), BF16),
        wk=pltpu.VMEM((DG, 256), BF16),
        wv=pltpu.VMEM((DG, 256), BF16),
        wo=pltpu.VMEM((256, D), BF16),
        wg=pltpu.VMEM((D, UNITS), BF16),
        wu=pltpu.VMEM((D, UNITS), BF16),
        wd=pltpu.VMEM((UNITS, D), BF16),
        loads=pltpu.SemaphoreType.DMA((10,)),
        normed=quarters(D, BF16),
        query=quarters(256, F32),
        key=pltpu.VMEM((128, 256), F32),
        keyn=pltpu.VMEM((128, 256), BF16),
        value=pltpu.VMEM((128, 256), BF16),
        att=quarters(256, BF16),
        part1=quarters(D, BF16),
        part2=quarters(D, BF16),
        part4=pltpu.VMEM((4, 32, DG), BF16),
        res=pltpu.VMEM((2, 128, D), F32),
        gain1=pltpu.VMEM((1, D), F32),
        gain2=pltpu.VMEM((1, D), F32),
        nh=quarters(D, BF16),
        rh=quarters(D, BF16),
        turned=pltpu.VMEM((D, 512), BF16),
        hgrad=pltpu.VMEM((512, UNITS), F32),
        gg=pltpu.VMEM((512, UNITS), BF16),
        ug=pltpu.VMEM((512, UNITS), BF16),
        qgrad=quarters(256, BF16),
        keyg=pltpu.VMEM((128, 256), F32),
        valg=pltpu.VMEM((128, 256), F32),
        kg=pltpu.VMEM((128, 256), BF16),
        vg=pltpu.VMEM((128, 256), BF16),
        down=pltpu.VMEM((120, D), F32),
        g1s=pltpu.SemaphoreType.DMA((4,)),
        g1r=pltpu.SemaphoreType.DMA((4,)),
        g2s=pltpu.SemaphoreType.DMA((4,)),
        g2r=pltpu.SemaphoreType.DMA((4,)),
    )
    sums = [pair_scratch(), pair_scratch(), sum_scratch(128, D), sum_scratch(32, DG)]
    jobs = [scatter_scratch(i) for i in range(len(PIECES))]
    return plain, sums, jobs


class Refs:
    pass


def layer_kernel(*refs):
    (lengths, again, fgain, states_h, patches_h, cot_h, wq_h, wk_h, wv_h, wo_h, wg_h, wu_h, wd_h,
     flat, out_bytes, out_patches) = refs[:16]
    plain, sums, jobs = layer_scratch()
    rest = list(refs[16:])
    r = Refs()
    for name in plain:
        setattr(r, name, rest.pop(0))
    r.hid = r.wd.at[0:512, 0:UNITS]
    r.attt = r.wd.at[512:768, 0:512]
    sum_refs = [[rest.pop(0) for _ in s] for s in sums]
    jobs = [(ScatterLate if i in LATE else Scatter)(i, [rest.pop(0) for _ in s]) for i, s in enumerate(jobs)]
    g, _, _, _ = heads_place()
    core = lax.rem(g, 2)

    moves = {}
    order = [
        ("patches", patches_h), ("wk", wk_h), ("wv", wv_h), ("states", states_h), ("wq", wq_h), ("wo", wo_h),
        ("cot", cot_h), ("wd", wd_h), ("wg", wg_h), ("wu", wu_h),
    ]
    for i, (name, src) in enumerate(order):
        moves[name] = pltpu.make_async_copy(src, getattr(r, name), r.loads.at[i])
    for name in ("patches", "wk", "wv", "states", "wq"):
        moves[name].start()
    r.gain1[...] = again[...].reshape(1, D)
    r.gain2[...] = fgain[...].reshape(1, D)
    greet()

    sum1 = PairSum(r.part1, sum_refs[0])
    sum2 = PairSum(r.part2, sum_refs[1])
    sum3 = HeadsSum(r.part1, 128, sum_refs[2])
    sum4 = HeadsSum(r.part4, 32, sum_refs[3])
    swap1 = CoreSwap(r.nh, r.g1s, r.g1r)
    swap2 = CoreSwap(r.rh, r.g2s, r.g2r)

    moves["patches"].wait()
    moves["wk"].wait()
    for name in ("wo", "cot", "wd", "wg", "wu"):
        moves[name].start()
    key = nn(r.patches[...], r.wk[...])
    r.key[...] = key
    for h in range(2):
        cols = slice(HEAD * h, HEAD * h + HEAD)
        one = key[:, cols]
        r.keyn[:, cols] = (one * inverse_rms(one)).astype(BF16)
    moves["wv"].wait()
    r.value[...] = nn(r.patches[...], r.wv[...]).astype(BF16)
    earlier = lax.broadcasted_iota(jnp.int32, (128, 128), 0) < lax.broadcasted_iota(jnp.int32, (128, 128), 1)
    spans = jnp.broadcast_to(lengths[...].astype(F32), (16, 128)).astype(BF16)
    starts = nn(spans, earlier.astype(F32).astype(BF16))[0:1]

    def head_probabilities(qi, h):
        cols = slice(HEAD * h, HEAD * h + HEAD)
        full = r.query[qi, :, cols]
        inverse = inverse_rms(full)
        query = (full * inverse).astype(BF16)
        scores = score_scale * nt(query, r.keyn[:, cols])
        position = (lax.broadcasted_iota(jnp.int32, (128, 128), 0) + qi * 128).astype(F32)
        weights = jnp.where(starts <= position, jnp.exp(scores), 0.0)
        return full, inverse, query, weights / jnp.sum(weights, axis=-1, keepdims=True)

    moves["states"].wait()
    moves["wq"].wait()
    moves["wo"].wait()

    def attend(qi):
        @pl.loop(0, 4)
        def _(k):
            at = rows_at(0, k, 32)
            x = r.states[qi, at].astype(F32)
            r.normed[qi, at] = (x * inverse_rms(x) * r.gain1[...]).astype(BF16)

        r.query[qi] = nn(r.normed[qi], r.wq[...])
        for h in range(2):
            cols = slice(HEAD * h, HEAD * h + HEAD)
            prob = head_probabilities(qi, h)[3]
            r.att[qi, :, cols] = nn(prob.astype(BF16), r.value[:, cols]).astype(BF16)
        for lo, hi in WIDE_TILES:
            r.part1[qi, :, lo:hi] = nn(r.att[qi], r.wo[:, lo:hi]).astype(BF16)

    for b in range(2):
        attend(2 * b + 1 - core)
        sum1.send_near(b)
        attend(2 * b + core)
        sum1.relay(b)

    moves["cot"].wait()
    moves["wd"].wait()

    @pl.loop(0, 2)
    def _(p):
        at = rows_at(0, p, 256)
        cot = r.cot[pl.ds(2 * p, 2)].reshape(256, D)
        for lo, hi in UNIT_TILES:
            r.hgrad[at, lo:hi] = nt(cot, r.wd[lo:hi, :])

    def residual(b):
        for c in range(2):
            sum1.arrive(b, c)

            @pl.loop(0, 2)
            def _(k):
                at = rows_at(64 * c, k, 32)
                res = r.states[2 * b + core, at].astype(F32) + sum1.total(b, at)
                r.res[b, at] = res
                r.nh[2 * b + core, at] = (res * inverse_rms(res) * r.gain2[...]).astype(BF16)

            swap1.give(b, c)

    def residual_back(b):
        for c in range(2):
            sum2.arrive(b, c)

            @pl.loop(0, 2)
            def _(k):
                at = rows_at(64 * c, k, 32)
                res = r.res[b, at]
                grad = norm_backward(res, inverse_rms(res), sum2.total(b, at) * r.gain2[...])
                grad = grad + r.cot[2 * b + core, at].astype(F32)
                r.res[b, at] = grad
                r.rh[2 * b + core, at] = grad.astype(BF16)

            swap2.give(b, c)

    residual(0)
    moves["wg"].wait()
    moves["wu"].wait()

    def feed(p):
        at = slice(256 * p, 256 * p + 256)
        normed = r.nh[pl.ds(2 * p, 2)].reshape(256, D)
        for lo, hi in UNIT_TILES:
            gate = nn(normed, r.wg[:, lo:hi])
            up = nn(normed, r.wu[:, lo:hi])
            back = r.hgrad[at, lo:hi]
            sigma = jax.nn.sigmoid(gate)
            active = gate * sigma
            r.hid[at, lo:hi] = (active * up).astype(BF16)
            r.gg[at, lo:hi] = (back * up * (sigma * (1.0 + gate * (1.0 - sigma)))).astype(BF16)
            r.ug[at, lo:hi] = (back * active).astype(BF16)
        for lo, hi in WIDE_TILES:
            part = nt(r.gg[at], r.wg[lo:hi, :]) + nt(r.ug[at], r.wu[lo:hi, :])
            r.part2[pl.ds(2 * p, 2), :, lo:hi] = part.astype(BF16).reshape(2, 128, hi - lo)

    def store(ref, at, rows, cols, new, again_):
        at = (*at, rows, cols)
        if again_:
            new = new + ref[at].astype(F32)
        ref[at] = new.astype(BF16)

    def turn(p):
        for q in (2 * p, 2 * p + 1):
            r.turned[:, 128 * q : 128 * q + 128] = r.nh[q].T

    def gate_up_grads(p):
        @pl.loop(0, 8)
        def _(c):
            rows = r.turned[rows_at(0, c, 160), 256 * p : 256 * p + 256]
            z, x = lax.div(c, 2), 2 * lax.rem(c, 2)
            for grad, row in ((r.gg, 0), (r.ug, 40)):
                for job, lo, hi in ((GU1, 0, 256), (GU1, 256, 512), (GU1, 512, 640), (GU2, 640, 896)):
                    got = nn(rows, grad[256 * p : 256 * p + 256, lo:hi])
                    col = lo if job == GU1 else 0
                    for j in range(4):
                        store(
                            jobs[job].grad, (z, x + j // 2, j % 2), slice(row, row + 40), slice(col, col + hi - lo),
                            got[40 * j : 40 * j + 40], p,
                        )

    def down_grads(p):
        for q in (2 * p, 2 * p + 1):
            r.turned[0:UNITS, 128 * q : 128 * q + 128] = r.hid[128 * q : 128 * q + 128].T

        @pl.loop(0, 8)
        def _(c):
            rows = r.turned[rows_at(0, c, 112), 256 * p : 256 * p + 256]
            for lo, hi in WIDE_TILES:
                r.down[0:112, lo:hi] = nn(rows, r.cot[2 * p : 2 * p + 2, :, lo:hi].reshape(256, hi - lo))
            z, x = lax.div(c, 2), 2 * lax.rem(c, 2)
            for j in range(4):
                store(
                    jobs[DN].grad, (z, x + j // 2, j % 2), slice(0, 32), slice(0, D), r.down[28 * j : 28 * j + 32], p
                )

    r.down[112:120] = jnp.zeros((8, D), F32)
    swap1.take(0)
    feed(0)
    sum2.send_near(0)
    turn(0)
    sum2.relay(0)
    gate_up_grads(0)
    residual(1)
    down_grads(0)
    swap1.take(1)
    sum1.drain()
    feed(1)
    sum2.send_near(1)
    turn(1)
    sum2.relay(1)
    gate_up_grads(1)
    jobs[GU1].start1()
    jobs[GU2].start1()
    residual_back(0)
    down_grads(1)
    jobs[GU2].relay1()
    jobs[DN].start1()

    r.keyg[...] = jnp.zeros((128, 256), F32)
    r.valg[...] = jnp.zeros((128, 256), F32)

    def attend_back(qi):
        agrad = nt(r.rh[qi], r.wo[...]).astype(BF16)
        for h in range(2):
            cols = slice(HEAD * h, HEAD * h + HEAD)
            full, inverse, query, prob = head_probabilities(qi, h)
            back = nt(agrad[:, cols], r.value[:, cols])
            inner = jnp.sum(prob * back, axis=-1, keepdims=True)
            score = (score_scale * prob * (back - inner)).astype(BF16)
            grad = nn(score, r.keyn[:, cols])
            r.keyg[:, cols] += tn(score, query)
            r.valg[:, cols] += tn(prob.astype(BF16), agrad[:, cols])
            r.qgrad[qi, :, cols] = norm_backward(full, inverse, grad).astype(BF16)

    attend_back(core)
    swap2.take(0)
    attend_back(1 - core)
    residual_back(1)
    attend_back(2 + core)
    swap2.take(1)
    sum2.drain()
    attend_back(3 - core)
    for h in range(2):
        cols = slice(HEAD * h, HEAD * h + HEAD)
        full = r.key[:, cols]
        r.kg[:, cols] = norm_backward(full, inverse_rms(full), r.keyg[:, cols]).astype(BF16)
    r.vg[...] = r.valg[...].astype(BF16)

    jobs[GU1].relay1()

    @pl.loop(0, 8)
    def _(n):
        rows = r.patches[:, rows_at(0, n, 512)].T
        z, x = lax.div(n, 2), 2 * lax.rem(n, 2)
        for job, grad in ((KK, r.kg), (VV, r.vg)):
            got = nn(rows, grad[...]).astype(BF16)
            for j in range(4):
                jobs[job].grad[z, x + j // 2, j % 2] = got[128 * j : 128 * j + 128]

    jobs[VV].start1()
    jobs[KK].start1()

    for q in range(4):
        r.turned[:, 128 * q : 128 * q + 128] = r.normed[q].T
        r.attt[:, 128 * q : 128 * q + 128] = r.att[q].T
    for half in range(2):
        for lo, hi in ((0, 256), (256, 512), (512, 640)):
            cols = slice(640 * half + lo, 640 * half + hi)
            r.hgrad[256 * half : 256 * half + 256, lo:hi] = nn(
                r.attt[...], r.rh[:, :, cols].reshape(512, hi - lo)
            )

    @pl.loop(0, 4)
    def _(c):
        got = nn(r.turned[rows_at(0, c, 320)], r.qgrad[...].reshape(512, 256))
        for j in range(8):
            mine = got[40 * j : 40 * j + 40]
            halves = [r.hgrad[rows_at(256 * half + 8 * j, c * 8, 8), 0:640] for half in range(2)]
            blocks = [mine[:, :128], mine[:, 128:]]
            blocks += [m[:, 128 * n : 128 * n + 128] for m in halves for n in range(5)]
            jobs[QO].grad[c, j // 2, j % 2] = jnp.concatenate(blocks, axis=0).astype(BF16)


    @pl.loop(0, 2)
    def _(p):
        grad = r.qgrad[pl.ds(2 * p, 2)].reshape(256, 256)
        for lo, hi in WIDE_TILES:
            r.part1[pl.ds(2 * p, 2), :, lo:hi] = nt(grad, r.wq[lo:hi, :]).astype(BF16).reshape(2, 128, hi - lo)

    sum3.send_near(0)
    sum3.send_near(1)

    @pl.loop(0, 16)
    def _(n):
        at = rows_at(0, n, 256)
        part = nt(r.kg[...], r.wk[at]) + nt(r.vg[...], r.wv[at])
        r.part4[:, :, at] = part.astype(BF16).reshape(4, 32, 256)

    sum4.send_near(0)
    sum4.send_near(1)
    sum3.relay()
    jobs[GU1].swap()
    jobs[GU2].swap()
    sum4.relay()
    jobs[DN].relay1()
    jobs[KK].relay1()
    jobs[VV].relay1()

    for c in range(2):
        sum3.arrive(c)

        @pl.loop(0, 2)
        def _(k):
            at = rows_at(64 * c, k, 32)
            x = r.states[g, at].astype(F32)
            grad = r.res[lax.div(g, 2), at] + norm_backward(x, inverse_rms(x), sum3.total(at) * r.gain1[...])
            out_bytes[at] = grad.astype(BF16)

    jobs[QO].start1()
    jobs[GU1].start2()
    jobs[DN].swap()
    jobs[QO].relay1()

    for c in range(2):
        sum4.arrive(c)

        @pl.loop(0, 4)
        def _(k):
            at = (pl.ds(16 * c, 16), rows_at(0, k, 1024))
            out_patches[at] = sum4.total(*at).astype(BF16)

    jobs[VV].start2()
    jobs[KK].start2()
    jobs[GU2].start2()
    jobs[KK].relay2()
    jobs[QO].start2()
    jobs[VV].relay2()
    jobs[GU1].relay2()
    jobs[QO].relay2()
    jobs[KK].start3()
    jobs[DN].start2()
    jobs[VV].start3()
    jobs[GU2].relay2()
    jobs[DN].relay2()
    jobs[QO].start3()
    for n in (GU1, GU2, KK, VV, DN, QO):
        place_piece(n, jobs[n].finish(), flat)
    for item in (*jobs, sum3, sum4, swap1, swap2):
        item.drain()


def shards(
    byte_states,
    patch_states,
    patch_lengths,
    cotangent,
    attention_gain,
    feedforward_gain,
    query_weight,
    key_weight,
    value_weight,
    output_weight,
    gate_weight,
    up_weight,
    down_weight,
    adam_first,
    adam_second,
):
    plain, sums, jobs = layer_scratch()
    vmem = pl.BlockSpec(memory_space=pltpu.VMEM)
    summed, input_grad, patch_grad = pl.pallas_call(
        layer_kernel,
        out_shape=(
            jax.ShapeDtypeStruct((FLAT, 128), F32),
            jax.ShapeDtypeStruct((128, D), BF16),
            jax.ShapeDtypeStruct((32, DG), BF16),
        ),
        in_specs=[vmem] * 3 + [pl.BlockSpec(memory_space=pl.ANY)] * 10,
        out_specs=(vmem, vmem, vmem),
        scratch_shapes=[*plain.values(), *(s for group in (*sums, *jobs) for s in group)],
        compiler_params=pltpu.CompilerParams(
            collective_id=0, has_side_effects=True, vmem_limit_bytes=63 * MIB
        ),
    )(
        patch_lengths,
        attention_gain,
        feedforward_gain,
        byte_states.reshape(4, 128, D),
        patch_states,
        cotangent.reshape(4, 128, D),
        query_weight,
        key_weight,
        value_weight,
        output_weight,
        gate_weight,
        up_weight,
        down_weight,
    )
    summed, adam_first, adam_second = lax.optimization_barrier((summed, adam_first, adam_second))
    gradient = summed * TOKEN_SCALE
    new_first = beta_first * adam_first.reshape(FLAT, 128) + (1.0 - beta_first) * gradient
    new_second = beta_second * adam_second.reshape(FLAT, 128) + (1.0 - beta_second) * gradient * gradient
    adam_step = new_first / bias_first / (jnp.sqrt(new_second / bias_second) + adam_epsilon)
    return (
        input_grad,
        patch_grad,
        new_first.reshape(1, -1),
        new_second.reshape(1, -1),
        adam_step.reshape(1, -1),
    )


def solution(mesh):
    placed = (
        P("dp", None),
        P("dp", None),
        P("dp", None),
        P("dp", None),
        P(),
        P(),
        P(None, "heads"),
        P(None, "heads"),
        P(None, "heads"),
        P("heads", None),
        P(None, "heads"),
        P(None, "heads"),
        P("heads", None),
        P("heads", "dp"),
        P("heads", "dp"),
    )
    return jax.shard_map(
        shards,
        mesh=mesh,
        in_specs=placed,
        out_specs=(
            P(("dp", "heads"), None),
            P(("dp", "heads"), None),
            P("heads", "dp"),
            P("heads", "dp"),
            P("heads", "dp"),
        ),
        check_vma=False,
    )
```

```python
import jax
import jax.numpy as jnp
from jax import lax
from jax.experimental import pallas as pl
from jax.experimental.pallas import tpu as pltpu
from jax.sharding import PartitionSpec as P

HEAD = 128

norm_epsilon = 1e-05
adam_epsilon = 1e-08
beta_first = 0.9
beta_second = 0.95
score_scale = 0.125
bias_first = 1.0 - 0.9**20
bias_second = 1.0 - 0.95**20

BF16 = jnp.bfloat16
F32 = jnp.float32
MESH_ID = pl.DeviceIdType.MESH
MIB = 1 << 20

D = 1280
DG = 4096
UNITS = 896
UNIT_TILES = ((0, 256), (256, 512), (512, 768), (768, 896))
WIDE_TILES = tuple((n, n + 256) for n in range(0, D, 256))
FLAT = 1512
TOKEN_SCALE = 16384.0**-0.5

GU1, GU2, DN, KK, VV, QO = range(6)
PIECES = (
    (80, 640, True),
    (80, 256, False),
    (32, 1280, False),
    (128, 256, True),
    (128, 256, False),
    (160, 128, True),
)
LATE = (KK, VV, QO)


def nn(left, right):
    return lax.dot_general(left, right, (((1,), (0,)), ((), ())), preferred_element_type=F32)


def nt(left, right):
    return lax.dot_general(left, right, (((1,), (1,)), ((), ())), preferred_element_type=F32)


def tn(left, right):
    return lax.dot_general(left, right, (((0,), (0,)), ((), ())), preferred_element_type=F32)


def inverse_rms(x):
    return lax.rsqrt(jnp.mean(x * x, axis=-1, keepdims=True) + norm_epsilon)


def norm_backward(x, inverse, scaled):
    inner = jnp.mean(scaled * x, axis=-1, keepdims=True)
    return inverse * scaled - x * (inverse * inverse * inverse) * inner


def place():
    dp = lax.axis_index("dp")
    return lax.div(dp, 8), lax.rem(lax.div(dp, 2), 4), lax.rem(dp, 2), lax.axis_index("heads")


def device_at(z, x, y, g):
    return (z * 8 + x * 2 + y, g)


def remote(src, dst, send, recv, dev):
    return pltpu.make_async_remote_copy(
        src_ref=src, dst_ref=dst, send_sem=send, recv_sem=recv, device_id=dev, device_id_type=MESH_ID
    )


def scatter_scratch(item):
    rows, cols, _ = PIECES[item]
    shapes = ((2,), (2, 2), ()) if item in LATE else ((4,), (), (2,))
    ends = [pltpu.VMEM((*m, rows, cols), BF16) for m in shapes]
    return [
        pltpu.VMEM((4, 4, 2, rows, cols), BF16),
        pltpu.VMEM((2, 2, 2, rows, cols), BF16),
        pltpu.VMEM((2, 4, 2, rows, cols), BF16),
        *ends,
        pltpu.SemaphoreType.DMA((13,)),
        pltpu.SemaphoreType.DMA((13,)),
    ]


class Scatter:
    def __init__(self, item, refs):
        rows, _, self.zfirst = PIECES[item]
        cut = 16 * ((rows // 16 + 1) // 2)
        self.halves = (slice(0, cut), slice(cut, rows))
        self.unpack(refs)
        z, x, self.y, self.g = place()
        self.f, self.s = (z, x) if self.zfirst else (x, z)
        self.live = {}

    def unpack(self, refs):
        self.grad, self.near, self.got, self.pairs, self.near2, self.got2, self.send, self.recv = refs

    def at(self, f, s):
        return (f, s) if self.zfirst else (s, f)

    def mine(self, s, y):
        return (*self.at(self.f, s), y)

    def who(self, f, s, y):
        z, x = self.at(f, s)
        return device_at(z, x, y, self.g)

    def copy(self, n, src, dst, dev):
        c = remote(src, dst, self.send.at[n], self.recv.at[n], dev)
        c.start()
        self.live[n] = c

    def start1(self):
        far = lax.rem(self.f + 2, 4)
        for i, d in enumerate((1, 3)):
            dev = self.who(lax.rem(self.f + d, 4), self.s, self.y)
            self.copy(i, self.grad.at[self.at(far, pl.ds(2 * i, 2))], self.near.at[i], dev)
        for i, d in enumerate((1, 3)):
            nxt = lax.rem(self.f + d, 4)
            dev = self.who(nxt, self.s, self.y)
            rest = pl.ds(2 * (1 - i), 2)
            self.copy(2 + i, self.grad.at[self.at(nxt, rest)], self.got.at[i, rest], dev)

    def relay1(self):
        for i, d in enumerate((1, 3)):
            nxt = lax.rem(self.f + d, 4)
            dev = self.who(nxt, self.s, self.y)
            self.live[i].wait_recv()

            @pl.loop(0, 4)
            def _(k):
                a, b = lax.div(k, 2), lax.rem(k, 2)
                own = self.grad[(*self.at(nxt, 2 * i + a), b)].astype(F32)
                self.near[i, a, b] = (own + self.near[i, a, b].astype(F32)).astype(BF16)

            self.copy(4 + i, self.near.at[i], self.got.at[i, pl.ds(2 * i, 2)], dev)

    def sum_mine(self, y):
        @pl.loop(0, 4)
        def _(a):
            own = self.grad[self.mine(a, y)].astype(F32)
            total = own + self.got[0, a, y].astype(F32) + self.got[1, a, y].astype(F32)
            self.grad[self.mine(a, y)] = total.astype(BF16)

    def swap(self):
        for n in (2, 3, 4, 5):
            self.live[n].wait_recv()
        other = 1 - self.y
        self.sum_mine(other)
        self.copy(12, self.grad.at[self.mine(slice(None), other)], self.pairs, self.who(self.f, self.s, other))
        self.sum_mine(self.y)

    def start2(self):
        self.live[12].wait_recv()

        @pl.loop(0, 4)
        def _(a):
            at = self.mine(a, self.y)
            self.grad[at] = (self.grad[at].astype(F32) + self.pairs[a].astype(F32)).astype(BF16)

        for i, d in enumerate((1, 3)):
            dev = self.who(self.f, lax.rem(self.s + d, 4), self.y)
            at = self.halves[i]
            self.copy(6 + i, self.grad.at[(*self.mine(lax.rem(self.s + 2, 4), self.y), at)], self.near2.at[at], dev)
        for i, d in enumerate((1, 3)):
            nxt = lax.rem(self.s + d, 4)
            dev = self.who(self.f, nxt, self.y)
            at = self.halves[1 - i]
            self.copy(8 + i, self.grad.at[(*self.mine(nxt, self.y), at)], self.got2.at[i, at], dev)

    def relay2(self):
        for i, d in enumerate((1, 3)):
            nxt = lax.rem(self.s + d, 4)
            dev = self.who(self.f, nxt, self.y)
            at = self.halves[i]
            self.live[6 + i].wait_recv()
            own = self.grad[(*self.mine(nxt, self.y), at)].astype(F32)
            self.near2[at] = (own + self.near2[at].astype(F32)).astype(BF16)
            self.copy(10 + i, self.near2.at[at], self.got2.at[i, at], dev)

    def finish(self):
        for n in (8, 9, 10, 11):
            self.live[n].wait_recv()
        own = self.grad[self.mine(self.s, self.y)].astype(F32)
        return own + self.got2[0].astype(F32) + self.got2[1].astype(F32)

    def drain(self):
        for c in self.live.values():
            c.wait_send()


class ScatterLate(Scatter):
    def unpack(self, refs):
        self.grad, self.near, self.got, self.near2, self.got2, self.last, self.send, self.recv = refs

    def start2(self):
        for n in (2, 3, 4, 5):
            self.live[n].wait_recv()

        @pl.loop(0, 8)
        def _(k):
            a, b = lax.div(k, 2), lax.rem(k, 2)
            own = self.grad[self.mine(a, b)].astype(F32)
            total = own + self.got[0, a, b].astype(F32) + self.got[1, a, b].astype(F32)
            self.grad[self.mine(a, b)] = total.astype(BF16)

        for i, d in enumerate((1, 3)):
            dev = self.who(self.f, lax.rem(self.s + d, 4), self.y)
            self.copy(6 + i, self.grad.at[self.mine(lax.rem(self.s + 2, 4), i)], self.near2.at[i], dev)
        for i, d in enumerate((1, 3)):
            nxt = lax.rem(self.s + d, 4)
            dev = self.who(self.f, nxt, self.y)
            self.copy(8 + i, self.grad.at[self.mine(nxt, 1 - i)], self.got2.at[i, 1 - i], dev)

    def relay2(self):
        for i, d in enumerate((1, 3)):
            nxt = lax.rem(self.s + d, 4)
            dev = self.who(self.f, nxt, self.y)
            self.live[6 + i].wait_recv()
            own = self.grad[self.mine(nxt, i)].astype(F32)
            self.near2[i] = (own + self.near2[i].astype(F32)).astype(BF16)
            self.copy(10 + i, self.near2.at[i], self.got2.at[i, i], dev)

    def start3(self):
        for n in (8, 9, 10, 11):
            self.live[n].wait_recv()
        for b in range(2):
            own = self.grad[self.mine(self.s, b)].astype(F32)
            total = own + self.got2[0, b].astype(F32) + self.got2[1, b].astype(F32)
            self.grad[self.mine(self.s, b)] = total.astype(BF16)
        other = 1 - self.y
        self.copy(12, self.grad.at[self.mine(self.s, other)], self.last, self.who(self.f, self.s, other))

    def finish(self):
        self.live[12].wait_recv()
        return self.grad[self.mine(self.s, self.y)].astype(F32) + self.last[...].astype(F32)


def heads_place():
    g = lax.axis_index("heads")
    y, core = lax.div(g, 2), lax.rem(g, 2)
    return g, y * 2 + 1 - core, (1 - y) * 2 + core, (1 - y) * 2 + 1 - core


def sum_scratch(rows, cols):
    return [
        pltpu.VMEM((2, rows, cols), BF16),
        pltpu.VMEM((rows, cols), BF16),
        pltpu.SemaphoreType.DMA((4,)),
        pltpu.SemaphoreType.DMA((4,)),
    ]


def pair_scratch():
    return [
        pltpu.VMEM((2, 128, D), BF16),
        pltpu.VMEM((2, 128, D), BF16),
        pltpu.SemaphoreType.DMA((6,)),
        pltpu.SemaphoreType.DMA((6,)),
    ]


class HeadsSum:
    def __init__(self, parts, rows, refs):
        self.parts, self.rows = parts, rows
        self.near, self.far, self.send, self.recv = refs
        self.live = {}
        self.dp = lax.axis_index("dp")
        self.g, self.mate, self.over, self.over_mate = heads_place()

    def send_near(self, slot):
        quarter = (self.over_mate, self.mate)[slot]
        c = remote(self.parts.at[quarter], self.near.at[slot], self.send.at[slot], self.recv.at[slot], (self.dp, self.mate))
        c.start()
        self.live[slot] = c

    def relay(self):
        self.live[0].wait_recv()
        half = self.rows // 2
        for c in range(2):

            @pl.loop(0, half // 16)
            def _(k):
                at = pl.ds(pl.multiple_of(c * half + 16 * k, 16), 16)
                total = self.near[0, at].astype(F32) + self.parts[self.over, at].astype(F32)
                self.near[0, at] = total.astype(BF16)

            at = pl.ds(c * half, half)
            copy = remote(
                self.near.at[0, at], self.far.at[at], self.send.at[2 + c], self.recv.at[2 + c], (self.dp, self.over)
            )
            copy.start()
            self.live[2 + c] = copy

    def arrive(self, c):
        if c == 0:
            self.live[1].wait_recv()
        self.live[2 + c].wait_recv()

    def total(self, *at):
        return (
            self.parts[(self.g, *at)].astype(F32) + self.near[(1, *at)].astype(F32) + self.far[at].astype(F32)
        )

    def drain(self):
        for c in self.live.values():
            c.wait_send()


class PairSum:
    def __init__(self, parts, refs):
        self.parts = parts
        self.near, self.far, self.send, self.recv = refs
        self.live = {}
        self.dp = lax.axis_index("dp")
        self.g, self.mate, self.over, _ = heads_place()
        self.core = lax.rem(self.g, 2)

    def copy(self, n, src, dst, dev):
        c = remote(src, dst, self.send.at[n], self.recv.at[n], (self.dp, dev))
        c.start()
        self.live[n] = c

    def send_near(self, b):
        self.copy(b, self.parts.at[2 * b + 1 - self.core], self.near.at[b], self.mate)

    def relay(self, b):
        self.live[b].wait_recv()
        for c in range(2):

            @pl.loop(0, 4)
            def _(k):
                at = pl.ds(pl.multiple_of(c * 64 + 16 * k, 16), 16)
                total = self.near[b, at].astype(F32) + self.parts[2 * b + self.core, at].astype(F32)
                self.near[b, at] = total.astype(BF16)

            at = pl.ds(c * 64, 64)
            self.copy(2 + 2 * b + c, self.near.at[b, at], self.far.at[b, at], self.over)

    def arrive(self, b, c):
        self.live[2 + 2 * b + c].wait_recv()

    def total(self, b, at):
        return self.near[b, at].astype(F32) + self.far[b, at].astype(F32)

    def drain(self):
        for c in self.live.values():
            c.wait_send()


class CoreSwap:
    def __init__(self, whole, send, recv):
        self.whole, self.send_sem, self.recv_sem = whole, send, recv
        self.live = {}
        self.dp = lax.axis_index("dp")
        self.g, self.mate, _, _ = heads_place()
        self.core = lax.rem(self.g, 2)

    def give(self, b, c):
        n = 2 * b + c
        ref = self.whole.at[2 * b + self.core, pl.ds(64 * c, 64)]
        copy = remote(ref, ref, self.send_sem.at[n], self.recv_sem.at[n], (self.dp, self.mate))
        copy.start()
        self.live[n] = copy

    def take(self, b):
        for c in range(2):
            self.live[2 * b + c].wait_recv()

    def drain(self):
        for c in self.live.values():
            c.wait_send()


def spread_rows(flat, start, per_row, block):
    rows, cols = block.shape
    for c in range(cols // 128):
        flat[pl.ds(start + c, rows, per_row), :] = block[:, c * 128 : (c + 1) * 128]


def place_piece(item, total, flat):
    if item == QO:
        for c in range(2):
            spread_rows(flat, c, 2, total[40 * c : 40 * c + 40])
        for c in range(10):
            spread_rows(flat, 592 + c, 10, total[80 + 8 * c : 88 + 8 * c])
    elif item == KK:
        spread_rows(flat, 80, 2, total)
    elif item == VV:
        spread_rows(flat, 336, 2, total)
    elif item == DN:
        spread_rows(flat, 1232, 10, total[0:28])
    else:
        first = 0 if item == GU1 else 5
        spread_rows(flat, 672 + first, 7, total[0:40])
        spread_rows(flat, 952 + first, 7, total[40:80])


def greet():
    z, x, y, g = place()
    dp = lax.axis_index("dp")
    _, mate, over, _ = heads_place()
    partners = [
        (dp, mate),
        (dp, over),
        device_at(lax.rem(z + 1, 4), x, y, g),
        device_at(lax.rem(z + 3, 4), x, y, g),
        device_at(z, lax.rem(x + 1, 4), y, g),
        device_at(z, lax.rem(x + 3, 4), y, g),
        device_at(z, x, 1 - y, g),
    ]
    barrier = pltpu.get_barrier_semaphore()
    for dev in partners:
        pl.semaphore_signal(barrier, inc=1, device_id=dev, device_id_type=MESH_ID)
    pl.semaphore_wait(barrier, len(partners))


def rows_at(first, k, size):
    return pl.ds(pl.multiple_of(first + size * k, size), size)


def layer_scratch():
    quarters = lambda cols, kind: pltpu.VMEM((4, 128, cols), kind)
    plain = dict(
        states=quarters(D, BF16),
        patches=pltpu.VMEM((128, DG), BF16),
        cot=quarters(D, BF16),
        wq=pltpu.VMEM((D, 256), BF16),
        wk=pltpu.VMEM((DG, 256), BF16),
        wv=pltpu.VMEM((DG, 256), BF16),
        wo=pltpu.VMEM((256, D), BF16),
        wg=pltpu.VMEM((D, UNITS), BF16),
        wu=pltpu.VMEM((D, UNITS), BF16),
        wd=pltpu.VMEM((UNITS, D), BF16),
        loads=pltpu.SemaphoreType.DMA((10,)),
        normed=quarters(D, BF16),
        query=quarters(256, F32),
        key=pltpu.VMEM((128, 256), F32),
        keyn=pltpu.VMEM((128, 256), BF16),
        value=pltpu.VMEM((128, 256), BF16),
        att=quarters(256, BF16),
        part1=quarters(D, BF16),
        part2=quarters(D, BF16),
        part4=pltpu.VMEM((4, 32, DG), BF16),
        res=pltpu.VMEM((2, 128, D), F32),
        gain1=pltpu.VMEM((1, D), F32),
        gain2=pltpu.VMEM((1, D), F32),
        nh=quarters(D, BF16),
        rh=quarters(D, BF16),
        turned=pltpu.VMEM((D, 512), BF16),
        hgrad=pltpu.VMEM((512, UNITS), F32),
        gg=pltpu.VMEM((512, UNITS), BF16),
        ug=pltpu.VMEM((512, UNITS), BF16),
        qgrad=quarters(256, BF16),
        keyg=pltpu.VMEM((128, 256), F32),
        valg=pltpu.VMEM((128, 256), F32),
        kg=pltpu.VMEM((128, 256), BF16),
        vg=pltpu.VMEM((128, 256), BF16),
        down=pltpu.VMEM((120, D), F32),
        g1s=pltpu.SemaphoreType.DMA((4,)),
        g1r=pltpu.SemaphoreType.DMA((4,)),
        g2s=pltpu.SemaphoreType.DMA((4,)),
        g2r=pltpu.SemaphoreType.DMA((4,)),
    )
    sums = [pair_scratch(), pair_scratch(), sum_scratch(128, D), sum_scratch(32, DG)]
    jobs = [scatter_scratch(i) for i in range(len(PIECES))]
    return plain, sums, jobs


class Refs:
    pass


def layer_kernel(*refs):
    (lengths, again, fgain, states_h, patches_h, cot_h, wq_h, wk_h, wv_h, wo_h, wg_h, wu_h, wd_h,
     flat, out_bytes, out_patches) = refs[:16]
    plain, sums, jobs = layer_scratch()
    rest = list(refs[16:])
    r = Refs()
    for name in plain:
        setattr(r, name, rest.pop(0))
    r.hid = r.wd.at[0:512, 0:UNITS]
    r.attt = r.wd.at[512:768, 0:512]
    sum_refs = [[rest.pop(0) for _ in s] for s in sums]
    jobs = [(ScatterLate if i in LATE else Scatter)(i, [rest.pop(0) for _ in s]) for i, s in enumerate(jobs)]
    g, _, _, _ = heads_place()
    core = lax.rem(g, 2)

    moves = {}
    order = [
        ("patches", patches_h), ("wk", wk_h), ("wv", wv_h), ("states", states_h), ("wq", wq_h), ("wo", wo_h),
        ("cot", cot_h), ("wd", wd_h), ("wg", wg_h), ("wu", wu_h),
    ]
    for i, (name, src) in enumerate(order):
        moves[name] = pltpu.make_async_copy(src, getattr(r, name), r.loads.at[i])
    for name in ("patches", "wk", "wv", "states", "wq"):
        moves[name].start()
    r.gain1[...] = again[...].reshape(1, D)
    r.gain2[...] = fgain[...].reshape(1, D)
    greet()

    sum1 = PairSum(r.part1, sum_refs[0])
    sum2 = PairSum(r.part2, sum_refs[1])
    sum3 = HeadsSum(r.part1, 128, sum_refs[2])
    sum4 = HeadsSum(r.part4, 32, sum_refs[3])
    swap1 = CoreSwap(r.nh, r.g1s, r.g1r)
    swap2 = CoreSwap(r.rh, r.g2s, r.g2r)

    moves["patches"].wait()
    moves["wk"].wait()
    for name in ("wo", "cot", "wd", "wg", "wu"):
        moves[name].start()
    key = nn(r.patches[...], r.wk[...])
    r.key[...] = key
    for h in range(2):
        cols = slice(HEAD * h, HEAD * h + HEAD)
        one = key[:, cols]
        r.keyn[:, cols] = (one * inverse_rms(one)).astype(BF16)
    moves["wv"].wait()
    r.value[...] = nn(r.patches[...], r.wv[...]).astype(BF16)
    earlier = lax.broadcasted_iota(jnp.int32, (128, 128), 0) < lax.broadcasted_iota(jnp.int32, (128, 128), 1)
    spans = jnp.broadcast_to(lengths[...].astype(F32), (16, 128)).astype(BF16)
    starts = nn(spans, earlier.astype(F32).astype(BF16))[0:1]

    def head_probabilities(qi, h):
        cols = slice(HEAD * h, HEAD * h + HEAD)
        full = r.query[qi, :, cols]
        inverse = inverse_rms(full)
        query = (full * inverse).astype(BF16)
        scores = score_scale * nt(query, r.keyn[:, cols])
        position = (lax.broadcasted_iota(jnp.int32, (128, 128), 0) + qi * 128).astype(F32)
        weights = jnp.where(starts <= position, jnp.exp(scores), 0.0)
        return full, inverse, query, weights / jnp.sum(weights, axis=-1, keepdims=True)

    moves["states"].wait()
    moves["wq"].wait()
    moves["wo"].wait()

    def attend(qi):
        @pl.loop(0, 4)
        def _(k):
            at = rows_at(0, k, 32)
            x = r.states[qi, at].astype(F32)
            r.normed[qi, at] = (x * inverse_rms(x) * r.gain1[...]).astype(BF16)

        r.query[qi] = nn(r.normed[qi], r.wq[...])
        for h in range(2):
            cols = slice(HEAD * h, HEAD * h + HEAD)
            prob = head_probabilities(qi, h)[3]
            r.att[qi, :, cols] = nn(prob.astype(BF16), r.value[:, cols]).astype(BF16)
        for lo, hi in WIDE_TILES:
            r.part1[qi, :, lo:hi] = nn(r.att[qi], r.wo[:, lo:hi]).astype(BF16)

    for b in range(2):
        attend(2 * b + 1 - core)
        sum1.send_near(b)
        attend(2 * b + core)
        sum1.relay(b)

    moves["cot"].wait()
    moves["wd"].wait()

    @pl.loop(0, 2)
    def _(p):
        at = rows_at(0, p, 256)
        cot = r.cot[pl.ds(2 * p, 2)].reshape(256, D)
        for lo, hi in UNIT_TILES:
            r.hgrad[at, lo:hi] = nt(cot, r.wd[lo:hi, :])

    def residual(b):
        for c in range(2):
            sum1.arrive(b, c)

            @pl.loop(0, 2)
            def _(k):
                at = rows_at(64 * c, k, 32)
                res = r.states[2 * b + core, at].astype(F32) + sum1.total(b, at)
                r.res[b, at] = res
                r.nh[2 * b + core, at] = (res * inverse_rms(res) * r.gain2[...]).astype(BF16)

            swap1.give(b, c)

    def residual_back(b):
        for c in range(2):
            sum2.arrive(b, c)

            @pl.loop(0, 2)
            def _(k):
                at = rows_at(64 * c, k, 32)
                res = r.res[b, at]
                grad = norm_backward(res, inverse_rms(res), sum2.total(b, at) * r.gain2[...])
                grad = grad + r.cot[2 * b + core, at].astype(F32)
                r.res[b, at] = grad
                r.rh[2 * b + core, at] = grad.astype(BF16)

            swap2.give(b, c)

    residual(0)
    moves["wg"].wait()
    moves["wu"].wait()

    def feed(p):
        at = slice(256 * p, 256 * p + 256)
        normed = r.nh[pl.ds(2 * p, 2)].reshape(256, D)
        for lo, hi in UNIT_TILES:
            gate = nn(normed, r.wg[:, lo:hi])
            up = nn(normed, r.wu[:, lo:hi])
            back = r.hgrad[at, lo:hi]
            sigma = jax.nn.sigmoid(gate)
            active = gate * sigma
            r.hid[at, lo:hi] = (active * up).astype(BF16)
            r.gg[at, lo:hi] = (back * up * (sigma * (1.0 + gate * (1.0 - sigma)))).astype(BF16)
            r.ug[at, lo:hi] = (back * active).astype(BF16)
        for lo, hi in WIDE_TILES:
            part = nt(r.gg[at], r.wg[lo:hi, :]) + nt(r.ug[at], r.wu[lo:hi, :])
            r.part2[pl.ds(2 * p, 2), :, lo:hi] = part.astype(BF16).reshape(2, 128, hi - lo)

    def store(ref, at, rows, cols, new, again_):
        at = (*at, rows, cols)
        if again_:
            new = new + ref[at].astype(F32)
        ref[at] = new.astype(BF16)

    def turn(p):
        for q in (2 * p, 2 * p + 1):
            r.turned[:, 128 * q : 128 * q + 128] = r.nh[q].T

    def gate_up_grads(p):
        @pl.loop(0, 8)
        def _(c):
            rows = r.turned[rows_at(0, c, 160), 256 * p : 256 * p + 256]
            z, x = lax.div(c, 2), 2 * lax.rem(c, 2)
            for grad, row in ((r.gg, 0), (r.ug, 40)):
                for job, lo, hi in ((GU1, 0, 256), (GU1, 256, 512), (GU1, 512, 640), (GU2, 640, 896)):
                    got = nn(rows, grad[256 * p : 256 * p + 256, lo:hi])
                    col = lo if job == GU1 else 0
                    for j in range(4):
                        store(
                            jobs[job].grad, (z, x + j // 2, j % 2), slice(row, row + 40), slice(col, col + hi - lo),
                            got[40 * j : 40 * j + 40], p,
                        )

    def down_grads(p):
        for q in (2 * p, 2 * p + 1):
            r.turned[0:UNITS, 128 * q : 128 * q + 128] = r.hid[128 * q : 128 * q + 128].T

        @pl.loop(0, 8)
        def _(c):
            rows = r.turned[rows_at(0, c, 112), 256 * p : 256 * p + 256]
            for lo, hi in WIDE_TILES:
                r.down[0:112, lo:hi] = nn(rows, r.cot[2 * p : 2 * p + 2, :, lo:hi].reshape(256, hi - lo))
            z, x = lax.div(c, 2), 2 * lax.rem(c, 2)
            for j in range(4):
                store(
                    jobs[DN].grad, (z, x + j // 2, j % 2), slice(0, 32), slice(0, D), r.down[28 * j : 28 * j + 32], p
                )

    r.down[112:120] = jnp.zeros((8, D), F32)
    swap1.take(0)
    feed(0)
    sum2.send_near(0)
    turn(0)
    sum2.relay(0)
    gate_up_grads(0)
    residual(1)
    down_grads(0)
    swap1.take(1)
    sum1.drain()
    feed(1)
    sum2.send_near(1)
    turn(1)
    sum2.relay(1)
    gate_up_grads(1)
    jobs[GU1].start1()
    jobs[GU2].start1()
    residual_back(0)
    down_grads(1)
    jobs[GU2].relay1()
    jobs[DN].start1()

    r.keyg[...] = jnp.zeros((128, 256), F32)
    r.valg[...] = jnp.zeros((128, 256), F32)

    def attend_back(qi):
        agrad = nt(r.rh[qi], r.wo[...]).astype(BF16)
        for h in range(2):
            cols = slice(HEAD * h, HEAD * h + HEAD)
            full, inverse, query, prob = head_probabilities(qi, h)
            back = nt(agrad[:, cols], r.value[:, cols])
            inner = jnp.sum(prob * back, axis=-1, keepdims=True)
            score = (score_scale * prob * (back - inner)).astype(BF16)
            grad = nn(score, r.keyn[:, cols])
            r.keyg[:, cols] += tn(score, query)
            r.valg[:, cols] += tn(prob.astype(BF16), agrad[:, cols])
            r.qgrad[qi, :, cols] = norm_backward(full, inverse, grad).astype(BF16)

    attend_back(core)
    swap2.take(0)
    attend_back(1 - core)
    residual_back(1)
    attend_back(2 + core)
    swap2.take(1)
    sum2.drain()
    attend_back(3 - core)
    for h in range(2):
        cols = slice(HEAD * h, HEAD * h + HEAD)
        full = r.key[:, cols]
        r.kg[:, cols] = norm_backward(full, inverse_rms(full), r.keyg[:, cols]).astype(BF16)
    r.vg[...] = r.valg[...].astype(BF16)

    jobs[GU1].relay1()

    @pl.loop(0, 8)
    def _(n):
        rows = r.patches[:, rows_at(0, n, 512)].T
        z, x = lax.div(n, 2), 2 * lax.rem(n, 2)
        for job, grad in ((KK, r.kg), (VV, r.vg)):
            got = nn(rows, grad[...]).astype(BF16)
            for j in range(4):
                jobs[job].grad[z, x + j // 2, j % 2] = got[128 * j : 128 * j + 128]

    jobs[VV].start1()
    jobs[KK].start1()

    for q in range(4):
        r.turned[:, 128 * q : 128 * q + 128] = r.normed[q].T
        r.attt[:, 128 * q : 128 * q + 128] = r.att[q].T
    for half in range(2):
        for lo, hi in ((0, 256), (256, 512), (512, 640)):
            cols = slice(640 * half + lo, 640 * half + hi)
            r.hgrad[256 * half : 256 * half + 256, lo:hi] = nn(
                r.attt[...], r.rh[:, :, cols].reshape(512, hi - lo)
            )

    @pl.loop(0, 4)
    def _(c):
        got = nn(r.turned[rows_at(0, c, 320)], r.qgrad[...].reshape(512, 256))
        for j in range(8):
            mine = got[40 * j : 40 * j + 40]
            halves = [r.hgrad[rows_at(256 * half + 8 * j, c * 8, 8), 0:640] for half in range(2)]
            blocks = [mine[:, :128], mine[:, 128:]]
            blocks += [m[:, 128 * n : 128 * n + 128] for m in halves for n in range(5)]
            jobs[QO].grad[c, j // 2, j % 2] = jnp.concatenate(blocks, axis=0).astype(BF16)


    @pl.loop(0, 2)
    def _(p):
        grad = r.qgrad[pl.ds(2 * p, 2)].reshape(256, 256)
        for lo, hi in WIDE_TILES:
            r.part1[pl.ds(2 * p, 2), :, lo:hi] = nt(grad, r.wq[lo:hi, :]).astype(BF16).reshape(2, 128, hi - lo)

    sum3.send_near(0)
    sum3.send_near(1)

    @pl.loop(0, 16)
    def _(n):
        at = rows_at(0, n, 256)
        part = nt(r.kg[...], r.wk[at]) + nt(r.vg[...], r.wv[at])
        r.part4[:, :, at] = part.astype(BF16).reshape(4, 32, 256)

    sum4.send_near(0)
    sum4.send_near(1)
    sum3.relay()
    jobs[GU1].swap()
    jobs[GU2].swap()
    sum4.relay()
    jobs[DN].relay1()
    jobs[KK].relay1()
    jobs[VV].relay1()

    for c in range(2):
        sum3.arrive(c)

        @pl.loop(0, 2)
        def _(k):
            at = rows_at(64 * c, k, 32)
            x = r.states[g, at].astype(F32)
            grad = r.res[lax.div(g, 2), at] + norm_backward(x, inverse_rms(x), sum3.total(at) * r.gain1[...])
            out_bytes[at] = grad.astype(BF16)

    jobs[QO].start1()
    jobs[GU1].start2()
    jobs[DN].swap()
    jobs[QO].relay1()

    for c in range(2):
        sum4.arrive(c)

        @pl.loop(0, 4)
        def _(k):
            at = (pl.ds(16 * c, 16), rows_at(0, k, 1024))
            out_patches[at] = sum4.total(*at).astype(BF16)

    jobs[VV].start2()
    jobs[KK].start2()
    jobs[GU2].start2()
    jobs[KK].relay2()
    jobs[QO].start2()
    jobs[VV].relay2()
    jobs[GU1].relay2()
    jobs[QO].relay2()
    jobs[KK].start3()
    jobs[DN].start2()
    jobs[VV].start3()
    jobs[GU2].relay2()
    jobs[DN].relay2()
    jobs[QO].start3()
    for n in (GU1, GU2, KK, VV, DN, QO):
        place_piece(n, jobs[n].finish(), flat)
    for item in (*jobs, sum3, sum4, swap1, swap2):
        item.drain()


def adam_kernel(summed, first, second, bytes_in, patches_in, new_first, new_second, step, bytes_out, patches_out):
    bytes_out[...] = bytes_in[...]
    patches_out[...] = patches_in[...]

    gradient = summed[...] * TOKEN_SCALE
    moment = beta_first * first[...] + (1.0 - beta_first) * gradient
    spread = beta_second * second[...] + (1.0 - beta_second) * gradient * gradient
    new_first[...] = moment
    new_second[...] = spread
    step[...] = moment / bias_first / (jnp.sqrt(spread / bias_second) + adam_epsilon)


def adam(summed, first, second, input_grad, patch_grad):
    vmem = pl.BlockSpec(memory_space=pltpu.VMEM)
    return pl.pallas_call(
        adam_kernel,
        out_shape=[jax.ShapeDtypeStruct((FLAT, 128), F32)] * 3
        + [jax.ShapeDtypeStruct(m.shape, m.dtype) for m in (input_grad, patch_grad)],
        in_specs=[vmem] * 5,
        out_specs=[vmem] * 5,
        compiler_params=pltpu.CompilerParams(vmem_limit_bytes=60 * MIB),
    )(summed, first, second, input_grad, patch_grad)


def shards(
    byte_states,
    patch_states,
    patch_lengths,
    cotangent,
    attention_gain,
    feedforward_gain,
    query_weight,
    key_weight,
    value_weight,
    output_weight,
    gate_weight,
    up_weight,
    down_weight,
    adam_first,
    adam_second,
):
    plain, sums, jobs = layer_scratch()
    vmem = pl.BlockSpec(memory_space=pltpu.VMEM)
    summed, input_grad, patch_grad = pl.pallas_call(
        layer_kernel,
        out_shape=(
            jax.ShapeDtypeStruct((FLAT, 128), F32),
            jax.ShapeDtypeStruct((128, D), BF16),
            jax.ShapeDtypeStruct((32, DG), BF16),
        ),
        in_specs=[vmem] * 3 + [pl.BlockSpec(memory_space=pl.ANY)] * 10,
        out_specs=(vmem, vmem, vmem),
        scratch_shapes=[*plain.values(), *(s for group in (*sums, *jobs) for s in group)],
        compiler_params=pltpu.CompilerParams(
            collective_id=0, has_side_effects=True, vmem_limit_bytes=63 * MIB
        ),
    )(
        patch_lengths,
        attention_gain,
        feedforward_gain,
        byte_states.reshape(4, 128, D),
        patch_states,
        cotangent.reshape(4, 128, D),
        query_weight,
        key_weight,
        value_weight,
        output_weight,
        gate_weight,
        up_weight,
        down_weight,
    )
    new_first, new_second, adam_step, input_grad, patch_grad = adam(
        summed, adam_first.reshape(FLAT, 128), adam_second.reshape(FLAT, 128), input_grad, patch_grad
    )
    return (
        input_grad,
        patch_grad,
        new_first.reshape(1, -1),
        new_second.reshape(1, -1),
        adam_step.reshape(1, -1),
    )


def solution(mesh):
    placed = (
        P("dp", None),
        P("dp", None),
        P("dp", None),
        P("dp", None),
        P(),
        P(),
        P(None, "heads"),
        P(None, "heads"),
        P(None, "heads"),
        P("heads", None),
        P(None, "heads"),
        P(None, "heads"),
        P("heads", None),
        P("heads", "dp"),
        P("heads", "dp"),
    )
    return jax.shard_map(
        shards,
        mesh=mesh,
        in_specs=placed,
        out_specs=(
            P(("dp", "heads"), None),
            P(("dp", "heads"), None),
            P("heads", "dp"),
            P("heads", "dp"),
            P("heads", "dp"),
        ),
        check_vma=False,
    )
```

```python
import jax
import jax.numpy as jnp
from jax import lax
from jax.experimental import pallas as pl
from jax.experimental.pallas import tpu as pltpu
from jax.sharding import PartitionSpec as P

HEAD = 128

norm_epsilon = 1e-05
adam_epsilon = 1e-08
beta_first = 0.9
beta_second = 0.95
score_scale = 0.125
bias_first = 1.0 - 0.9**20
bias_second = 1.0 - 0.95**20

BF16 = jnp.bfloat16
F32 = jnp.float32
MESH_ID = pl.DeviceIdType.MESH
MIB = 1 << 20

D = 1280
DG = 4096
UNITS = 896
UNIT_TILES = ((0, 256), (256, 512), (512, 768), (768, 896))
WIDE_TILES = tuple((n, n + 256) for n in range(0, D, 256))
FLAT = 1512
TOKEN_SCALE = 16384.0**-0.5

GU1, GU2, DN, KK, VV, QO = range(6)
PIECES = (
    (80, 640, True),
    (80, 256, False),
    (32, 1280, False),
    (128, 256, True),
    (128, 256, False),
    (160, 128, True),
)
LATE = (KK, VV, QO)


def nn(left, right):
    return lax.dot_general(left, right, (((1,), (0,)), ((), ())), preferred_element_type=F32)


def nt(left, right):
    return lax.dot_general(left, right, (((1,), (1,)), ((), ())), preferred_element_type=F32)


def tn(left, right):
    return lax.dot_general(left, right, (((0,), (0,)), ((), ())), preferred_element_type=F32)


def inverse_rms(x):
    return lax.rsqrt(jnp.mean(x * x, axis=-1, keepdims=True) + norm_epsilon)


def norm_backward(x, inverse, scaled):
    inner = jnp.mean(scaled * x, axis=-1, keepdims=True)
    return inverse * scaled - x * (inverse * inverse * inverse) * inner


def place():
    dp = lax.axis_index("dp")
    return lax.div(dp, 8), lax.rem(lax.div(dp, 2), 4), lax.rem(dp, 2), lax.axis_index("heads")


def device_at(z, x, y, g):
    return (z * 8 + x * 2 + y, g)


def remote(src, dst, send, recv, dev):
    return pltpu.make_async_remote_copy(
        src_ref=src, dst_ref=dst, send_sem=send, recv_sem=recv, device_id=dev, device_id_type=MESH_ID
    )


def scatter_scratch(item):
    rows, cols, _ = PIECES[item]
    shapes = ((2,), (2, 2), ()) if item in LATE else ((4,), (), (2,))
    ends = [pltpu.VMEM((*m, rows, cols), BF16) for m in shapes]
    return [
        pltpu.VMEM((4, 4, 2, rows, cols), BF16),
        pltpu.VMEM((2, 2, 2, rows, cols), BF16),
        pltpu.VMEM((2, 4, 2, rows, cols), BF16),
        *ends,
        pltpu.SemaphoreType.DMA((13,)),
        pltpu.SemaphoreType.DMA((13,)),
    ]


class Scatter:
    def __init__(self, item, refs):
        rows, _, self.zfirst = PIECES[item]
        cut = 16 * ((rows // 16 + 1) // 2)
        self.halves = (slice(0, cut), slice(cut, rows))
        self.unpack(refs)
        z, x, self.y, self.g = place()
        self.f, self.s = (z, x) if self.zfirst else (x, z)
        self.live = {}

    def unpack(self, refs):
        self.grad, self.near, self.got, self.pairs, self.near2, self.got2, self.send, self.recv = refs

    def at(self, f, s):
        return (f, s) if self.zfirst else (s, f)

    def mine(self, s, y):
        return (*self.at(self.f, s), y)

    def who(self, f, s, y):
        z, x = self.at(f, s)
        return device_at(z, x, y, self.g)

    def copy(self, n, src, dst, dev):
        c = remote(src, dst, self.send.at[n], self.recv.at[n], dev)
        c.start()
        self.live[n] = c

    def start1(self):
        self.start_far()
        self.start_next()

    def start_far(self):
        far = lax.rem(self.f + 2, 4)
        for i, d in enumerate((1, 3)):
            dev = self.who(lax.rem(self.f + d, 4), self.s, self.y)
            self.copy(i, self.grad.at[self.at(far, pl.ds(2 * i, 2))], self.near.at[i], dev)

    def start_next(self):
        for i, d in enumerate((1, 3)):
            nxt = lax.rem(self.f + d, 4)
            dev = self.who(nxt, self.s, self.y)
            rest = pl.ds(2 * (1 - i), 2)
            self.copy(2 + i, self.grad.at[self.at(nxt, rest)], self.got.at[i, rest], dev)

    def relay1(self):
        for i, d in enumerate((1, 3)):
            nxt = lax.rem(self.f + d, 4)
            dev = self.who(nxt, self.s, self.y)
            self.live[i].wait_recv()

            @pl.loop(0, 4)
            def _(k):
                a, b = lax.div(k, 2), lax.rem(k, 2)
                own = self.grad[(*self.at(nxt, 2 * i + a), b)].astype(F32)
                self.near[i, a, b] = (own + self.near[i, a, b].astype(F32)).astype(BF16)

            self.copy(4 + i, self.near.at[i], self.got.at[i, pl.ds(2 * i, 2)], dev)

    def sum_mine(self, y):
        @pl.loop(0, 4)
        def _(a):
            own = self.grad[self.mine(a, y)].astype(F32)
            total = own + self.got[0, a, y].astype(F32) + self.got[1, a, y].astype(F32)
            self.grad[self.mine(a, y)] = total.astype(BF16)

    def swap(self):
        for n in (2, 3, 4, 5):
            self.live[n].wait_recv()
        other = 1 - self.y
        self.sum_mine(other)
        self.copy(12, self.grad.at[self.mine(slice(None), other)], self.pairs, self.who(self.f, self.s, other))
        self.sum_mine(self.y)

    def start2(self):
        self.live[12].wait_recv()

        @pl.loop(0, 4)
        def _(a):
            at = self.mine(a, self.y)
            self.grad[at] = (self.grad[at].astype(F32) + self.pairs[a].astype(F32)).astype(BF16)

        for i, d in enumerate((1, 3)):
            dev = self.who(self.f, lax.rem(self.s + d, 4), self.y)
            at = self.halves[i]
            self.copy(6 + i, self.grad.at[(*self.mine(lax.rem(self.s + 2, 4), self.y), at)], self.near2.at[at], dev)
        for i, d in enumerate((1, 3)):
            nxt = lax.rem(self.s + d, 4)
            dev = self.who(self.f, nxt, self.y)
            at = self.halves[1 - i]
            self.copy(8 + i, self.grad.at[(*self.mine(nxt, self.y), at)], self.got2.at[i, at], dev)

    def relay2(self):
        for i, d in enumerate((1, 3)):
            nxt = lax.rem(self.s + d, 4)
            dev = self.who(self.f, nxt, self.y)
            at = self.halves[i]
            self.live[6 + i].wait_recv()
            own = self.grad[(*self.mine(nxt, self.y), at)].astype(F32)
            self.near2[at] = (own + self.near2[at].astype(F32)).astype(BF16)
            self.copy(10 + i, self.near2.at[at], self.got2.at[i, at], dev)

    def finish(self):
        for n in (8, 9, 10, 11):
            self.live[n].wait_recv()
        own = self.grad[self.mine(self.s, self.y)].astype(F32)
        return own + self.got2[0].astype(F32) + self.got2[1].astype(F32)

    def drain(self):
        for c in self.live.values():
            c.wait_send()


class ScatterLate(Scatter):
    def unpack(self, refs):
        self.grad, self.near, self.got, self.near2, self.got2, self.last, self.send, self.recv = refs

    def start2(self):
        for n in (2, 3, 4, 5):
            self.live[n].wait_recv()

        @pl.loop(0, 8)
        def _(k):
            a, b = lax.div(k, 2), lax.rem(k, 2)
            own = self.grad[self.mine(a, b)].astype(F32)
            total = own + self.got[0, a, b].astype(F32) + self.got[1, a, b].astype(F32)
            self.grad[self.mine(a, b)] = total.astype(BF16)

        for i, d in enumerate((1, 3)):
            dev = self.who(self.f, lax.rem(self.s + d, 4), self.y)
            self.copy(6 + i, self.grad.at[self.mine(lax.rem(self.s + 2, 4), i)], self.near2.at[i], dev)
        for i, d in enumerate((1, 3)):
            nxt = lax.rem(self.s + d, 4)
            dev = self.who(self.f, nxt, self.y)
            self.copy(8 + i, self.grad.at[self.mine(nxt, 1 - i)], self.got2.at[i, 1 - i], dev)

    def relay2(self):
        for i, d in enumerate((1, 3)):
            nxt = lax.rem(self.s + d, 4)
            dev = self.who(self.f, nxt, self.y)
            self.live[6 + i].wait_recv()
            own = self.grad[self.mine(nxt, i)].astype(F32)
            self.near2[i] = (own + self.near2[i].astype(F32)).astype(BF16)
            self.copy(10 + i, self.near2.at[i], self.got2.at[i, i], dev)

    def start3(self):
        for n in (8, 9, 10, 11):
            self.live[n].wait_recv()
        for b in range(2):
            own = self.grad[self.mine(self.s, b)].astype(F32)
            total = own + self.got2[0, b].astype(F32) + self.got2[1, b].astype(F32)
            self.grad[self.mine(self.s, b)] = total.astype(BF16)
        other = 1 - self.y
        self.copy(12, self.grad.at[self.mine(self.s, other)], self.last, self.who(self.f, self.s, other))

    def finish(self):
        self.live[12].wait_recv()
        return self.grad[self.mine(self.s, self.y)].astype(F32) + self.last[...].astype(F32)


def heads_place():
    g = lax.axis_index("heads")
    y, core = lax.div(g, 2), lax.rem(g, 2)
    return g, y * 2 + 1 - core, (1 - y) * 2 + core, (1 - y) * 2 + 1 - core


def sum_scratch(rows, cols):
    return [
        pltpu.VMEM((2, rows, cols), BF16),
        pltpu.VMEM((rows, cols), BF16),
        pltpu.SemaphoreType.DMA((4,)),
        pltpu.SemaphoreType.DMA((4,)),
    ]


def pair_scratch():
    return [
        pltpu.VMEM((2, 128, D), BF16),
        pltpu.VMEM((2, 128, D), BF16),
        pltpu.SemaphoreType.DMA((6,)),
        pltpu.SemaphoreType.DMA((6,)),
    ]


class HeadsSum:
    def __init__(self, parts, rows, refs):
        self.parts, self.rows = parts, rows
        self.near, self.far, self.send, self.recv = refs
        self.live = {}
        self.dp = lax.axis_index("dp")
        self.g, self.mate, self.over, self.over_mate = heads_place()

    def send_near(self, slot):
        quarter = (self.over_mate, self.mate)[slot]
        c = remote(self.parts.at[quarter], self.near.at[slot], self.send.at[slot], self.recv.at[slot], (self.dp, self.mate))
        c.start()
        self.live[slot] = c

    def relay(self):
        self.live[0].wait_recv()
        half = self.rows // 2
        for c in range(2):

            @pl.loop(0, half // 16)
            def _(k):
                at = pl.ds(pl.multiple_of(c * half + 16 * k, 16), 16)
                total = self.near[0, at].astype(F32) + self.parts[self.over, at].astype(F32)
                self.near[0, at] = total.astype(BF16)

            at = pl.ds(c * half, half)
            copy = remote(
                self.near.at[0, at], self.far.at[at], self.send.at[2 + c], self.recv.at[2 + c], (self.dp, self.over)
            )
            copy.start()
            self.live[2 + c] = copy

    def arrive(self, c):
        if c == 0:
            self.live[1].wait_recv()
        self.live[2 + c].wait_recv()

    def total(self, *at):
        return (
            self.parts[(self.g, *at)].astype(F32) + self.near[(1, *at)].astype(F32) + self.far[at].astype(F32)
        )

    def drain(self):
        for c in self.live.values():
            c.wait_send()


class PairSum:
    def __init__(self, parts, refs):
        self.parts = parts
        self.near, self.far, self.send, self.recv = refs
        self.live = {}
        self.dp = lax.axis_index("dp")
        self.g, self.mate, self.over, _ = heads_place()
        self.core = lax.rem(self.g, 2)

    def copy(self, n, src, dst, dev):
        c = remote(src, dst, self.send.at[n], self.recv.at[n], (self.dp, dev))
        c.start()
        self.live[n] = c

    def send_near(self, b):
        self.copy(b, self.parts.at[2 * b + 1 - self.core], self.near.at[b], self.mate)

    def relay(self, b):
        self.live[b].wait_recv()
        for c in range(2):

            @pl.loop(0, 4)
            def _(k):
                at = pl.ds(pl.multiple_of(c * 64 + 16 * k, 16), 16)
                total = self.near[b, at].astype(F32) + self.parts[2 * b + self.core, at].astype(F32)
                self.near[b, at] = total.astype(BF16)

            at = pl.ds(c * 64, 64)
            self.copy(2 + 2 * b + c, self.near.at[b, at], self.far.at[b, at], self.over)

    def arrive(self, b, c):
        self.live[2 + 2 * b + c].wait_recv()

    def total(self, b, at):
        return self.near[b, at].astype(F32) + self.far[b, at].astype(F32)

    def drain(self):
        for c in self.live.values():
            c.wait_send()


class CoreSwap:
    def __init__(self, whole, send, recv):
        self.whole, self.send_sem, self.recv_sem = whole, send, recv
        self.live = {}
        self.dp = lax.axis_index("dp")
        self.g, self.mate, _, _ = heads_place()
        self.core = lax.rem(self.g, 2)

    def give(self, b, c):
        n = 2 * b + c
        ref = self.whole.at[2 * b + self.core, pl.ds(64 * c, 64)]
        copy = remote(ref, ref, self.send_sem.at[n], self.recv_sem.at[n], (self.dp, self.mate))
        copy.start()
        self.live[n] = copy

    def take(self, b):
        for c in range(2):
            self.live[2 * b + c].wait_recv()

    def drain(self):
        for c in self.live.values():
            c.wait_send()


def spread_rows(flat, start, per_row, block):
    rows, cols = block.shape
    for c in range(cols // 128):
        flat[pl.ds(start + c, rows, per_row), :] = block[:, c * 128 : (c + 1) * 128]


def place_piece(item, total, flat):
    if item == QO:
        for c in range(2):
            spread_rows(flat, c, 2, total[40 * c : 40 * c + 40])
        for c in range(10):
            spread_rows(flat, 592 + c, 10, total[80 + 8 * c : 88 + 8 * c])
    elif item == KK:
        spread_rows(flat, 80, 2, total)
    elif item == VV:
        spread_rows(flat, 336, 2, total)
    elif item == DN:
        spread_rows(flat, 1232, 10, total[0:28])
    else:
        first = 0 if item == GU1 else 5
        spread_rows(flat, 672 + first, 7, total[0:40])
        spread_rows(flat, 952 + first, 7, total[40:80])


def greet():
    z, x, y, g = place()
    dp = lax.axis_index("dp")
    _, mate, over, _ = heads_place()
    partners = [
        (dp, mate),
        (dp, over),
        device_at(lax.rem(z + 1, 4), x, y, g),
        device_at(lax.rem(z + 3, 4), x, y, g),
        device_at(z, lax.rem(x + 1, 4), y, g),
        device_at(z, lax.rem(x + 3, 4), y, g),
        device_at(z, x, 1 - y, g),
    ]
    barrier = pltpu.get_barrier_semaphore()
    for dev in partners:
        pl.semaphore_signal(barrier, inc=1, device_id=dev, device_id_type=MESH_ID)
    return lambda: pl.semaphore_wait(barrier, len(partners))


def rows_at(first, k, size):
    return pl.ds(pl.multiple_of(first + size * k, size), size)


def layer_scratch():
    quarters = lambda cols, kind: pltpu.VMEM((4, 128, cols), kind)
    plain = dict(
        states=quarters(D, BF16),
        patches=pltpu.VMEM((128, DG), BF16),
        cot=quarters(D, BF16),
        wq=pltpu.VMEM((D, 256), BF16),
        wk=pltpu.VMEM((DG, 256), BF16),
        wv=pltpu.VMEM((DG, 256), BF16),
        wo=pltpu.VMEM((256, D), BF16),
        wg=pltpu.VMEM((D, UNITS), BF16),
        wu=pltpu.VMEM((D, UNITS), BF16),
        wd=pltpu.VMEM((UNITS, D), BF16),
        loads=pltpu.SemaphoreType.DMA((10,)),
        normed=quarters(D, BF16),
        query=quarters(256, F32),
        key=pltpu.VMEM((128, 256), F32),
        keyn=pltpu.VMEM((128, 256), BF16),
        value=pltpu.VMEM((128, 256), BF16),
        att=quarters(256, BF16),
        part1=quarters(D, BF16),
        part2=quarters(D, BF16),
        part4=pltpu.VMEM((4, 32, DG), BF16),
        res=pltpu.VMEM((2, 128, D), F32),
        gain1=pltpu.VMEM((1, D), F32),
        gain2=pltpu.VMEM((1, D), F32),
        nh=quarters(D, BF16),
        rh=quarters(D, BF16),
        turned=pltpu.VMEM((D, 512), BF16),
        hgrad=pltpu.VMEM((512, UNITS), F32),
        gg=pltpu.VMEM((512, UNITS), BF16),
        ug=pltpu.VMEM((512, UNITS), BF16),
        qgrad=quarters(256, BF16),
        keyg=pltpu.VMEM((128, 256), F32),
        valg=pltpu.VMEM((128, 256), F32),
        kg=pltpu.VMEM((128, 256), BF16),
        vg=pltpu.VMEM((128, 256), BF16),
        down=pltpu.VMEM((120, D), F32),
        g1s=pltpu.SemaphoreType.DMA((4,)),
        g1r=pltpu.SemaphoreType.DMA((4,)),
        g2s=pltpu.SemaphoreType.DMA((4,)),
        g2r=pltpu.SemaphoreType.DMA((4,)),
    )
    sums = [pair_scratch(), pair_scratch(), sum_scratch(128, D), sum_scratch(32, DG)]
    jobs = [scatter_scratch(i) for i in range(len(PIECES))]
    return plain, sums, jobs


class Refs:
    pass


def layer_kernel(*refs):
    (lengths, again, fgain, states_h, patches_h, cot_h, wq_h, wk_h, wv_h, wo_h, wg_h, wu_h, wd_h,
     flat, out_bytes, out_patches) = refs[:16]
    plain, sums, jobs = layer_scratch()
    rest = list(refs[16:])
    r = Refs()
    for name in plain:
        setattr(r, name, rest.pop(0))
    r.hid = r.wd.at[0:512, 0:UNITS]
    r.attt = r.wd.at[512:768, 0:512]
    sum_refs = [[rest.pop(0) for _ in s] for s in sums]
    jobs = [(ScatterLate if i in LATE else Scatter)(i, [rest.pop(0) for _ in s]) for i, s in enumerate(jobs)]
    g, _, _, _ = heads_place()
    core = lax.rem(g, 2)

    moves = {}
    order = [
        ("patches", patches_h), ("wk", wk_h), ("wv", wv_h), ("states", states_h), ("wq", wq_h), ("wo", wo_h),
        ("cot", cot_h), ("wd", wd_h), ("wg", wg_h), ("wu", wu_h),
    ]
    for i, (name, src) in enumerate(order):
        moves[name] = pltpu.make_async_copy(src, getattr(r, name), r.loads.at[i])
    for name in ("patches", "wk", "wv", "states", "wq"):
        moves[name].start()
    r.gain1[...] = again[...].reshape(1, D)
    r.gain2[...] = fgain[...].reshape(1, D)
    all_here = greet()

    sum1 = PairSum(r.part1, sum_refs[0])
    sum2 = PairSum(r.part2, sum_refs[1])
    sum3 = HeadsSum(r.part1, 128, sum_refs[2])
    sum4 = HeadsSum(r.part4, 32, sum_refs[3])
    swap1 = CoreSwap(r.nh, r.g1s, r.g1r)
    swap2 = CoreSwap(r.rh, r.g2s, r.g2r)

    moves["patches"].wait()
    moves["wk"].wait()
    for name in ("wo", "cot", "wd", "wg", "wu"):
        moves[name].start()
    key = nn(r.patches[...], r.wk[...])
    r.key[...] = key
    for h in range(2):
        cols = slice(HEAD * h, HEAD * h + HEAD)
        one = key[:, cols]
        r.keyn[:, cols] = (one * inverse_rms(one)).astype(BF16)
    moves["wv"].wait()
    r.value[...] = nn(r.patches[...], r.wv[...]).astype(BF16)
    earlier = lax.broadcasted_iota(jnp.int32, (128, 128), 0) < lax.broadcasted_iota(jnp.int32, (128, 128), 1)
    spans = jnp.broadcast_to(lengths[...].astype(F32), (16, 128)).astype(BF16)
    starts = nn(spans, earlier.astype(F32).astype(BF16))[0:1]

    def head_probabilities(qi, h):
        cols = slice(HEAD * h, HEAD * h + HEAD)
        full = r.query[qi, :, cols]
        inverse = inverse_rms(full)
        query = (full * inverse).astype(BF16)
        scores = score_scale * nt(query, r.keyn[:, cols])
        position = (lax.broadcasted_iota(jnp.int32, (128, 128), 0) + qi * 128).astype(F32)
        weights = jnp.where(starts <= position, jnp.exp(scores), 0.0)
        return full, inverse, query, weights / jnp.sum(weights, axis=-1, keepdims=True)

    moves["states"].wait()
    moves["wq"].wait()
    moves["wo"].wait()

    def attend(qi):
        @pl.loop(0, 4)
        def _(k):
            at = rows_at(0, k, 32)
            x = r.states[qi, at].astype(F32)
            r.normed[qi, at] = (x * inverse_rms(x) * r.gain1[...]).astype(BF16)

        r.query[qi] = nn(r.normed[qi], r.wq[...])
        for h in range(2):
            cols = slice(HEAD * h, HEAD * h + HEAD)
            prob = head_probabilities(qi, h)[3]
            r.att[qi, :, cols] = nn(prob.astype(BF16), r.value[:, cols]).astype(BF16)
        for lo, hi in WIDE_TILES:
            r.part1[qi, :, lo:hi] = nn(r.att[qi], r.wo[:, lo:hi]).astype(BF16)

    for b in range(2):
        attend(2 * b + 1 - core)
        if b == 0:
            all_here()
        sum1.send_near(b)
        attend(2 * b + core)
        sum1.relay(b)

    moves["cot"].wait()
    moves["wd"].wait()

    @pl.loop(0, 2)
    def _(p):
        at = rows_at(0, p, 256)
        cot = r.cot[pl.ds(2 * p, 2)].reshape(256, D)
        for lo, hi in UNIT_TILES:
            r.hgrad[at, lo:hi] = nt(cot, r.wd[lo:hi, :])

    def residual(b):
        for c in range(2):
            sum1.arrive(b, c)

            @pl.loop(0, 2)
            def _(k):
                at = rows_at(64 * c, k, 32)
                res = r.states[2 * b + core, at].astype(F32) + sum1.total(b, at)
                r.res[b, at] = res
                r.nh[2 * b + core, at] = (res * inverse_rms(res) * r.gain2[...]).astype(BF16)

            swap1.give(b, c)

    def residual_back(b):
        for c in range(2):
            sum2.arrive(b, c)

            @pl.loop(0, 2)
            def _(k):
                at = rows_at(64 * c, k, 32)
                res = r.res[b, at]
                grad = norm_backward(res, inverse_rms(res), sum2.total(b, at) * r.gain2[...])
                grad = grad + r.cot[2 * b + core, at].astype(F32)
                r.res[b, at] = grad
                r.rh[2 * b + core, at] = grad.astype(BF16)

            swap2.give(b, c)

    residual(0)
    moves["wg"].wait()
    moves["wu"].wait()

    def feed(p):
        at = slice(256 * p, 256 * p + 256)
        normed = r.nh[pl.ds(2 * p, 2)].reshape(256, D)
        for lo, hi in UNIT_TILES:
            gate = nn(normed, r.wg[:, lo:hi])
            up = nn(normed, r.wu[:, lo:hi])
            back = r.hgrad[at, lo:hi]
            sigma = jax.nn.sigmoid(gate)
            active = gate * sigma
            r.hid[at, lo:hi] = (active * up).astype(BF16)
            r.gg[at, lo:hi] = (back * up * (sigma * (1.0 + gate * (1.0 - sigma)))).astype(BF16)
            r.ug[at, lo:hi] = (back * active).astype(BF16)
        for lo, hi in WIDE_TILES:
            part = nt(r.gg[at], r.wg[lo:hi, :]) + nt(r.ug[at], r.wu[lo:hi, :])
            r.part2[pl.ds(2 * p, 2), :, lo:hi] = part.astype(BF16).reshape(2, 128, hi - lo)

    def store(ref, at, rows, cols, new, again_):
        at = (*at, rows, cols)
        if again_:
            new = new + ref[at].astype(F32)
        ref[at] = new.astype(BF16)

    def turn(p):
        for q in (2 * p, 2 * p + 1):
            r.turned[:, 128 * q : 128 * q + 128] = r.nh[q].T

    def gate_up_grads(p, count, chunk):
        @pl.loop(0, count)
        def _(k):
            c = chunk(k)
            rows = r.turned[rows_at(0, c, 160), 256 * p : 256 * p + 256]
            z, x = lax.div(c, 2), 2 * lax.rem(c, 2)
            for grad, row in ((r.gg, 0), (r.ug, 40)):
                for job, lo, hi in ((GU1, 0, 256), (GU1, 256, 512), (GU1, 512, 640), (GU2, 640, 896)):
                    got = nn(rows, grad[256 * p : 256 * p + 256, lo:hi])
                    col = lo if job == GU1 else 0
                    for j in range(4):
                        store(
                            jobs[job].grad, (z, x + j // 2, j % 2), slice(row, row + 40), slice(col, col + hi - lo),
                            got[40 * j : 40 * j + 40], p,
                        )

    def down_grads(p):
        for q in (2 * p, 2 * p + 1):
            r.turned[0:UNITS, 128 * q : 128 * q + 128] = r.hid[128 * q : 128 * q + 128].T

        @pl.loop(0, 8)
        def _(c):
            rows = r.turned[rows_at(0, c, 112), 256 * p : 256 * p + 256]
            for lo, hi in WIDE_TILES:
                r.down[0:112, lo:hi] = nn(rows, r.cot[2 * p : 2 * p + 2, :, lo:hi].reshape(256, hi - lo))
            z, x = lax.div(c, 2), 2 * lax.rem(c, 2)
            for j in range(4):
                store(
                    jobs[DN].grad, (z, x + j // 2, j % 2), slice(0, 32), slice(0, D), r.down[28 * j : 28 * j + 32], p
                )

    r.down[112:120] = jnp.zeros((8, D), F32)
    swap1.take(0)
    feed(0)
    sum2.send_near(0)
    turn(0)
    sum2.relay(0)
    gate_up_grads(0, 8, lambda k: k)
    residual(1)
    down_grads(0)
    swap1.take(1)
    sum1.drain()
    feed(1)
    sum2.send_near(1)
    turn(1)
    sum2.relay(1)
    own_z = place()[0]
    gate_up_grads(1, 2, lambda k: 2 * lax.rem(own_z + 2, 4) + k)
    jobs[GU1].start_far()
    gate_up_grads(1, 4, lambda k: 2 * lax.rem(own_z + 1 + 2 * lax.div(k, 2), 4) + lax.rem(k, 2))
    jobs[GU1].start_next()
    gate_up_grads(1, 2, lambda k: 2 * own_z + k)
    jobs[GU2].start1()
    residual_back(0)
    down_grads(1)
    r.keyg[...] = jnp.zeros((128, 256), F32)
    r.valg[...] = jnp.zeros((128, 256), F32)

    def attend_back(qi):
        agrad = nt(r.rh[qi], r.wo[...]).astype(BF16)
        for h in range(2):
            cols = slice(HEAD * h, HEAD * h + HEAD)
            full, inverse, query, prob = head_probabilities(qi, h)
            back = nt(agrad[:, cols], r.value[:, cols])
            inner = jnp.sum(prob * back, axis=-1, keepdims=True)
            score = (score_scale * prob * (back - inner)).astype(BF16)
            grad = nn(score, r.keyn[:, cols])
            r.keyg[:, cols] += tn(score, query)
            r.valg[:, cols] += tn(prob.astype(BF16), agrad[:, cols])
            r.qgrad[qi, :, cols] = norm_backward(full, inverse, grad).astype(BF16)

    attend_back(core)
    swap2.take(0)
    attend_back(1 - core)
    jobs[GU2].relay1()
    jobs[DN].start1()
    residual_back(1)
    attend_back(2 + core)
    swap2.take(1)
    sum2.drain()
    attend_back(3 - core)
    for h in range(2):
        cols = slice(HEAD * h, HEAD * h + HEAD)
        full = r.key[:, cols]
        r.kg[:, cols] = norm_backward(full, inverse_rms(full), r.keyg[:, cols]).astype(BF16)
    r.vg[...] = r.valg[...].astype(BF16)

    jobs[GU1].relay1()

    @pl.loop(0, 8)
    def _(n):
        rows = r.patches[:, rows_at(0, n, 512)].T
        z, x = lax.div(n, 2), 2 * lax.rem(n, 2)
        for job, grad in ((KK, r.kg), (VV, r.vg)):
            got = nn(rows, grad[...]).astype(BF16)
            for j in range(4):
                jobs[job].grad[z, x + j // 2, j % 2] = got[128 * j : 128 * j + 128]

    jobs[VV].start1()
    jobs[KK].start1()
    jobs[GU2].swap()

    for q in range(4):
        r.turned[:, 128 * q : 128 * q + 128] = r.normed[q].T
        r.attt[:, 128 * q : 128 * q + 128] = r.att[q].T
    for half in range(2):
        for lo, hi in ((0, 256), (256, 512), (512, 640)):
            cols = slice(640 * half + lo, 640 * half + hi)
            r.hgrad[256 * half : 256 * half + 256, lo:hi] = nn(
                r.attt[...], r.rh[:, :, cols].reshape(512, hi - lo)
            )

    @pl.loop(0, 4)
    def _(c):
        got = nn(r.turned[rows_at(0, c, 320)], r.qgrad[...].reshape(512, 256))
        for j in range(8):
            mine = got[40 * j : 40 * j + 40]
            halves = [r.hgrad[rows_at(256 * half + 8 * j, c * 8, 8), 0:640] for half in range(2)]
            blocks = [mine[:, :128], mine[:, 128:]]
            blocks += [m[:, 128 * n : 128 * n + 128] for m in halves for n in range(5)]
            jobs[QO].grad[c, j // 2, j % 2] = jnp.concatenate(blocks, axis=0).astype(BF16)


    @pl.loop(0, 2)
    def _(p):
        grad = r.qgrad[pl.ds(2 * p, 2)].reshape(256, 256)
        for lo, hi in WIDE_TILES:
            r.part1[pl.ds(2 * p, 2), :, lo:hi] = nt(grad, r.wq[lo:hi, :]).astype(BF16).reshape(2, 128, hi - lo)

    sum3.send_near(0)
    sum3.send_near(1)

    @pl.loop(0, 16)
    def _(n):
        at = rows_at(0, n, 256)
        part = nt(r.kg[...], r.wk[at]) + nt(r.vg[...], r.wv[at])
        r.part4[:, :, at] = part.astype(BF16).reshape(4, 32, 256)

    sum4.send_near(0)
    sum4.send_near(1)
    sum3.relay()
    jobs[GU1].swap()
    sum4.relay()
    jobs[DN].relay1()
    jobs[KK].relay1()
    jobs[VV].relay1()

    for c in range(2):
        sum3.arrive(c)

        @pl.loop(0, 2)
        def _(k):
            at = rows_at(64 * c, k, 32)
            x = r.states[g, at].astype(F32)
            grad = r.res[lax.div(g, 2), at] + norm_backward(x, inverse_rms(x), sum3.total(at) * r.gain1[...])
            out_bytes[at] = grad.astype(BF16)

    jobs[QO].start1()
    jobs[GU1].start2()
    jobs[DN].swap()
    jobs[QO].relay1()

    for c in range(2):
        sum4.arrive(c)

        @pl.loop(0, 4)
        def _(k):
            at = (pl.ds(16 * c, 16), rows_at(0, k, 1024))
            out_patches[at] = sum4.total(*at).astype(BF16)

    jobs[VV].start2()
    jobs[KK].start2()
    jobs[GU2].start2()
    jobs[KK].relay2()
    jobs[QO].start2()
    jobs[VV].relay2()
    jobs[GU1].relay2()
    jobs[QO].relay2()
    jobs[KK].start3()
    jobs[DN].start2()
    jobs[VV].start3()
    jobs[GU2].relay2()
    jobs[DN].relay2()
    jobs[QO].start3()
    for n in (GU1, GU2, KK, VV, DN, QO):
        place_piece(n, jobs[n].finish(), flat)
    for item in (*jobs, sum3, sum4, swap1, swap2):
        item.drain()


def adam_kernel(summed, first, second, bytes_in, patches_in, new_first, new_second, step, bytes_out, patches_out):
    bytes_out[...] = bytes_in[...]
    patches_out[...] = patches_in[...]

    gradient = summed[...] * TOKEN_SCALE
    moment = beta_first * first[...] + (1.0 - beta_first) * gradient
    spread = beta_second * second[...] + (1.0 - beta_second) * gradient * gradient
    new_first[...] = moment
    new_second[...] = spread
    step[...] = moment / bias_first / (jnp.sqrt(spread / bias_second) + adam_epsilon)


def adam(summed, first, second, input_grad, patch_grad):
    vmem = pl.BlockSpec(memory_space=pltpu.VMEM)
    return pl.pallas_call(
        adam_kernel,
        out_shape=[jax.ShapeDtypeStruct((FLAT, 128), F32)] * 3
        + [jax.ShapeDtypeStruct(m.shape, m.dtype) for m in (input_grad, patch_grad)],
        in_specs=[vmem] * 5,
        out_specs=[vmem] * 5,
        compiler_params=pltpu.CompilerParams(vmem_limit_bytes=60 * MIB),
    )(summed, first, second, input_grad, patch_grad)


def shards(
    byte_states,
    patch_states,
    patch_lengths,
    cotangent,
    attention_gain,
    feedforward_gain,
    query_weight,
    key_weight,
    value_weight,
    output_weight,
    gate_weight,
    up_weight,
    down_weight,
    adam_first,
    adam_second,
):
    plain, sums, jobs = layer_scratch()
    vmem = pl.BlockSpec(memory_space=pltpu.VMEM)
    summed, input_grad, patch_grad = pl.pallas_call(
        layer_kernel,
        out_shape=(
            jax.ShapeDtypeStruct((FLAT, 128), F32),
            jax.ShapeDtypeStruct((128, D), BF16),
            jax.ShapeDtypeStruct((32, DG), BF16),
        ),
        in_specs=[vmem] * 3 + [pl.BlockSpec(memory_space=pl.ANY)] * 10,
        out_specs=(vmem, vmem, vmem),
        scratch_shapes=[*plain.values(), *(s for group in (*sums, *jobs) for s in group)],
        compiler_params=pltpu.CompilerParams(
            collective_id=0, has_side_effects=True, vmem_limit_bytes=63 * MIB
        ),
    )(
        patch_lengths,
        attention_gain,
        feedforward_gain,
        byte_states.reshape(4, 128, D),
        patch_states,
        cotangent.reshape(4, 128, D),
        query_weight,
        key_weight,
        value_weight,
        output_weight,
        gate_weight,
        up_weight,
        down_weight,
    )
    new_first, new_second, adam_step, input_grad, patch_grad = adam(
        summed, adam_first.reshape(FLAT, 128), adam_second.reshape(FLAT, 128), input_grad, patch_grad
    )
    return (
        input_grad,
        patch_grad,
        new_first.reshape(1, -1),
        new_second.reshape(1, -1),
        adam_step.reshape(1, -1),
    )


def solution(mesh):
    placed = (
        P("dp", None),
        P("dp", None),
        P("dp", None),
        P("dp", None),
        P(),
        P(),
        P(None, "heads"),
        P(None, "heads"),
        P(None, "heads"),
        P("heads", None),
        P(None, "heads"),
        P(None, "heads"),
        P("heads", None),
        P("heads", "dp"),
        P("heads", "dp"),
    )
    return jax.shard_map(
        shards,
        mesh=mesh,
        in_specs=placed,
        out_specs=(
            P(("dp", "heads"), None),
            P(("dp", "heads"), None),
            P("heads", "dp"),
            P("heads", "dp"),
            P("heads", "dp"),
        ),
        check_vma=False,
    )
```

```python
import jax
import jax.numpy as jnp
from jax import lax
from jax.experimental import pallas as pl
from jax.experimental.pallas import tpu as pltpu
from jax.sharding import PartitionSpec as P

HEAD = 128

norm_epsilon = 1e-05
adam_epsilon = 1e-08
beta_first = 0.9
beta_second = 0.95
score_scale = 0.125
bias_first = 1.0 - 0.9**20
bias_second = 1.0 - 0.95**20

BF16 = jnp.bfloat16
F32 = jnp.float32
MESH_ID = pl.DeviceIdType.MESH
MIB = 1 << 20

D = 1280
DG = 4096
UNITS = 896
UNIT_TILES = ((0, 256), (256, 512), (512, 768), (768, 896))
WIDE_TILES = tuple((n, n + 256) for n in range(0, D, 256))
FLAT = 1512
TOKEN_SCALE = 16384.0**-0.5

GU1, GU2, DN, KK, VV, QO = range(6)
PIECES = (
    (80, 512, True),
    (80, 384, False),
    (32, 1152, False),
    (128, 256, True),
    (128, 256, False),
    (160, 128, True),
)
LATE = (KK, VV, QO)


def nn(left, right):
    return lax.dot_general(left, right, (((1,), (0,)), ((), ())), preferred_element_type=F32)


def nt(left, right):
    return lax.dot_general(left, right, (((1,), (1,)), ((), ())), preferred_element_type=F32)


def tn(left, right):
    return lax.dot_general(left, right, (((0,), (0,)), ((), ())), preferred_element_type=F32)


def inverse_rms(x):
    return lax.rsqrt(jnp.mean(x * x, axis=-1, keepdims=True) + norm_epsilon)


def norm_backward(x, inverse, scaled):
    inner = jnp.mean(scaled * x, axis=-1, keepdims=True)
    return inverse * scaled - x * (inverse * inverse * inverse) * inner


def place():
    dp = lax.axis_index("dp")
    return lax.div(dp, 8), lax.rem(lax.div(dp, 2), 4), lax.rem(dp, 2), lax.axis_index("heads")


def device_at(z, x, y, g):
    return (z * 8 + x * 2 + y, g)


def remote(src, dst, send, recv, dev):
    return pltpu.make_async_remote_copy(
        src_ref=src, dst_ref=dst, send_sem=send, recv_sem=recv, device_id=dev, device_id_type=MESH_ID
    )


def scatter_scratch(item):
    rows, cols, _ = PIECES[item]
    shapes = ((2,), (2, 2), ()) if item in LATE else ((4,), (), (2,))
    ends = [pltpu.VMEM((*m, rows, cols), BF16) for m in shapes]
    return [
        pltpu.VMEM((4, 4, 2, rows, cols), BF16),
        pltpu.VMEM((2, 2, 2, rows, cols), BF16),
        pltpu.VMEM((2, 4, 2, rows, cols), BF16),
        *ends,
        pltpu.SemaphoreType.DMA((13,)),
        pltpu.SemaphoreType.DMA((13,)),
    ]


class Scatter:
    def __init__(self, item, refs):
        rows, _, self.zfirst = PIECES[item]
        cut = 16 * ((rows // 16 + 1) // 2)
        self.halves = (slice(0, cut), slice(cut, rows))
        self.unpack(refs)
        z, x, self.y, self.g = place()
        self.f, self.s = (z, x) if self.zfirst else (x, z)
        self.live = {}

    def unpack(self, refs):
        self.grad, self.near, self.got, self.pairs, self.near2, self.got2, self.send, self.recv = refs

    def at(self, f, s):
        return (f, s) if self.zfirst else (s, f)

    def mine(self, s, y):
        return (*self.at(self.f, s), y)

    def who(self, f, s, y):
        z, x = self.at(f, s)
        return device_at(z, x, y, self.g)

    def copy(self, n, src, dst, dev):
        c = remote(src, dst, self.send.at[n], self.recv.at[n], dev)
        c.start()
        self.live[n] = c

    def start1(self):
        self.start_far()
        self.start_next()

    def start_far(self):
        far = lax.rem(self.f + 2, 4)
        for i, d in enumerate((1, 3)):
            dev = self.who(lax.rem(self.f + d, 4), self.s, self.y)
            self.copy(i, self.grad.at[self.at(far, pl.ds(2 * i, 2))], self.near.at[i], dev)

    def start_next(self):
        for i, d in enumerate((1, 3)):
            nxt = lax.rem(self.f + d, 4)
            dev = self.who(nxt, self.s, self.y)
            rest = pl.ds(2 * (1 - i), 2)
            self.copy(2 + i, self.grad.at[self.at(nxt, rest)], self.got.at[i, rest], dev)

    def relay1(self):
        for i, d in enumerate((1, 3)):
            nxt = lax.rem(self.f + d, 4)
            dev = self.who(nxt, self.s, self.y)
            self.live[i].wait_recv()

            @pl.loop(0, 4)
            def _(k):
                a, b = lax.div(k, 2), lax.rem(k, 2)
                own = self.grad[(*self.at(nxt, 2 * i + a), b)].astype(F32)
                self.near[i, a, b] = (own + self.near[i, a, b].astype(F32)).astype(BF16)

            self.copy(4 + i, self.near.at[i], self.got.at[i, pl.ds(2 * i, 2)], dev)

    def sum_mine(self, y):
        @pl.loop(0, 4)
        def _(a):
            own = self.grad[self.mine(a, y)].astype(F32)
            total = own + self.got[0, a, y].astype(F32) + self.got[1, a, y].astype(F32)
            self.grad[self.mine(a, y)] = total.astype(BF16)

    def swap(self):
        for n in (2, 3, 4, 5):
            self.live[n].wait_recv()
        other = 1 - self.y
        self.sum_mine(other)
        self.copy(12, self.grad.at[self.mine(slice(None), other)], self.pairs, self.who(self.f, self.s, other))
        self.sum_mine(self.y)

    def start2(self):
        self.live[12].wait_recv()

        @pl.loop(0, 4)
        def _(a):
            at = self.mine(a, self.y)
            self.grad[at] = (self.grad[at].astype(F32) + self.pairs[a].astype(F32)).astype(BF16)

        for i, d in enumerate((1, 3)):
            dev = self.who(self.f, lax.rem(self.s + d, 4), self.y)
            at = self.halves[i]
            self.copy(6 + i, self.grad.at[(*self.mine(lax.rem(self.s + 2, 4), self.y), at)], self.near2.at[at], dev)
        for i, d in enumerate((1, 3)):
            nxt = lax.rem(self.s + d, 4)
            dev = self.who(self.f, nxt, self.y)
            at = self.halves[1 - i]
            self.copy(8 + i, self.grad.at[(*self.mine(nxt, self.y), at)], self.got2.at[i, at], dev)

    def relay2(self):
        for i, d in enumerate((1, 3)):
            nxt = lax.rem(self.s + d, 4)
            dev = self.who(self.f, nxt, self.y)
            at = self.halves[i]
            self.live[6 + i].wait_recv()
            own = self.grad[(*self.mine(nxt, self.y), at)].astype(F32)
            self.near2[at] = (own + self.near2[at].astype(F32)).astype(BF16)
            self.copy(10 + i, self.near2.at[at], self.got2.at[i, at], dev)

    def finish(self):
        for n in (8, 9, 10, 11):
            self.live[n].wait_recv()
        own = self.grad[self.mine(self.s, self.y)].astype(F32)
        return own + self.got2[0].astype(F32) + self.got2[1].astype(F32)

    def drain(self):
        for c in self.live.values():
            c.wait_send()


class ScatterLate(Scatter):
    def unpack(self, refs):
        self.grad, self.near, self.got, self.near2, self.got2, self.last, self.send, self.recv = refs

    def start2(self):
        for n in (2, 3, 4, 5):
            self.live[n].wait_recv()

        @pl.loop(0, 8)
        def _(k):
            a, b = lax.div(k, 2), lax.rem(k, 2)
            own = self.grad[self.mine(a, b)].astype(F32)
            total = own + self.got[0, a, b].astype(F32) + self.got[1, a, b].astype(F32)
            self.grad[self.mine(a, b)] = total.astype(BF16)

        for i, d in enumerate((1, 3)):
            dev = self.who(self.f, lax.rem(self.s + d, 4), self.y)
            self.copy(6 + i, self.grad.at[self.mine(lax.rem(self.s + 2, 4), i)], self.near2.at[i], dev)
        for i, d in enumerate((1, 3)):
            nxt = lax.rem(self.s + d, 4)
            dev = self.who(self.f, nxt, self.y)
            self.copy(8 + i, self.grad.at[self.mine(nxt, 1 - i)], self.got2.at[i, 1 - i], dev)

    def relay2(self):
        for i, d in enumerate((1, 3)):
            nxt = lax.rem(self.s + d, 4)
            dev = self.who(self.f, nxt, self.y)
            self.live[6 + i].wait_recv()
            own = self.grad[self.mine(nxt, i)].astype(F32)
            self.near2[i] = (own + self.near2[i].astype(F32)).astype(BF16)
            self.copy(10 + i, self.near2.at[i], self.got2.at[i, i], dev)

    def start3(self):
        for n in (8, 9, 10, 11):
            self.live[n].wait_recv()
        for b in range(2):
            own = self.grad[self.mine(self.s, b)].astype(F32)
            total = own + self.got2[0, b].astype(F32) + self.got2[1, b].astype(F32)
            self.grad[self.mine(self.s, b)] = total.astype(BF16)
        other = 1 - self.y
        self.copy(12, self.grad.at[self.mine(self.s, other)], self.last, self.who(self.f, self.s, other))

    def finish(self):
        self.live[12].wait_recv()
        return self.grad[self.mine(self.s, self.y)].astype(F32) + self.last[...].astype(F32)


def heads_place():
    g = lax.axis_index("heads")
    y, core = lax.div(g, 2), lax.rem(g, 2)
    return g, y * 2 + 1 - core, (1 - y) * 2 + core, (1 - y) * 2 + 1 - core


def sum_scratch(rows, cols):
    return [
        pltpu.VMEM((2, rows, cols), BF16),
        pltpu.VMEM((rows, cols), BF16),
        pltpu.SemaphoreType.DMA((4,)),
        pltpu.SemaphoreType.DMA((4,)),
    ]


def pair_scratch():
    return [
        pltpu.VMEM((2, 128, D), BF16),
        pltpu.VMEM((2, 128, D), BF16),
        pltpu.SemaphoreType.DMA((6,)),
        pltpu.SemaphoreType.DMA((6,)),
    ]


class HeadsSum:
    def __init__(self, parts, rows, refs):
        self.parts, self.rows = parts, rows
        self.near, self.far, self.send, self.recv = refs
        self.live = {}
        self.dp = lax.axis_index("dp")
        self.g, self.mate, self.over, self.over_mate = heads_place()

    def send_near(self, slot):
        quarter = (self.over_mate, self.mate)[slot]
        c = remote(self.parts.at[quarter], self.near.at[slot], self.send.at[slot], self.recv.at[slot], (self.dp, self.mate))
        c.start()
        self.live[slot] = c

    def relay(self):
        self.live[0].wait_recv()
        half = self.rows // 2
        for c in range(2):

            @pl.loop(0, half // 16)
            def _(k):
                at = pl.ds(pl.multiple_of(c * half + 16 * k, 16), 16)
                total = self.near[0, at].astype(F32) + self.parts[self.over, at].astype(F32)
                self.near[0, at] = total.astype(BF16)

            at = pl.ds(c * half, half)
            copy = remote(
                self.near.at[0, at], self.far.at[at], self.send.at[2 + c], self.recv.at[2 + c], (self.dp, self.over)
            )
            copy.start()
            self.live[2 + c] = copy

    def arrive(self, c):
        if c == 0:
            self.live[1].wait_recv()
        self.live[2 + c].wait_recv()

    def total(self, *at):
        return (
            self.parts[(self.g, *at)].astype(F32) + self.near[(1, *at)].astype(F32) + self.far[at].astype(F32)
        )

    def drain(self):
        for c in self.live.values():
            c.wait_send()


class PairSum:
    def __init__(self, parts, refs):
        self.parts = parts
        self.near, self.far, self.send, self.recv = refs
        self.live = {}
        self.dp = lax.axis_index("dp")
        self.g, self.mate, self.over, _ = heads_place()
        self.core = lax.rem(self.g, 2)

    def copy(self, n, src, dst, dev):
        c = remote(src, dst, self.send.at[n], self.recv.at[n], (self.dp, dev))
        c.start()
        self.live[n] = c

    def send_near(self, b):
        self.copy(b, self.parts.at[2 * b + 1 - self.core], self.near.at[b], self.mate)

    def relay(self, b):
        self.live[b].wait_recv()
        for c in range(2):

            @pl.loop(0, 4)
            def _(k):
                at = pl.ds(pl.multiple_of(c * 64 + 16 * k, 16), 16)
                total = self.near[b, at].astype(F32) + self.parts[2 * b + self.core, at].astype(F32)
                self.near[b, at] = total.astype(BF16)

            at = pl.ds(c * 64, 64)
            self.copy(2 + 2 * b + c, self.near.at[b, at], self.far.at[b, at], self.over)

    def arrive(self, b, c):
        self.live[2 + 2 * b + c].wait_recv()

    def total(self, b, at):
        return self.near[b, at].astype(F32) + self.far[b, at].astype(F32)

    def drain(self):
        for c in self.live.values():
            c.wait_send()


class CoreSwap:
    def __init__(self, whole, send, recv):
        self.whole, self.send_sem, self.recv_sem = whole, send, recv
        self.live = {}
        self.dp = lax.axis_index("dp")
        self.g, self.mate, _, _ = heads_place()
        self.core = lax.rem(self.g, 2)

    def give(self, b, c):
        n = 2 * b + c
        ref = self.whole.at[2 * b + self.core, pl.ds(64 * c, 64)]
        copy = remote(ref, ref, self.send_sem.at[n], self.recv_sem.at[n], (self.dp, self.mate))
        copy.start()
        self.live[n] = copy

    def take(self, b):
        for c in range(2):
            self.live[2 * b + c].wait_recv()

    def drain(self):
        for c in self.live.values():
            c.wait_send()


def spread_rows(flat, start, per_row, block):
    rows, cols = block.shape
    for c in range(cols // 128):
        flat[pl.ds(start + c, rows, per_row), :] = block[:, c * 128 : (c + 1) * 128]


def place_piece(item, total, flat):
    if item == QO:
        for c in range(2):
            spread_rows(flat, c, 2, total[40 * c : 40 * c + 40])
        for c in range(10):
            spread_rows(flat, 592 + c, 10, total[80 + 8 * c : 88 + 8 * c])
    elif item == KK:
        spread_rows(flat, 80, 2, total)
    elif item == VV:
        spread_rows(flat, 336, 2, total)
    elif item == DN:
        spread_rows(flat, 1232, 10, total[0:28])
        for m in range(7):
            spread_rows(flat, 1241 + 40 * m, 10, total[28:32, 128 * m : 128 * m + 128])
    else:
        first = 0 if item == GU1 else 4
        spread_rows(flat, 672 + first, 7, total[0:40])
        spread_rows(flat, 952 + first, 7, total[40:80])


def greet():
    z, x, y, g = place()
    dp = lax.axis_index("dp")
    _, mate, over, _ = heads_place()
    partners = [
        (dp, mate),
        (dp, over),
        device_at(lax.rem(z + 1, 4), x, y, g),
        device_at(lax.rem(z + 3, 4), x, y, g),
        device_at(z, lax.rem(x + 1, 4), y, g),
        device_at(z, lax.rem(x + 3, 4), y, g),
        device_at(z, x, 1 - y, g),
    ]
    barrier = pltpu.get_barrier_semaphore()
    for dev in partners:
        pl.semaphore_signal(barrier, inc=1, device_id=dev, device_id_type=MESH_ID)
    return lambda: pl.semaphore_wait(barrier, len(partners))


def rows_at(first, k, size):
    return pl.ds(pl.multiple_of(first + size * k, size), size)


def layer_scratch():
    quarters = lambda cols, kind: pltpu.VMEM((4, 128, cols), kind)
    plain = dict(
        states=quarters(D, BF16),
        patches=pltpu.VMEM((128, DG), BF16),
        cot=quarters(D, BF16),
        wq=pltpu.VMEM((D, 256), BF16),
        wk=pltpu.VMEM((DG, 256), BF16),
        wv=pltpu.VMEM((DG, 256), BF16),
        wo=pltpu.VMEM((256, D), BF16),
        wg=pltpu.VMEM((D, UNITS), BF16),
        wu=pltpu.VMEM((D, UNITS), BF16),
        wd=pltpu.VMEM((UNITS, D), BF16),
        loads=pltpu.SemaphoreType.DMA((10,)),
        normed=quarters(D, BF16),
        query=quarters(256, F32),
        key=pltpu.VMEM((128, 256), F32),
        keyn=pltpu.VMEM((128, 256), BF16),
        value=pltpu.VMEM((128, 256), BF16),
        att=quarters(256, BF16),
        part1=quarters(D, BF16),
        part2=quarters(D, BF16),
        part4=pltpu.VMEM((4, 32, DG), BF16),
        res=pltpu.VMEM((2, 128, D), F32),
        gain1=pltpu.VMEM((1, D), F32),
        gain2=pltpu.VMEM((1, D), F32),
        nh=quarters(D, BF16),
        rh=quarters(D, BF16),
        turned=pltpu.VMEM((D, 512), BF16),
        hgrad=pltpu.VMEM((512, UNITS), F32),
        gg=pltpu.VMEM((512, UNITS), BF16),
        ug=pltpu.VMEM((512, UNITS), BF16),
        qgrad=quarters(256, BF16),
        keyg=pltpu.VMEM((128, 256), F32),
        valg=pltpu.VMEM((128, 256), F32),
        kg=pltpu.VMEM((128, 256), BF16),
        vg=pltpu.VMEM((128, 256), BF16),
        down=pltpu.VMEM((112, D), F32),
        lined=pltpu.VMEM((32, 1152), F32),
        g1s=pltpu.SemaphoreType.DMA((4,)),
        g1r=pltpu.SemaphoreType.DMA((4,)),
        g2s=pltpu.SemaphoreType.DMA((4,)),
        g2r=pltpu.SemaphoreType.DMA((4,)),
    )
    sums = [pair_scratch(), pair_scratch(), sum_scratch(128, D), sum_scratch(32, DG)]
    jobs = [scatter_scratch(i) for i in range(len(PIECES))]
    return plain, sums, jobs


class Refs:
    pass


def layer_kernel(*refs):
    (lengths, again, fgain, states_h, patches_h, cot_h, wq_h, wk_h, wv_h, wo_h, wg_h, wu_h, wd_h,
     flat, out_bytes, out_patches) = refs[:16]
    plain, sums, jobs = layer_scratch()
    rest = list(refs[16:])
    r = Refs()
    for name in plain:
        setattr(r, name, rest.pop(0))
    r.hid = r.wd.at[0:512, 0:UNITS]
    r.attt = r.wd.at[512:768, 0:512]
    sum_refs = [[rest.pop(0) for _ in s] for s in sums]
    jobs = [(ScatterLate if i in LATE else Scatter)(i, [rest.pop(0) for _ in s]) for i, s in enumerate(jobs)]
    g, _, _, _ = heads_place()
    core = lax.rem(g, 2)

    moves = {}
    order = [
        ("patches", patches_h), ("wk", wk_h), ("wv", wv_h), ("states", states_h), ("wq", wq_h), ("wo", wo_h),
        ("cot", cot_h), ("wd", wd_h), ("wg", wg_h), ("wu", wu_h),
    ]
    for i, (name, src) in enumerate(order):
        moves[name] = pltpu.make_async_copy(src, getattr(r, name), r.loads.at[i])
    for name in ("patches", "wk", "wv", "states", "wq"):
        moves[name].start()
    r.gain1[...] = again[...].reshape(1, D)
    r.gain2[...] = fgain[...].reshape(1, D)
    all_here = greet()

    sum1 = PairSum(r.part1, sum_refs[0])
    sum2 = PairSum(r.part2, sum_refs[1])
    sum3 = HeadsSum(r.part1, 128, sum_refs[2])
    sum4 = HeadsSum(r.part4, 32, sum_refs[3])
    swap1 = CoreSwap(r.nh, r.g1s, r.g1r)
    swap2 = CoreSwap(r.rh, r.g2s, r.g2r)

    moves["patches"].wait()
    moves["wk"].wait()
    for name in ("wo", "cot", "wd", "wg", "wu"):
        moves[name].start()
    key = nn(r.patches[...], r.wk[...])
    r.key[...] = key
    for h in range(2):
        cols = slice(HEAD * h, HEAD * h + HEAD)
        one = key[:, cols]
        r.keyn[:, cols] = (one * inverse_rms(one)).astype(BF16)
    moves["wv"].wait()
    r.value[...] = nn(r.patches[...], r.wv[...]).astype(BF16)
    earlier = lax.broadcasted_iota(jnp.int32, (128, 128), 0) < lax.broadcasted_iota(jnp.int32, (128, 128), 1)
    spans = jnp.broadcast_to(lengths[...].astype(F32), (16, 128)).astype(BF16)
    starts = nn(spans, earlier.astype(F32).astype(BF16))[0:1]

    def head_probabilities(qi, h):
        cols = slice(HEAD * h, HEAD * h + HEAD)
        full = r.query[qi, :, cols]
        inverse = inverse_rms(full)
        query = (full * inverse).astype(BF16)
        scores = score_scale * nt(query, r.keyn[:, cols])
        position = (lax.broadcasted_iota(jnp.int32, (128, 128), 0) + qi * 128).astype(F32)
        weights = jnp.where(starts <= position, jnp.exp(scores), 0.0)
        return full, inverse, query, weights / jnp.sum(weights, axis=-1, keepdims=True)

    moves["states"].wait()
    moves["wq"].wait()
    moves["wo"].wait()

    def attend(qi):
        @pl.loop(0, 4)
        def _(k):
            at = rows_at(0, k, 32)
            x = r.states[qi, at].astype(F32)
            r.normed[qi, at] = (x * inverse_rms(x) * r.gain1[...]).astype(BF16)

        r.query[qi] = nn(r.normed[qi], r.wq[...])
        for h in range(2):
            cols = slice(HEAD * h, HEAD * h + HEAD)
            prob = head_probabilities(qi, h)[3]
            r.att[qi, :, cols] = nn(prob.astype(BF16), r.value[:, cols]).astype(BF16)
        for lo, hi in WIDE_TILES:
            r.part1[qi, :, lo:hi] = nn(r.att[qi], r.wo[:, lo:hi]).astype(BF16)

    for b in range(2):
        attend(2 * b + 1 - core)
        if b == 0:
            all_here()
        sum1.send_near(b)
        attend(2 * b + core)
        sum1.relay(b)

    moves["cot"].wait()
    moves["wd"].wait()

    @pl.loop(0, 2)
    def _(p):
        at = rows_at(0, p, 256)
        cot = r.cot[pl.ds(2 * p, 2)].reshape(256, D)
        for lo, hi in UNIT_TILES:
            r.hgrad[at, lo:hi] = nt(cot, r.wd[lo:hi, :])

    def residual(b):
        for c in range(2):
            sum1.arrive(b, c)

            @pl.loop(0, 2)
            def _(k):
                at = rows_at(64 * c, k, 32)
                res = r.states[2 * b + core, at].astype(F32) + sum1.total(b, at)
                r.res[b, at] = res
                r.nh[2 * b + core, at] = (res * inverse_rms(res) * r.gain2[...]).astype(BF16)

            swap1.give(b, c)

    def residual_back(b):
        for c in range(2):
            sum2.arrive(b, c)

            @pl.loop(0, 2)
            def _(k):
                at = rows_at(64 * c, k, 32)
                res = r.res[b, at]
                grad = norm_backward(res, inverse_rms(res), sum2.total(b, at) * r.gain2[...])
                grad = grad + r.cot[2 * b + core, at].astype(F32)
                r.res[b, at] = grad
                r.rh[2 * b + core, at] = grad.astype(BF16)

            swap2.give(b, c)

    residual(0)
    moves["wg"].wait()
    moves["wu"].wait()

    def feed(p):
        at = slice(256 * p, 256 * p + 256)
        normed = r.nh[pl.ds(2 * p, 2)].reshape(256, D)
        for lo, hi in UNIT_TILES:
            gate = nn(normed, r.wg[:, lo:hi])
            up = nn(normed, r.wu[:, lo:hi])
            back = r.hgrad[at, lo:hi]
            sigma = jax.nn.sigmoid(gate)
            active = gate * sigma
            r.hid[at, lo:hi] = (active * up).astype(BF16)
            r.gg[at, lo:hi] = (back * up * (sigma * (1.0 + gate * (1.0 - sigma)))).astype(BF16)
            r.ug[at, lo:hi] = (back * active).astype(BF16)
        for lo, hi in WIDE_TILES:
            part = nt(r.gg[at], r.wg[lo:hi, :]) + nt(r.ug[at], r.wu[lo:hi, :])
            r.part2[pl.ds(2 * p, 2), :, lo:hi] = part.astype(BF16).reshape(2, 128, hi - lo)

    def store(ref, at, rows, cols, new, again_):
        at = (*at, rows, cols)
        if again_:
            new = new + ref[at].astype(F32)
        ref[at] = new.astype(BF16)

    def turn(p):
        for q in (2 * p, 2 * p + 1):
            r.turned[:, 128 * q : 128 * q + 128] = r.nh[q].T

    def gate_up_grads(p, count, chunk):
        @pl.loop(0, count)
        def _(k):
            c = chunk(k)
            rows = r.turned[rows_at(0, c, 160), 256 * p : 256 * p + 256]
            z, x = lax.div(c, 2), 2 * lax.rem(c, 2)
            for grad, row in ((r.gg, 0), (r.ug, 40)):
                for job, lo, hi in ((GU1, 0, 256), (GU1, 256, 512), (GU2, 512, 768), (GU2, 768, 896)):
                    got = nn(rows, grad[256 * p : 256 * p + 256, lo:hi])
                    col = lo if job == GU1 else lo - 512
                    for j in range(4):
                        store(
                            jobs[job].grad, (z, x + j // 2, j % 2), slice(row, row + 40), slice(col, col + hi - lo),
                            got[40 * j : 40 * j + 40], p,
                        )

    def down_grads(p):
        for q in (2 * p, 2 * p + 1):
            r.turned[0:UNITS, 128 * q : 128 * q + 128] = r.hid[128 * q : 128 * q + 128].T

        @pl.loop(0, 8)
        def _(c):
            rows = r.turned[rows_at(0, c, 112), 256 * p : 256 * p + 256]
            for lo, hi in WIDE_TILES:
                r.down[:, lo:hi] = nn(rows, r.cot[2 * p : 2 * p + 2, :, lo:hi].reshape(256, hi - lo))
            z, x = lax.div(c, 2), 2 * lax.rem(c, 2)
            for j in range(4):
                r.lined[0:28] = r.down[28 * j : 28 * j + 28, 0:1152]
                for m in range(7):
                    r.lined[28:32, 128 * m : 128 * m + 128] = r.down[28 * j + 4 * m : 28 * j + 4 * m + 4, 1152:1280]
                store(jobs[DN].grad, (z, x + j // 2, j % 2), slice(0, 32), slice(0, 1152), r.lined[...], p)

    r.lined[...] = jnp.zeros((32, 1152), F32)
    swap1.take(0)
    feed(0)
    sum2.send_near(0)
    turn(0)
    sum2.relay(0)
    gate_up_grads(0, 8, lambda k: k)
    residual(1)
    down_grads(0)
    swap1.take(1)
    sum1.drain()
    feed(1)
    sum2.send_near(1)
    turn(1)
    sum2.relay(1)
    own_z = place()[0]
    gate_up_grads(1, 2, lambda k: 2 * lax.rem(own_z + 2, 4) + k)
    jobs[GU1].start_far()
    gate_up_grads(1, 4, lambda k: 2 * lax.rem(own_z + 1 + 2 * lax.div(k, 2), 4) + lax.rem(k, 2))
    jobs[GU1].start_next()
    gate_up_grads(1, 2, lambda k: 2 * own_z + k)
    jobs[GU2].start1()
    residual_back(0)
    down_grads(1)
    r.keyg[...] = jnp.zeros((128, 256), F32)
    r.valg[...] = jnp.zeros((128, 256), F32)

    def attend_back(qi):
        agrad = nt(r.rh[qi], r.wo[...]).astype(BF16)
        for h in range(2):
            cols = slice(HEAD * h, HEAD * h + HEAD)
            full, inverse, query, prob = head_probabilities(qi, h)
            back = nt(agrad[:, cols], r.value[:, cols])
            inner = jnp.sum(prob * back, axis=-1, keepdims=True)
            score = (score_scale * prob * (back - inner)).astype(BF16)
            grad = nn(score, r.keyn[:, cols])
            r.keyg[:, cols] += tn(score, query)
            r.valg[:, cols] += tn(prob.astype(BF16), agrad[:, cols])
            r.qgrad[qi, :, cols] = norm_backward(full, inverse, grad).astype(BF16)

    attend_back(core)
    swap2.take(0)
    attend_back(1 - core)
    jobs[GU2].relay1()
    jobs[DN].start1()
    residual_back(1)
    attend_back(2 + core)
    swap2.take(1)
    sum2.drain()
    attend_back(3 - core)
    for h in range(2):
        cols = slice(HEAD * h, HEAD * h + HEAD)
        full = r.key[:, cols]
        r.kg[:, cols] = norm_backward(full, inverse_rms(full), r.keyg[:, cols]).astype(BF16)
    r.vg[...] = r.valg[...].astype(BF16)

    jobs[GU1].relay1()

    @pl.loop(0, 8)
    def _(n):
        rows = r.patches[:, rows_at(0, n, 512)].T
        z, x = lax.div(n, 2), 2 * lax.rem(n, 2)
        for job, grad in ((KK, r.kg), (VV, r.vg)):
            got = nn(rows, grad[...]).astype(BF16)
            for j in range(4):
                jobs[job].grad[z, x + j // 2, j % 2] = got[128 * j : 128 * j + 128]

    jobs[VV].start1()
    jobs[KK].start1()
    jobs[GU2].swap()

    for q in range(4):
        r.turned[:, 128 * q : 128 * q + 128] = r.normed[q].T
        r.attt[:, 128 * q : 128 * q + 128] = r.att[q].T
    for half in range(2):
        for lo, hi in ((0, 256), (256, 512), (512, 640)):
            cols = slice(640 * half + lo, 640 * half + hi)
            r.hgrad[256 * half : 256 * half + 256, lo:hi] = nn(
                r.attt[...], r.rh[:, :, cols].reshape(512, hi - lo)
            )

    @pl.loop(0, 4)
    def _(c):
        got = nn(r.turned[rows_at(0, c, 320)], r.qgrad[...].reshape(512, 256))
        for j in range(8):
            mine = got[40 * j : 40 * j + 40]
            halves = [r.hgrad[rows_at(256 * half + 8 * j, c * 8, 8), 0:640] for half in range(2)]
            blocks = [mine[:, :128], mine[:, 128:]]
            blocks += [m[:, 128 * n : 128 * n + 128] for m in halves for n in range(5)]
            jobs[QO].grad[c, j // 2, j % 2] = jnp.concatenate(blocks, axis=0).astype(BF16)


    @pl.loop(0, 2)
    def _(p):
        grad = r.qgrad[pl.ds(2 * p, 2)].reshape(256, 256)
        for lo, hi in WIDE_TILES:
            r.part1[pl.ds(2 * p, 2), :, lo:hi] = nt(grad, r.wq[lo:hi, :]).astype(BF16).reshape(2, 128, hi - lo)

    sum3.send_near(0)
    sum3.send_near(1)

    @pl.loop(0, 16)
    def _(n):
        at = rows_at(0, n, 256)
        part = nt(r.kg[...], r.wk[at]) + nt(r.vg[...], r.wv[at])
        r.part4[:, :, at] = part.astype(BF16).reshape(4, 32, 256)

    sum4.send_near(0)
    sum4.send_near(1)
    sum3.relay()
    jobs[GU1].swap()
    sum4.relay()
    jobs[DN].relay1()
    jobs[KK].relay1()
    jobs[VV].relay1()

    for c in range(2):
        sum3.arrive(c)

        @pl.loop(0, 2)
        def _(k):
            at = rows_at(64 * c, k, 32)
            x = r.states[g, at].astype(F32)
            grad = r.res[lax.div(g, 2), at] + norm_backward(x, inverse_rms(x), sum3.total(at) * r.gain1[...])
            out_bytes[at] = grad.astype(BF16)

    jobs[QO].start1()
    jobs[GU1].start2()
    jobs[DN].swap()
    jobs[QO].relay1()

    for c in range(2):
        sum4.arrive(c)

        @pl.loop(0, 4)
        def _(k):
            at = (pl.ds(16 * c, 16), rows_at(0, k, 1024))
            out_patches[at] = sum4.total(*at).astype(BF16)

    jobs[VV].start2()
    jobs[KK].start2()
    jobs[GU2].start2()
    jobs[KK].relay2()
    jobs[QO].start2()
    jobs[VV].relay2()
    jobs[GU1].relay2()
    jobs[QO].relay2()
    jobs[KK].start3()
    jobs[DN].start2()
    jobs[VV].start3()
    jobs[GU2].relay2()
    jobs[DN].relay2()
    jobs[QO].start3()
    for n in (GU1, GU2, KK, VV, DN, QO):
        place_piece(n, jobs[n].finish(), flat)
    for item in (*jobs, sum3, sum4, swap1, swap2):
        item.drain()


def adam_kernel(summed, first, second, bytes_in, patches_in, new_first, new_second, step, bytes_out, patches_out):
    bytes_out[...] = bytes_in[...]
    patches_out[...] = patches_in[...]

    gradient = summed[...] * TOKEN_SCALE
    moment = beta_first * first[...] + (1.0 - beta_first) * gradient
    spread = beta_second * second[...] + (1.0 - beta_second) * gradient * gradient
    new_first[...] = moment
    new_second[...] = spread
    step[...] = moment / bias_first / (jnp.sqrt(spread / bias_second) + adam_epsilon)


def adam(summed, first, second, input_grad, patch_grad):
    vmem = pl.BlockSpec(memory_space=pltpu.VMEM)
    return pl.pallas_call(
        adam_kernel,
        out_shape=[jax.ShapeDtypeStruct((FLAT, 128), F32)] * 3
        + [jax.ShapeDtypeStruct(m.shape, m.dtype) for m in (input_grad, patch_grad)],
        in_specs=[vmem] * 5,
        out_specs=[vmem] * 5,
        compiler_params=pltpu.CompilerParams(vmem_limit_bytes=60 * MIB),
    )(summed, first, second, input_grad, patch_grad)


def shards(
    byte_states,
    patch_states,
    patch_lengths,
    cotangent,
    attention_gain,
    feedforward_gain,
    query_weight,
    key_weight,
    value_weight,
    output_weight,
    gate_weight,
    up_weight,
    down_weight,
    adam_first,
    adam_second,
):
    plain, sums, jobs = layer_scratch()
    vmem = pl.BlockSpec(memory_space=pltpu.VMEM)
    summed, input_grad, patch_grad = pl.pallas_call(
        layer_kernel,
        out_shape=(
            jax.ShapeDtypeStruct((FLAT, 128), F32),
            jax.ShapeDtypeStruct((128, D), BF16),
            jax.ShapeDtypeStruct((32, DG), BF16),
        ),
        in_specs=[vmem] * 3 + [pl.BlockSpec(memory_space=pl.ANY)] * 10,
        out_specs=(vmem, vmem, vmem),
        scratch_shapes=[*plain.values(), *(s for group in (*sums, *jobs) for s in group)],
        compiler_params=pltpu.CompilerParams(
            collective_id=0, has_side_effects=True, vmem_limit_bytes=63 * MIB
        ),
    )(
        patch_lengths,
        attention_gain,
        feedforward_gain,
        byte_states.reshape(4, 128, D),
        patch_states,
        cotangent.reshape(4, 128, D),
        query_weight,
        key_weight,
        value_weight,
        output_weight,
        gate_weight,
        up_weight,
        down_weight,
    )
    new_first, new_second, adam_step, input_grad, patch_grad = adam(
        summed, adam_first.reshape(FLAT, 128), adam_second.reshape(FLAT, 128), input_grad, patch_grad
    )
    return (
        input_grad,
        patch_grad,
        new_first.reshape(1, -1),
        new_second.reshape(1, -1),
        adam_step.reshape(1, -1),
    )


def solution(mesh):
    placed = (
        P("dp", None),
        P("dp", None),
        P("dp", None),
        P("dp", None),
        P(),
        P(),
        P(None, "heads"),
        P(None, "heads"),
        P(None, "heads"),
        P("heads", None),
        P(None, "heads"),
        P(None, "heads"),
        P("heads", None),
        P("heads", "dp"),
        P("heads", "dp"),
    )
    return jax.shard_map(
        shards,
        mesh=mesh,
        in_specs=placed,
        out_specs=(
            P(("dp", "heads"), None),
            P(("dp", "heads"), None),
            P("heads", "dp"),
            P("heads", "dp"),
            P("heads", "dp"),
        ),
        check_vma=False,
    )
```
